32 devices in a mesh: ctx: 8 (over z, y), shard: 4 (over x, core).
Axes of the slice: x: 2, y: 2, z: 4, core: 2. Of those that a mesh axis runs over, the one named last changes fastest.
Arguments:
- inputs: bfloat16 [4096, 1600], P(('shard', 'ctx')), may hold values from -6 to 6
- positions: int32 [4096], P(('shard', 'ctx')), may hold values from 0 to 1279, as said below
- segments: int32 [4096], P(('shard', 'ctx')), may hold values from 0 to 7, as said below
- cotangent: bfloat16 [4096, 1600], P(('shard', 'ctx')), may hold values from -6 to 6
- ln1_gain: bfloat16 [1600], P('shard'), may hold values from 0.5 to 1.5
- ln1_bias: bfloat16 [1600], P('shard'), may hold values from -3 to 3
- w_qkv: bfloat16 [1600, 4800], P('shard'), may hold values from -0.15625 to 0.15625
- qv_bias: bfloat16 [3200], P('shard'), may hold values from -3 to 3
- w_out: bfloat16 [1600, 1600], P('shard'), may hold values from -2.5 to 2.5
- out_bias: bfloat16 [1600], P('shard'), may hold values from -3 to 3
- ln2_gain: bfloat16 [1600], P('shard'), may hold values from 0.5 to 1.5
- ln2_bias: bfloat16 [1600], P('shard'), may hold values from -3 to 3
- w_fc: bfloat16 [1600, 6400], P('shard'), may hold values from -0.15625 to 0.15625
- fc_bias: bfloat16 [6400], P('shard'), may hold values from -3 to 3
- w_proj: bfloat16 [6400, 1600], P('shard'), may hold values from -0.078125 to 0.078125
- proj_bias: bfloat16 [1600], P('shard'), may hold values from -3 to 3
Outputs:
- output: bfloat16 [4096, 1600], P(('shard', 'ctx'))
- input_grad: float32 [4096, 1600], P(('shard', 'ctx'))
- grad_ln1_gain: float32 [1600], P('shard')
- grad_ln1_bias: float32 [1600], P('shard')
- grad_w_qkv: float32 [1600, 4800], P('shard')
- grad_qv_bias: float32 [3200], P('shard')
- grad_w_out: float32 [1600, 1600], P('shard')
- grad_out_bias: float32 [1600], P('shard')
- grad_ln2_gain: float32 [1600], P('shard')
- grad_ln2_bias: float32 [1600], P('shard')
- grad_w_fc: float32 [1600, 6400], P('shard')
- grad_fc_bias: float32 [6400], P('shard')
- grad_w_proj: float32 [6400, 1600], P('shard')
- grad_proj_bias: float32 [1600], P('shard')
The draws below stay inside these ranges and needn't reach their ends.
Inputs may be any that keep to these rules, and one draw needn't show every extreme that they name: The tokens form 4 sequences of 1024 consecutive rows. Each sequence holds two documents, first id 2 s then 2 s + 1 for sequence s; one of them has fewer than 128 tokens, at the start or at the end. Along a document positions rise by one. The short document starts below 1024, and at 0 in the first sequence; the long one ends at 1279. `segments`: ids never fall along a sequence.
All inputs are finite; a program needn't handle non-finite values.
Results may differ from the reference program's by a relative error of at most 0.018.
Values may be sent and summed in bfloat16 or wider, within the bound.
A program may use at most 448 MiB of HBM per device.

```python
import math
import jax
import jax.numpy as jnp
from jax import lax

HEADS = 25
HEAD_DIM = 64
D = 1600
FF = 6400
BLOCK = 256
TOK_DEV = 128
SEQ = 1024
SEQS = 4
TOKENS = 4096


def documents(key):
    short_len = jax.random.randint(jax.random.fold_in(key, 11), (SEQS,), 1, TOK_DEV)
    short_first = jax.random.randint(jax.random.fold_in(key, 12), (SEQS,), 0, 2)
    short_start = jax.random.randint(jax.random.fold_in(key, 13), (SEQS,), 0, 4 * BLOCK)
    short_start = short_start * (jnp.arange(SEQS, dtype=jnp.int32) > 0).astype(jnp.int32)
    long_start = BLOCK + short_len
    token_index = jnp.arange(SEQ, dtype=jnp.int32)
    boundary = jnp.where(short_first == 1, short_len, SEQ - short_len)
    second = (token_index[None, :] >= boundary[:, None]).astype(jnp.int32)
    within = token_index[None, :] - second * boundary[:, None]
    is_short = second != short_first[:, None]
    offset = jnp.where(is_short, short_start[:, None], long_start[:, None])
    token_pos = (within + offset).reshape(SEQS * SEQ).astype(jnp.int32)
    token_seg = (2 * jnp.arange(SEQS, dtype=jnp.int32)[:, None] + second).reshape(SEQS * SEQ).astype(jnp.int32)
    return (token_pos, token_seg)


def draw_positions(key, part):
    return documents(key)[0]


def draw_segments(key, part):
    return documents(key)[1]


def block_levels(rng, shape, cuts, smallest, top_value):
    def one(position, shards_of):
        heights = jax.random.uniform(jax.random.fold_in(jax.random.fold_in(rng, 6), position), (shards_of,), jnp.float32, smallest / len(cuts), top_value / len(cuts))
        return jnp.repeat(jnp.exp(heights), shape[position] // shards_of).reshape((-1,) + (1,) * (len(shape) - position - 1))

    factor_of = one(*cuts[0])
    for cut in cuts[1:]:
        factor_of = factor_of * one(*cut)
    return factor_of


def noise(stream_key, extent, scale, reach, shards=(), kind=jnp.bfloat16):
    drawn = scale * jax.random.normal(stream_key, extent, jnp.float32)
    if shards:
        drawn = drawn * block_levels(stream_key, extent, shards, -0.22, 0.18)
    return jnp.clip(drawn, -reach, reach).astype(kind)


def setup_inputs(seed: int = 0) -> dict:
    streams_of = jax.random.split(jax.random.key(seed), 17)
    return {
        "inputs": noise(streams_of[0], (TOKENS, D), 1.0, 6.0, ((0, 32),)),
        "positions": draw_positions(jax.random.fold_in(streams_of[16], 71), 0),
        "segments": draw_segments(jax.random.fold_in(streams_of[16], 71), 0),
        "cotangent": noise(streams_of[3], (TOKENS, D), 1.0, 6.0, ((0, 32),)),
        "ln1_gain": jnp.clip(1.0 + 0.1 * jax.random.normal(streams_of[4], (D,), jnp.float32), 0.5, 1.5).astype(jnp.bfloat16),
        "ln1_bias": noise(streams_of[5], (D,), 0.5, 3.0, ((0, 4),)),
        "w_qkv": noise(streams_of[6], (D, 3 * D), D ** -0.5, 0.15625, ((0, 4),)),
        "qv_bias": noise(streams_of[7], (2 * D,), 0.5, 3.0, ((0, 4),)),
        "w_out": noise(streams_of[8], (D, D), (max(D // 256, 1)) ** -0.5, 2.5, ((0, 4),)),
        "out_bias": noise(streams_of[9], (D,), 0.5, 3.0, ((0, 4),)),
        "ln2_gain": jnp.clip(1.0 + 0.1 * jax.random.normal(streams_of[10], (D,), jnp.float32), 0.5, 1.5).astype(jnp.bfloat16),
        "ln2_bias": noise(streams_of[11], (D,), 0.5, 3.0, ((0, 4),)),
        "w_fc": noise(streams_of[12], (D, FF), D ** -0.5, 0.15625, ((0, 4),)),
        "fc_bias": noise(streams_of[13], (FF,), 0.5, 3.0, ((0, 4),)),
        "w_proj": noise(streams_of[14], (FF, D), FF ** -0.5, 0.078125, ((0, 4),)),
        "proj_bias": noise(streams_of[15], (D,), 0.5, 3.0, ((0, 4),)),
    }


@jax.custom_vjp
def low(v):
    return lax.optimization_barrier(v.astype(jnp.bfloat16)).astype(jnp.float32)

@jax.custom_vjp
def low_back(v):
    return v

def low_keep(v):
    return (low(v), None)

def low_pass(kept, grad):
    return (grad,)

def back_keep(v):
    return (v, None)

def back_low(kept, grad):
    return (low(grad),)
low.defvjp(low_keep, low_pass)
low_back.defvjp(back_keep, back_low)
EPSILON = 1e-05
HIGHEST = lax.Precision.HIGHEST

def round_both(values):
    return low_back(low(values))

def normalize(values, gain, offset):
    centre = lax.optimization_barrier(jnp.mean(values, axis=-1, keepdims=True))
    centred = values - centre
    spread = lax.optimization_barrier(jnp.mean(centred * centred, axis=-1, keepdims=True))
    return centred * lax.rsqrt(spread + EPSILON) * gain + offset

def matmul(left, right):
    return jnp.dot(left, right, precision=HIGHEST)

def attention(queries, keys_all, values_all, token_pos, token_seg):
    qblock = math.gcd(SEQ, 512)
    score_scale = 1.0 / math.sqrt(HEAD_DIM)
    query_blocks = queries.reshape(SEQ // qblock, qblock, HEADS, HEAD_DIM)
    pos_blocks = token_pos.reshape(SEQ // qblock, qblock)
    seg_blocks = token_seg.reshape(SEQ // qblock, qblock)
    key_group = token_pos // BLOCK

    def one_block(items):
        query_rows, query_pos, query_seg = items
        scores = jnp.einsum('thd,shd->hts', query_rows, keys_all, precision=HIGHEST) * score_scale
        same_doc = query_seg[:, None] == token_seg[None, :]
        earlier = key_group[None, :] <= (query_pos // BLOCK)[:, None]
        allowed = jnp.logical_and(same_doc, earlier)
        scores = low_back(jnp.where(allowed[None], scores, -1e+30))
        weights = low(jax.nn.softmax(scores, axis=-1))
        return jnp.einsum('hts,shd->thd', weights, values_all, precision=HIGHEST)
    mixed = lax.map(jax.checkpoint(one_block), (query_blocks, pos_blocks, seg_blocks))
    return mixed.reshape(SEQ, D)

def block_layer(resid_in, token_pos, token_seg, params):
    ln1_gain, ln1_bias, w_qkv, qv_bias, w_out, out_bias, ln2_gain, ln2_bias, w_fc, fc_bias, w_proj, proj_bias = params
    hidden_one = low(normalize(resid_in, ln1_gain, ln1_bias))
    packed = matmul(hidden_one, w_qkv)
    queries = round_both(packed[:, :D] + qv_bias[:D]).reshape(SEQ, HEADS, HEAD_DIM)
    keys_all = round_both(packed[:, D:2 * D]).reshape(SEQ, HEADS, HEAD_DIM)
    values_all = round_both(packed[:, 2 * D:] + qv_bias[D:]).reshape(SEQ, HEADS, HEAD_DIM)
    mixed = round_both(attention(queries, keys_all, values_all, token_pos, token_seg))
    middle = resid_in + low_back(matmul(mixed, w_out) + out_bias)
    hidden_two = low(normalize(middle, ln2_gain, ln2_bias))
    pre_act = low_back(matmul(hidden_two, w_fc) + fc_bias)
    activated = low(jax.nn.gelu(pre_act, approximate=True))
    return middle + low_back(matmul(activated, w_proj) + proj_bias)

def reference(inputs, positions, segments, cotangent, ln1_gain, ln1_bias, w_qkv, qv_bias, w_out, out_bias, ln2_gain, ln2_bias, w_fc, fc_bias, w_proj, proj_bias):
    params = tuple((weight.astype(jnp.float32) for weight in (ln1_gain, ln1_bias, w_qkv, qv_bias, w_out, out_bias, ln2_gain, ln2_bias, w_fc, fc_bias, w_proj, proj_bias)))
    seq_inputs = inputs.astype(jnp.float32).reshape(SEQS, SEQ, D)
    seq_cotangent = cotangent.astype(jnp.float32).reshape(SEQS, SEQ, D)
    seq_pos = positions.reshape(SEQS, SEQ)
    seq_seg = segments.reshape(SEQS, SEQ)

    def per_sequence(totals, items):
        resid_in, cot_rows, token_pos, token_seg = items

        def forward(resid_rows, *weights):
            return block_layer(resid_rows, token_pos, token_seg, weights)
        result, pullback = jax.vjp(forward, resid_in, *params)
        grads = pullback(cot_rows)
        totals = tuple((total + grad for total, grad in zip(totals, grads[1:])))
        return (totals, (result.astype(jnp.bfloat16), grads[0]))
    zeros_init = tuple((jnp.zeros_like(weight) for weight in params))
    totals, (results, input_grads) = lax.scan(per_sequence, zeros_init, (seq_inputs, seq_cotangent, seq_pos, seq_seg))
    return (results.reshape(TOKENS, D), input_grads.reshape(TOKENS, D), totals[0], totals[1], totals[2], totals[3], totals[4], totals[5], totals[6], totals[7], totals[8], totals[9], totals[10], totals[11])
```

```python
import functools
import math

import jax
import jax.numpy as jnp
from jax import lax
from jax.experimental import pallas as pl
from jax.experimental.pallas import tpu as pltpu
from jax.sharding import Mesh, PartitionSpec as P

HEAD_DIM = 64
BLOCK = 256
EPSILON = 1e-05
NEGATIVE = -1e30
SEG_STEP = 65536
BF16 = jnp.bfloat16
F32 = jnp.float32


def attention_forward_kernel(q_ref, k_ref, v_ref, codeq_ref, codek_ref, out_ref, lse_ref):
    heads = q_ref.shape[1] // HEAD_DIM
    code_q = codeq_ref[...]
    low_q = (code_q // SEG_STEP) * SEG_STEP
    code_k = codek_ref[...]
    allowed = jnp.logical_and(code_k >= low_q, code_k <= code_q)
    outs = []
    sums = []
    for h in range(heads):
        cols = slice(h * HEAD_DIM, (h + 1) * HEAD_DIM)
        scores = lax.dot_general(
            q_ref[:, cols], k_ref[:, cols], (((1,), (1,)), ((), ())), preferred_element_type=F32
        )
        scores = jnp.where(allowed, scores, NEGATIVE)
        top = jnp.max(scores, axis=-1, keepdims=True)
        unnorm = jnp.exp(scores - top)
        total = jnp.sum(unnorm, axis=-1, keepdims=True)
        mixed = jnp.dot(unnorm.astype(BF16), v_ref[:, cols], preferred_element_type=F32)
        outs.append((mixed / total).astype(BF16))
        sums.append(top + jnp.log(total))
    out_ref[...] = jnp.concatenate(outs, axis=1)
    lse_ref[...] = jnp.concatenate(sums, axis=1)


def attention_backward_kernel(
    q_ref, k_ref, v_ref, do_ref, lse_ref, codeq_ref, codek_ref, dq_ref, dk_ref, dv_ref, dk_acc, dv_acc
):
    step = pl.program_id(0)
    heads = q_ref.shape[1] // HEAD_DIM

    @pl.when(step == 0)
    def _():
        dk_acc[...] = jnp.zeros_like(dk_acc)
        dv_acc[...] = jnp.zeros_like(dv_acc)

    code_q = codeq_ref[...]
    low_q = (code_q // SEG_STEP) * SEG_STEP
    code_k = codek_ref[...]
    allowed = jnp.logical_and(code_k >= low_q, code_k <= code_q)
    dqs = []
    dks = []
    dvs = []
    contract_last = (((1,), (1,)), ((), ()))
    contract_first = (((0,), (0,)), ((), ()))
    for h in range(heads):
        cols = slice(h * HEAD_DIM, (h + 1) * HEAD_DIM)
        q = q_ref[:, cols]
        do = do_ref[:, cols]
        k = k_ref[:, cols]
        scores = lax.dot_general(q, k, contract_last, preferred_element_type=F32)
        scores = jnp.where(allowed, scores, NEGATIVE)
        probs = jnp.exp(scores - lse_ref[:, h : h + 1])
        dp = lax.dot_general(do, v_ref[:, cols], contract_last, preferred_element_type=F32)
        delta = jnp.sum(probs * dp, axis=-1, keepdims=True)
        ds = (probs * (dp - delta)).astype(BF16)
        dqs.append(jnp.dot(ds, k, preferred_element_type=F32))
        dks.append(lax.dot_general(ds, q, contract_first, preferred_element_type=F32))
        dvs.append(
            lax.dot_general(probs.astype(BF16), do, contract_first, preferred_element_type=F32)
        )
    scale = 1.0 / math.sqrt(HEAD_DIM)
    dq_ref[...] = (jnp.concatenate(dqs, axis=1) * scale).astype(BF16)
    dk_acc[...] += jnp.concatenate(dks, axis=1)
    dv_acc[...] += jnp.concatenate(dvs, axis=1)

    @pl.when(step == pl.num_programs(0) - 1)
    def _():
        dk_ref[...] = dk_acc[...].astype(BF16)
        dv_ref[...] = dv_acc[...].astype(BF16)


QUERY_ROWS = 256


def attention_forward(q, k, v, code):
    tokens, width = q.shape
    heads = width // HEAD_DIM
    rows = min(QUERY_ROWS, tokens)
    row_block = pl.BlockSpec((rows, width), lambda i: (i, 0))
    whole = pl.BlockSpec((tokens, width), lambda i: (0, 0))
    pairs = heads * tokens * tokens
    return pl.pallas_call(
        attention_forward_kernel,
        grid=(tokens // rows,),
        in_specs=[
            row_block,
            whole,
            whole,
            pl.BlockSpec((rows, 1), lambda i: (i, 0)),
            pl.BlockSpec((1, tokens), lambda i: (0, 0)),
        ],
        out_specs=[row_block, pl.BlockSpec((rows, heads), lambda i: (i, 0))],
        out_shape=[
            jax.ShapeDtypeStruct((tokens, width), BF16),
            jax.ShapeDtypeStruct((tokens, heads), F32),
        ],
        compiler_params=pltpu.CompilerParams(vmem_limit_bytes=48 << 20),
        cost_estimate=pl.CostEstimate(
            flops=4 * pairs * HEAD_DIM, bytes_accessed=8 * tokens * width, transcendentals=pairs
        ),
        name="attention_forward",
    )(q, k, v, code.reshape(tokens, 1), code.reshape(1, tokens))


def attention_backward(q, k, v, do, lse, code):
    tokens, width = q.shape
    heads = width // HEAD_DIM
    rows = min(QUERY_ROWS, tokens)
    row_block = pl.BlockSpec((rows, width), lambda i: (i, 0))
    whole = pl.BlockSpec((tokens, width), lambda i: (0, 0))
    pairs = heads * tokens * tokens
    return pl.pallas_call(
        attention_backward_kernel,
        grid=(tokens // rows,),
        in_specs=[
            row_block,
            whole,
            whole,
            row_block,
            pl.BlockSpec((rows, heads), lambda i: (i, 0)),
            pl.BlockSpec((rows, 1), lambda i: (i, 0)),
            pl.BlockSpec((1, tokens), lambda i: (0, 0)),
        ],
        out_specs=[row_block, whole, whole],
        out_shape=[jax.ShapeDtypeStruct((tokens, width), BF16)] * 3,
        scratch_shapes=[pltpu.VMEM((tokens, width), F32)] * 2,
        compiler_params=pltpu.CompilerParams(vmem_limit_bytes=48 << 20),
        cost_estimate=pl.CostEstimate(
            flops=10 * pairs * HEAD_DIM, bytes_accessed=14 * tokens * width, transcendentals=pairs
        ),
        name="attention_backward",
    )(q, k, v, do, lse, code.reshape(tokens, 1), code.reshape(1, tokens))


def swap(x, axis, bit):
    size = lax.axis_size(axis)
    return lax.ppermute(x, axis, [(i, i ^ bit) for i in range(size)])


def bits_of(size):
    return [1 << i for i in range(size.bit_length() - 1)]


def unxor(blocks, index):
    blocks = list(blocks)
    for bit in bits_of(len(blocks)):
        on = (index & bit) != 0
        blocks = [jnp.where(on, blocks[m ^ bit], blocks[m]) for m in range(len(blocks))]
    return blocks


CORE = ("s", 1)


def plane_orders():
    chips = [("s", 2)] + [("r", bit) for bit in bits_of(lax.axis_size("r"))]
    return [chips + [CORE], chips[::-1] + [CORE]]


def plane_gather(x):
    rows = x.shape[0]
    halves = []
    for part, order in enumerate(plane_orders()):
        state = x[part * rows // 2 : (part + 1) * rows // 2][None]
        for axis, bit in order:
            state = jnp.concatenate([state, swap(state, axis, bit)], axis=0)
        halves.append(state)
    return jnp.stack(halves)


def plane_masks():
    found = []
    for order in plane_orders():
        masks = [(0, 0)]
        for axis, bit in order:
            step = (bit, 0) if axis == "s" else (0, bit)
            masks = masks + [(a ^ step[0], b ^ step[1]) for a, b in masks]
        found.append(masks)
    return found


def plane_scatter(partial):
    done = []
    for part, order in enumerate(plane_orders()):
        state = partial[part]
        for axis, bit in order[::-1]:
            keep, send = jnp.split(state, 2, axis=0)
            state = keep.astype(F32) + swap(send.astype(BF16), axis, bit).astype(F32)
        done.append(state[0])
    return jnp.concatenate(done, axis=0)


def sum_over_line(x, backward):
    size = lax.axis_size("z")
    me = lax.axis_index("z")
    order = list(range(size))
    if backward:
        order = order[::-1]
    total = x
    for i in range(size - 1):
        arrived = lax.ppermute(total, "z", [(order[i], order[i + 1])])
        total = (x.astype(F32) + arrived.astype(F32)).astype(BF16)
    current = total
    for i in reversed(range(size - 1)):
        current = lax.ppermute(current, "z", [(order[i + 1], order[i])])
        total = jnp.where(me == order[i], current, total)
    return total


def gather_over_r(x):
    state = x[None]
    for bit in bits_of(lax.axis_size("r")):
        state = jnp.concatenate([state, swap(state, "r", bit)], axis=0)
    return [state[m] for m in range(state.shape[0])]


def sum_everywhere(x):
    for axis in ("s", "r", "z"):
        for bit in bits_of(lax.axis_size(axis)):
            x = x + swap(x, axis, bit)
    return x


def transposed(x):
    z_size, r_size, s_size = (lax.axis_size(a) for a in ("z", "r", "s"))
    perm = [
        ((z * r_size + r) * s_size + s, (s * r_size + r) * s_size + z)
        for z in range(z_size)
        for r in range(r_size)
        for s in range(s_size)
    ]
    return lax.ppermute(x, ("z", "r", "s"), perm)


def gather_over_s(x):
    state = x[None]
    for bit in (2, 1):
        state = jnp.concatenate([state, swap(state, "s", bit)], axis=0)
    return [state[0], state[2], state[1], state[3]]


def norm_parts(values):
    centre = jnp.mean(values, axis=-1, keepdims=True)
    centred = values - centre
    spread = jnp.mean(centred * centred, axis=-1, keepdims=True)
    inverse = lax.rsqrt(spread + EPSILON)
    return centred * inverse, inverse


def norm_backward(grad, normed, inverse, gain):
    scaled = grad * gain
    mean_scaled = jnp.mean(scaled, axis=-1, keepdims=True)
    mean_product = jnp.mean(scaled * normed, axis=-1, keepdims=True)
    grad_in = inverse * (scaled - mean_scaled - normed * mean_product)
    return grad_in, jnp.sum(grad * normed, axis=0), jnp.sum(grad, axis=0)


def gelu_parts(u):
    c = math.sqrt(2.0 / math.pi)
    squared = u * u
    t = jnp.tanh(c * (u + 0.044715 * (u * squared)))
    half = 0.5 * (1.0 + t)
    slope = half + 0.5 * u * (1.0 - t * t) * (c * (1.0 + 3.0 * 0.044715 * squared))
    return u * half, slope


def dot(a, b, contract=((1,), (0,))):
    return lax.dot_general(a, b, (contract, ((), ())), preferred_element_type=F32)


ACROSS_TOKENS = ((0,), (0,))
ON_LAST = ((1,), (1,))


def local(
    inputs,
    positions,
    segments,
    cotangent,
    ln1_gain,
    ln1_bias,
    w_qkv,
    qv_bias,
    w_out,
    out_bias,
    ln2_gain,
    ln2_bias,
    w_fc,
    fc_bias,
    w_proj,
    proj_bias,
):
    s = lax.axis_index("s")
    r = lax.axis_index("r")
    s_size = lax.axis_size("s")
    r_size = lax.axis_size("r")
    devices = s_size * r_size
    me = s * r_size + r
    rows, width = inputs.shape
    heads = width // HEAD_DIM
    tokens = rows * devices
    own_heads = -(-heads // devices)
    own_cols = own_heads * HEAD_DIM
    ff = w_fc.shape[1]
    own_ff = ff // devices
    shard_rows = width // s_size
    score_scale = 1.0 / math.sqrt(HEAD_DIM)

    x_low = transposed(inputs)
    cot_low = transposed(cotangent)
    code = transposed(segments * SEG_STEP + positions // BLOCK)

    small = [ln1_gain, ln1_bias, qv_bias, out_bias, ln2_gain, ln2_bias, proj_bias]
    small_sizes = [a.shape[0] for a in small]
    small_blocks = jnp.stack(unxor(gather_over_s(jnp.concatenate(small)), s))
    small_full = []
    start = 0
    for size in small_sizes:
        small_full.append(small_blocks[:, start : start + size].reshape(-1).astype(F32))
        start += size
    gain_one, bias_one, qv_full, outb_full, gain_two, bias_two, projb_full = small_full

    def head_pad(a):
        missing = own_heads * devices * HEAD_DIM - width
        return jnp.pad(a, [(0, 0)] * (a.ndim - 1) + [(0, missing)])

    qkv_split = jnp.stack(
        [head_pad(part).reshape(shard_rows, devices, own_cols) for part in jnp.split(w_qkv, 3, axis=1)],
        axis=2,
    )
    qkv_split = jnp.transpose(qkv_split, (1, 0, 2, 3)).reshape(devices, shard_rows, 3 * own_cols)

    def for_others(split):
        got = []
        for m in range(s_size):
            mine = lax.dynamic_index_in_dim(split, (s ^ m) * r_size + r, 0, keepdims=False)
            got.append(mine if m == 0 else swap(mine, "s", m))
        return jnp.concatenate(unxor(got, s), axis=0)

    own_qkv = for_others(qkv_split)

    resid = x_low.astype(F32)
    normed_one, inverse_one = norm_parts(resid)
    hidden_one_own = (normed_one * gain_one + bias_one).astype(BF16)
    hidden_one = plane_gather(hidden_one_own).reshape(tokens, width)
    code_all = plane_gather(code).reshape(tokens)
    packed = dot(hidden_one, own_qkv)
    q_bias = lax.dynamic_slice_in_dim(head_pad(qv_full[:width]), me * own_cols, own_cols)
    v_bias = lax.dynamic_slice_in_dim(head_pad(qv_full[width:]), me * own_cols, own_cols)
    queries = (packed[:, :own_cols] + q_bias).astype(BF16) * jnp.asarray(score_scale, BF16)
    keys = packed[:, own_cols : 2 * own_cols].astype(BF16)
    values = (packed[:, 2 * own_cols :] + v_bias).astype(BF16)
    attended, lse = attention_forward(queries, keys, values, code_all)

    att_blocks = attended.reshape(2, devices, rows // 2, own_cols)
    masks = plane_masks()
    got = {}
    for m in range(devices):
        mask = (m // r_size, m % r_size)
        block = jnp.concatenate([att_blocks[part, masks[part].index(mask)] for part in range(2)], axis=0)
        if mask[0]:
            block = swap(block, "s", mask[0]) if not mask[1] else block
        if mask[1] and not mask[0]:
            block = swap(block, "r", mask[1])
        elif mask[0] and mask[1]:
            pairs = [
                (a * s_size + b, (a ^ mask[1]) * s_size + (b ^ mask[0]))
                for a in range(r_size)
                for b in range(s_size)
            ]
            block = lax.ppermute(block, ("r", "s"), pairs)
        got[m] = block
    attended_own = jnp.concatenate(unxor([got[m] for m in range(devices)], me), axis=1)[:, :width]

    full_out = jnp.concatenate(unxor(gather_over_s(w_out), s), axis=0)
    middle = resid + (dot(attended_own, full_out) + outb_full)
    normed_two, inverse_two = norm_parts(middle)
    hidden_two_own = (normed_two * gain_two + bias_two).astype(BF16)
    hidden_two = plane_gather(hidden_two_own).reshape(tokens, width)
    cot = plane_gather(cot_low).reshape(tokens, width)

    fc_split = jnp.stack(jnp.split(w_fc, devices, axis=1))
    own_fc = for_others(fc_split)
    own_fcb = lax.dynamic_slice_in_dim(fc_bias, r * own_ff, own_ff).astype(F32)
    own_proj = lax.dynamic_slice_in_dim(w_proj, r * own_ff, own_ff, axis=0)
    pre_act = dot(hidden_two, own_fc) + own_fcb
    activated, slope = gelu_parts(pre_act)
    activated = activated.astype(BF16)
    grad_act = dot(cot, own_proj, ON_LAST)
    grad_pre = (grad_act * slope).astype(BF16)
    plane_shape = (2, devices, rows // 2, width)
    grad_w_proj = dot(activated, cot, ACROSS_TOKENS).astype(BF16)
    grad_hidden_two = plane_scatter(dot(grad_pre, own_fc, ON_LAST).astype(BF16).reshape(plane_shape))
    grad_w_fc = dot(hidden_two, grad_pre, ACROSS_TOKENS).astype(BF16)
    proj_sum = plane_scatter(dot(activated, own_proj).astype(BF16).reshape(plane_shape))
    output_own = (middle + (proj_sum + projb_full)).astype(BF16)
    grad_fcb = jnp.sum(grad_pre.astype(F32), axis=0)

    cot_own = cot_low.astype(F32)
    grad_in_two, grad_gain_two, grad_bias_two = norm_backward(
        grad_hidden_two, normed_two, inverse_two, gain_two
    )
    grad_middle = cot_own + grad_in_two
    grad_branch_own = grad_middle.astype(BF16)
    grad_outb = jnp.sum(grad_branch_own.astype(F32), axis=0)
    grad_projb = jnp.sum(cot_own, axis=0)
    grad_branch = plane_gather(grad_branch_own).reshape(tokens, width)
    padded_out = jnp.pad(full_out, ((0, own_cols * devices - width), (0, 0)))
    own_out = lax.dynamic_slice_in_dim(padded_out, me * own_cols, own_cols, axis=0)
    grad_attended = dot(grad_branch, own_out, ON_LAST).astype(BF16)
    dq, dk, dv = attention_backward(queries, keys, values, grad_attended, lse, code_all)
    grad_packed = jnp.concatenate([dq, dk, dv], axis=1)

    attended_all = plane_gather(attended_own).reshape(tokens, width)
    own_rows = shard_rows // r_size
    attended_cols = lax.dynamic_slice_in_dim(attended_all, me * own_rows, own_rows, axis=1)
    grad_w_out = dot(attended_cols, grad_branch, ACROSS_TOKENS).astype(BF16)

    grad_hidden_one = plane_scatter(dot(grad_packed, own_qkv, ON_LAST).astype(BF16).reshape(plane_shape))
    grad_w_qkv = dot(hidden_one, grad_packed, ACROSS_TOKENS).astype(BF16)
    grad_in_one, grad_gain_one, grad_bias_one = norm_backward(
        grad_hidden_one, normed_one, inverse_one, gain_one
    )
    input_grad_own = grad_middle + grad_in_one
    output = transposed(output_own)
    input_grad = transposed(input_grad_own.astype(BF16)).astype(F32)

    grad_qb = jnp.sum(dq.astype(F32), axis=0)
    grad_vb = jnp.sum(dv.astype(F32), axis=0)

    def placed(values_in, total, offset):
        zeros = jnp.zeros((total,), F32)
        return lax.dynamic_update_slice_in_dim(zeros, values_in, offset, axis=0)

    head_total = own_cols * devices
    vector = jnp.concatenate(
        [
            grad_gain_one,
            grad_bias_one,
            placed(grad_qb, head_total, me * own_cols)[:width],
            placed(grad_vb, head_total, me * own_cols)[:width],
            grad_outb,
            grad_gain_two,
            grad_bias_two,
            placed(grad_fcb, ff, me * own_ff),
            grad_projb,
        ]
    )
    summed = sum_everywhere(vector)
    pieces = []
    start = 0
    for size in (width, width, 2 * width, width, width, width, ff, width):
        own = size // s_size
        pieces.append(lax.dynamic_slice_in_dim(summed, start + s * own, own))
        start += size
    g_gain_one, g_bias_one, g_qv, g_outb, g_gain_two, g_bias_two, g_fcb, g_projb = pieces

    def rows_home(grad, chunks):
        size = grad.shape[0] // chunks
        parts = [
            sum_over_line(grad[i * size : (i + 1) * size], i % 2 == 1) for i in range(chunks)
        ]
        per_part = [gather_over_r(part) for part in parts]
        by_r = [
            jnp.concatenate([per_part[i][m] for i in range(chunks)], axis=0) for m in range(r_size)
        ]
        return jnp.concatenate(unxor(by_r, r), axis=0).astype(F32)

    def columns_home(grad):
        blocks = unxor(jnp.split(grad, s_size, axis=0), s)
        found = [[None] * s_size for _ in range(r_size)]
        for m in range(s_size):
            part = sum_over_line(blocks[m], m % 2 == 1)
            part = part if m == 0 else swap(part, "s", m)
            for j, block in enumerate(gather_over_r(part)):
                found[j][m] = block
        by_r = [unxor(found[j], s) for j in range(r_size)]
        by_s = [unxor([by_r[j][i] for j in range(r_size)], r) for i in range(s_size)]
        return [by_s[i][j] for i in range(s_size) for j in range(r_size)]

    g_proj = rows_home(grad_w_proj, 4)
    g_fc = jnp.concatenate(columns_home(grad_w_fc), axis=1).astype(F32)
    g_out = rows_home(grad_w_out, 1)
    qkv_blocks = columns_home(grad_w_qkv)
    g_qkv = jnp.concatenate(
        [
            jnp.concatenate([b[:, i * own_cols : (i + 1) * own_cols] for b in qkv_blocks], axis=1)[
                :, :width
            ]
            for i in range(3)
        ],
        axis=1,
    ).astype(F32)

    return (
        output,
        input_grad,
        g_gain_one,
        g_bias_one,
        g_qkv,
        g_qv,
        g_out,
        g_outb,
        g_gain_two,
        g_bias_two,
        g_fc,
        g_fcb,
        g_proj,
        g_projb,
    )


def solution(mesh):
    ctx, shard = mesh.devices.shape
    fine = Mesh(mesh.devices.reshape(shard, ctx // shard, shard), ("z", "r", "s"))
    tokens = ("s", "z", "r")
    arg_specs = (
        P(tokens, None),
        P(tokens),
        P(tokens),
        P(tokens, None),
        P("s"),
        P("s"),
        P("s", None),
        P("s"),
        P("s", None),
        P("s"),
        P("s"),
        P("s"),
        P("s", None),
        P("s"),
        P("s", None),
        P("s"),
    )
    out_specs = (P(tokens, None), P(tokens, None)) + arg_specs[4:]
    return jax.shard_map(local, mesh=fine, in_specs=arg_specs, out_specs=out_specs, check_vma=False)
```

```python
import math

import jax
import jax.numpy as jnp
from jax import lax
from jax.experimental import pallas as pl
from jax.experimental.pallas import tpu as pltpu
from jax.sharding import Mesh, PartitionSpec as P

HEAD_DIM = 64
BLOCK = 256
EPSILON = 1e-05
NEGATIVE = -1e30
SEG_STEP = 65536
BF16 = jnp.bfloat16
F32 = jnp.float32


def bits_of(size):
    return [1 << i for i in range(size.bit_length() - 1)]


def norm_parts(values):
    centre = jnp.mean(values, axis=-1, keepdims=True)
    centred = values - centre
    spread = jnp.mean(centred * centred, axis=-1, keepdims=True)
    inverse = lax.rsqrt(spread + EPSILON)
    return centred * inverse, inverse


def gelu_parts(u):
    c = math.sqrt(2.0 / math.pi)
    squared = u * u
    t = jnp.tanh(c * (u + 0.044715 * (u * squared)))
    half = 0.5 * (1.0 + t)
    slope = half + 0.5 * u * (1.0 - t * t) * (c * (1.0 + 3.0 * 0.044715 * squared))
    return u * half, slope


def dot(a, b, contract=((1,), (0,))):
    return lax.dot_general(a, b, (contract, ((), ())), preferred_element_type=F32)


ACROSS_TOKENS = ((0,), (0,))
ON_LAST = ((1,), (1,))


MESH_ID = pl.DeviceIdType.MESH


def remote(src, dst, send_sem, recv_sem, **device):
    return pltpu.make_async_remote_copy(
        src_ref=src,
        dst_ref=dst,
        send_sem=send_sem,
        recv_sem=recv_sem,
        device_id=device,
        device_id_type=MESH_ID,
    )


def partner(axis, bit):
    return {axis: lax.axis_index(axis) ^ bit}


def plane_device(offset, r_size):
    found = {}
    if offset // r_size:
        found["s"] = lax.axis_index("s") ^ (offset // r_size)
    if offset % r_size:
        found["r"] = lax.axis_index("r") ^ (offset % r_size)
    return found


def tree_of(order, r_size):
    levels = []
    known = [(0, 0)]
    for axis, bit in order:
        step = bit * r_size if axis == "s" else bit
        known = known + [(o ^ step, depth + 1) for o, depth in known]
    found = {}
    for o, depth in known:
        if o == 0:
            continue
        for axis, bit in order[::-1]:
            step = bit * r_size if axis == "s" else bit
            if o & step:
                found.setdefault(depth, []).append((o, o ^ step, axis, bit))
                break
    for depth in sorted(found):
        levels.append(found[depth])
    return levels


def chip_orders(r_size):
    chips = [("s", 2)] + [("r", bit) for bit in bits_of(r_size)]
    return [chips + [("s", 1)], chips[::-1] + [("s", 1)]]


class Gather:
    def __init__(self, block, send_sem, recv_sem, r_size, parts=2, own=None):
        self.block = block
        self.own = own or block
        self.send_sem = send_sem
        self.recv_sem = recv_sem
        self.levels = [tree_of(order, r_size) for order in chip_orders(r_size)[:parts]]
        self.parts = parts
        self.arrived = set()

    def copy(self, part, transfer):
        offset, source, axis, bit = transfer
        src = self.own(0, part) if source == 0 else self.block(source, part)
        return remote(
            src,
            self.block(offset, part),
            self.send_sem.at[part, offset],
            self.recv_sem.at[part, offset],
            **partner(axis, bit),
        )

    def transfers(self):
        for level in range(len(self.levels[0])):
            for i in range(len(self.levels[0][level])):
                for part in range(self.parts):
                    yield level, part, self.levels[part][level][i]

    def find(self, part, offset):
        for _, p, t in self.transfers():
            if p == part and t[0] == offset:
                return t

    def need(self, part, offset):
        if offset and (part, offset) not in self.arrived:
            self.arrived.add((part, offset))
            self.copy(part, self.find(part, offset)).wait_recv()

    def start(self, level):
        for lv, part, t in self.transfers():
            if lv == level:
                self.need(part, t[1])
                self.copy(part, t).start()

    def start_rest(self):
        for level in range(1, len(self.levels[0])):
            self.start(level)

    def need_all(self):
        for _, part, t in self.transfers():
            self.need(part, t[0])

    def close(self):
        self.need_all()
        for _, part, t in self.transfers():
            self.copy(part, t).wait_send()


def attention_rows(rows, first, q_ref, k_ref, v_ref, code_q, code_k):
    heads = q_ref.shape[1] // HEAD_DIM
    low_q = (code_q // SEG_STEP) * SEG_STEP
    allowed = jnp.logical_and(code_k >= low_q, code_k <= code_q)
    outs = []
    sums = []
    for h in range(heads):
        cols = slice(h * HEAD_DIM, (h + 1) * HEAD_DIM)
        scores = lax.dot_general(
            q_ref[pl.ds(first, rows), cols],
            k_ref[:, cols],
            (((1,), (1,)), ((), ())),
            preferred_element_type=F32,
        )
        scores = jnp.where(allowed, scores, NEGATIVE)
        top = jnp.max(scores, axis=-1, keepdims=True)
        unnorm = jnp.exp(scores - top)
        total = jnp.sum(unnorm, axis=-1, keepdims=True)
        mixed = jnp.dot(unnorm.astype(BF16), v_ref[:, cols], preferred_element_type=F32)
        outs.append((mixed / total).astype(BF16))
        sums.append(top + jnp.log(total))
    return jnp.concatenate(outs, axis=1), jnp.concatenate(sums, axis=1)


def split_rows(n):
    first = -(-n // 32) * 16
    return ((0, first), (first, n - first))


class WeightPush:
    def __init__(self, source, dest, rows, send_sem, recv_sem, across):
        self.source, self.dest, self.rows = source, dest, rows
        self.send_sem, self.recv_sem = send_sem, recv_sem
        self.across = across

    def core_copy(self):
        s = lax.axis_index("s")
        return remote(
            self.source(s ^ 1),
            self.dest(s, 0, self.rows),
            self.send_sem.at[0],
            self.recv_sem.at[0],
            s=s ^ 1,
        )

    def chip_copy(self, m, part, landed=None):
        s = lax.axis_index("s")
        first, count = split_rows(self.rows)[part]
        return remote(
            self.source(s ^ m).at[pl.ds(first, count)],
            self.dest(s, first, count),
            self.send_sem.at[m],
            self.recv_sem.at[m],
            s=s ^ m,
        )

    def relay_copy(self, m, part):
        s = lax.axis_index("s")
        first, count = split_rows(self.rows)[part]
        ref = self.dest(s ^ m, first, count)
        return remote(
            ref, ref, self.send_sem.at[2 + m], self.recv_sem.at[2 + m], z=lax.axis_index("z") ^ 1
        )

    def per_part(self, act):
        odd = lax.axis_index("z") % 2
        for part in range(2):

            @pl.when(odd == part)
            def _(part=part):
                act(part)

    def start(self):
        if 1 in self.across:
            self.core_copy().start()

        def act(part):
            for m in self.across:
                if m != 1:
                    self.chip_copy(m, part).start()

        self.per_part(act)

    def relay(self):
        def act(part):
            for m in self.across:
                if m != 1:
                    self.chip_copy(m, part).wait_recv()
                    self.relay_copy(m, part).start()

        self.per_part(act)

    def need(self):
        if 1 in self.across:
            self.core_copy().wait_recv()

        def act(part):
            for m in self.across:
                if m != 1:
                    self.relay_copy(m, 1 - part).wait_recv()

        self.per_part(act)

    def close(self):
        if 1 in self.across:
            self.core_copy().wait_send()

        def act(part):
            for m in self.across:
                if m != 1:
                    self.chip_copy(m, part).wait_send()
                    self.relay_copy(m, part).wait_send()

        self.per_part(act)


def forward_kernel(
    x_in, cot_in, code_in, small_in, smallh_in, wq_in, wf_in, wo_in,
    h1_out, h2_out, cot_out, wf_out, wq_out, wo_out, q_ref, k_ref, v_ref, att_ref, lse_ref, code_out,
    middle_out, x_own, small_ref, smallh_ref,
    code_land, small_land, smallh_land, h1, wq_vm, stage_q, wf_vm, stage_f, own_q, full_out, att_land, h2_own,
    x_sem, code_sem, cot_sem, small_sem, load_sem, h1_send, h1_recv, cd_send, cd_recv, ct_send, ct_recv, h2_send,
    h2_recv, wq_send, wq_recv, wf_send, wf_recv, wo_send, wo_recv, at_send, at_recv, out_sem,
):
    s, r, z = (lax.axis_index(a) for a in ("s", "r", "z"))
    s_size, r_size = lax.axis_size("s"), lax.axis_size("r")
    devices = s_size * r_size
    me = s * r_size + r
    rows, width = x_in.shape
    tokens = rows * devices
    own_cols = q_ref.shape[1]
    own_ff = wf_out.shape[1]
    shard_rows = wq_in.shape[0]

    def shard_at(i, first=0, count=shard_rows):
        return pl.ds(pl.multiple_of(i * shard_rows + first, 16), count)

    barrier = pltpu.get_barrier_semaphore()
    for offset in range(1, devices):
        pl.semaphore_signal(barrier, inc=1, device_id=plane_device(offset, r_size), device_id_type=MESH_ID)
    pl.semaphore_signal(barrier, inc=1, device_id={"z": z ^ 1}, device_id_type=MESH_ID)

    @pl.when(s != z)
    def _():
        pl.semaphore_signal(barrier, inc=1, device_id={"z": s, "s": z}, device_id_type=MESH_ID)

    pl.semaphore_wait(barrier, devices + jnp.where(s != z, 1, 0))

    def moved(src, dst, sem):
        far = remote(src, dst, sem.at[0], sem.at[1], z=s, s=z)
        near = pltpu.make_async_copy(src, dst, sem.at[1])

        @pl.when(s != z)
        def _():
            far.start()

        @pl.when(s == z)
        def _():
            near.start()

        def arrived():
            @pl.when(s != z)
            def _():
                far.wait_recv()

            @pl.when(s == z)
            def _():
                near.wait()

        def sent():
            @pl.when(s != z)
            def _():
                far.wait_send()

        return arrived, sent

    x_arrived, x_sent = moved(x_in, x_own, x_sem)
    code_arrived, code_sent = moved(code_in, code_land.at[0], code_sem)
    loads = [
        pltpu.make_async_copy(wq_in, wq_vm, load_sem.at[0]),
        pltpu.make_async_copy(wf_in, wf_vm, load_sem.at[1]),
        pltpu.make_async_copy(wo_in, full_out.at[shard_at(s)], load_sem.at[2]),
    ]
    for load in loads:
        load.start()
    small_copies = []
    for m in range(1, s_size):
        small_copies.append(
            remote(small_in, small_land.at[m], small_sem.at[0, m], small_sem.at[1, m], s=s ^ m)
        )
        small_copies.append(
            remote(smallh_in, smallh_land.at[m], small_sem.at[2, m], small_sem.at[3, m], s=s ^ m)
        )
    for copy in small_copies:
        copy.start()
    if full_out.shape[0] > width:
        full_out[width:, :] = jnp.zeros((full_out.shape[0] - width, width), BF16)

    loads[0].wait()
    for s2 in range(s_size):
        for r2 in range(r_size):

            @pl.when(r == r2)
            def _(s2=s2, r2=r2):
                device = s2 * r_size + r2
                for part in range(3):
                    lo = device * own_cols
                    n = max(0, min(own_cols, width - lo))
                    if n:
                        stage_q[s2, :, part * own_cols : part * own_cols + n] = wq_vm[
                            :, part * width + lo : part * width + lo + n
                        ]
                    if n < own_cols:
                        stage_q[s2, :, part * own_cols + n : (part + 1) * own_cols] = jnp.zeros(
                            (shard_rows, own_cols - n), BF16
                        )

    push_q = WeightPush(
        lambda i: stage_q.at[i],
        lambda i, first, count: own_q.at[shard_at(i, first, count)],
        shard_rows, wq_send, wq_recv, (1, 2, 3),
    )
    push_q.start()
    own_q[shard_at(s), :] = stage_q[s]

    for copy in small_copies:
        copy.wait_recv()
    small = small_in[...]
    smallh = smallh_in[...]
    for m in range(1, s_size):
        small = small + small_land[m]
        smallh = smallh + smallh_land[m]
    small_ref[...] = small
    smallh_ref[...] = smallh
    gain_one, bias_one, out_bias, gain_two, bias_two = (small_ref[i : i + 1, :] for i in range(5))
    x_arrived()
    cot_arrived, cot_sent = moved(cot_in, cot_out.at[pl.ds(0, rows)], cot_sem)
    resid = x_own[...].astype(F32)
    normed, _ = norm_parts(resid)
    h1[0:rows, :] = (normed * gain_one + bias_one).astype(BF16)
    half = rows // 2

    def block_of(ref):
        return lambda offset, part: ref.at[pl.ds(offset * rows + part * half, half)]

    gather_one = Gather(block_of(h1), h1_send, h1_recv, r_size)
    gather_one.start(0)
    code_arrived()
    gather_code = Gather(lambda offset, part: code_land.at[offset], cd_send, cd_recv, r_size, parts=1)
    gather_code.start(0)

    loads[1].wait()
    for s2 in range(s_size):
        for r2 in range(r_size):

            @pl.when(r == r2)
            def _(s2=s2, r2=r2):
                lo = (s2 * r_size + r2) * own_ff
                stage_f[s2] = wf_vm[:, lo : lo + own_ff]

    gather_one.start(1)
    gather_code.start(1)
    push_q.relay()
    for level in range(2, len(gather_one.levels[0])):
        gather_one.start(level)
        gather_code.start(level)

    push_o = WeightPush(
        lambda i: full_out.at[shard_at(s)],
        lambda i, first, count: full_out.at[shard_at(i, first, count)],
        shard_rows, wo_send, wo_recv, (1, 2),
    )
    push_f = WeightPush(
        lambda i: stage_f.at[i],
        lambda i, first, count: wf_out.at[shard_at(i, first, count)],
        shard_rows, wf_send, wf_recv, (1, 2, 3),
    )
    own_f = pltpu.make_async_copy(
        stage_f.at[s], wf_out.at[shard_at(s)], load_sem.at[1]
    )
    own_f.start()
    gather_one.need_all()
    loads[2].wait()
    push_o.start()
    push_f.start()

    push_q.need()
    save_q = pltpu.make_async_copy(own_q, wq_out, out_sem.at[0])
    save_q.start()
    save_h = pltpu.make_async_copy(h1, h1_out, out_sem.at[1])
    save_h.start()
    q_bias = smallh_ref[pl.ds(me, 1), :]
    v_bias = smallh_ref[pl.ds(devices + me, 1), :]
    step = min(512, tokens)
    score_scale = jnp.asarray(1.0 / math.sqrt(HEAD_DIM), BF16)

    def project(i, carry):
        at = pl.ds(pl.multiple_of(i * step, step), step)
        packed = jnp.dot(h1[at, :], own_q[...], preferred_element_type=F32)
        q_ref[at, :] = (packed[:, :own_cols] + q_bias).astype(BF16) * score_scale
        k_ref[at, :] = packed[:, own_cols : 2 * own_cols].astype(BF16)
        v_ref[at, :] = (packed[:, 2 * own_cols :] + v_bias).astype(BF16)
        return carry

    lax.fori_loop(0, tokens // step, project, 0)
    cot_arrived()
    gather_cot = Gather(block_of(cot_out), ct_send, ct_recv, r_size)
    gather_cot.start(0)
    gather_code.need_all()
    code_out[...] = code_land[:, 0, :]
    code_row = jnp.concatenate([code_land[i, 0:1, :] for i in range(devices)], axis=1)

    q_rows = min(rows if tokens > 2048 else 256, tokens)

    def attend(i, carry):
        first = pl.multiple_of(i * q_rows, q_rows)
        per = q_rows // rows
        code_col = jnp.concatenate(
            [jnp.transpose(code_land[i * per + j])[:, 0:1] for j in range(per)], axis=0
        )
        out, sums = attention_rows(q_rows, first, q_ref, k_ref, v_ref, code_col, code_row)
        att_ref[pl.ds(first, q_rows), :] = out
        lse_ref[pl.ds(first, q_rows), :] = sums
        return carry

    lax.fori_loop(0, tokens // q_rows, attend, 0)

    at_copies = []
    for offset in range(1, devices):
        at_copies.append(
            remote(
                att_ref.at[pl.ds(offset * rows, rows)],
                att_land.at[me],
                at_send.at[offset],
                at_recv.at[offset],
                **plane_device(offset, r_size),
            )
        )
    for copy in at_copies:
        copy.start()
    att_land[me] = att_ref[0:rows, :]
    push_o.relay()
    push_o.need()
    far = full_out.at[shard_at(s ^ 2)]
    out_core = remote(far, far, wo_send.at[5], wo_recv.at[5], s=s ^ 1)
    out_core.start()
    gather_cot.start(1)
    for copy in at_copies:
        copy.wait_recv()
    out_core.wait_recv()
    middle = resid + out_bias
    for device in range(devices):
        middle = middle + jnp.dot(
            att_land[device],
            full_out[device * own_cols : (device + 1) * own_cols, :],
            preferred_element_type=F32,
        )
    middle_out[...] = middle
    normed, _ = norm_parts(middle)
    h2_own[...] = (normed * gain_two + bias_two).astype(BF16)
    save_h2 = pltpu.make_async_copy(h2_own, h2_out.at[pl.ds(0, rows)], out_sem.at[2])
    save_h2.start()
    gather_two = Gather(
        block_of(h2_out), h2_send, h2_recv, r_size, own=lambda o, part: h2_own.at[pl.ds(part * half, half)]
    )
    gather_two.start(0)
    save_o = pltpu.make_async_copy(
        full_out.at[pl.ds(pl.multiple_of(me * own_cols, own_cols), own_cols)], wo_out, out_sem.at[3]
    )
    save_o.start()
    for level in range(2, len(gather_cot.levels[0])):
        gather_cot.start(level)
    push_f.relay()
    gather_two.start_rest()
    gather_two.close()
    gather_cot.close()
    gather_one.close()
    gather_code.close()
    push_f.need()
    for push in (push_q, push_o, push_f):
        push.close()
    out_core.wait_send()
    for copy in at_copies + small_copies:
        copy.wait_send()
    x_sent()
    code_sent()
    cot_sent()
    own_f.wait()
    for save in (save_q, save_h, save_h2, save_o):
        save.wait()


def forward_part(x, cot, code, small, smallh, w_qkv, w_fc, w_out):
    s_size, r_size = lax.axis_size("s"), lax.axis_size("r")
    devices = s_size * r_size
    rows, width = x.shape
    tokens = rows * devices
    shard_rows = w_qkv.shape[0]
    heads = width // HEAD_DIM
    own_heads = -(-heads // devices)
    own_cols = own_heads * HEAD_DIM
    own_ff = w_fc.shape[1] // devices
    anywhere = pl.BlockSpec(memory_space=pl.ANY)
    vmem = pl.BlockSpec(memory_space=pltpu.VMEM)
    shape = jax.ShapeDtypeStruct
    dma = pltpu.SemaphoreType.DMA
    flops = 2 * tokens * width * 3 * own_cols + 4 * own_heads * tokens * tokens * HEAD_DIM
    return pl.pallas_call(
        forward_kernel,
        in_specs=[anywhere, anywhere, anywhere, vmem, vmem, anywhere, anywhere, anywhere],
        out_specs=[anywhere] * 6 + [vmem] * 10,
        out_shape=[
            shape((tokens, width), BF16),
            shape((tokens, width), BF16),
            shape((tokens, width), BF16),
            shape((width, own_ff), BF16),
            shape((width, 3 * own_cols), BF16),
            shape((own_cols, width), BF16),
            shape((tokens, own_cols), BF16),
            shape((tokens, own_cols), BF16),
            shape((tokens, own_cols), BF16),
            shape((tokens, own_cols), BF16),
            shape((tokens, own_heads), F32),
            shape((devices, rows), jnp.int32),
            shape((rows, width), F32),
            shape((rows, width), BF16),
            shape(small.shape, F32),
            shape(smallh.shape, F32),
        ],
        scratch_shapes=[
            pltpu.VMEM((devices, 8, rows), jnp.int32),
            pltpu.VMEM((s_size,) + small.shape, F32),
            pltpu.VMEM((s_size,) + smallh.shape, F32),
            pltpu.VMEM((tokens, width), BF16),
            pltpu.VMEM(w_qkv.shape, BF16),
            pltpu.VMEM((s_size, shard_rows, 3 * own_cols), BF16),
            pltpu.VMEM(w_fc.shape, BF16),
            pltpu.VMEM((s_size, shard_rows, own_ff), BF16),
            pltpu.VMEM((width, 3 * own_cols), BF16),
            pltpu.VMEM((devices * own_cols, width), BF16),
            pltpu.VMEM((devices, rows, own_cols), BF16),
            pltpu.VMEM((rows, width), BF16),
            dma((2,)), dma((2,)), dma((2,)), dma((4, s_size)), dma((3,)),
            dma((2, devices)), dma((2, devices)), dma((1, devices)), dma((1, devices)),
            dma((2, devices)), dma((2, devices)), dma((2, devices)), dma((2, devices)),
            dma((6,)), dma((6,)), dma((6,)), dma((6,)), dma((6,)), dma((6,)),
            dma((devices,)), dma((devices,)), dma((4,)),
        ],
        compiler_params=pltpu.CompilerParams(
            collective_id=0, has_side_effects=True, vmem_limit_bytes=60 << 20
        ),
        cost_estimate=pl.CostEstimate(flops=flops, bytes_accessed=40 << 20, transcendentals=0),
        name="forward_part",
    )(x, cot, code, small, smallh, w_qkv, w_fc, w_out)


class Scatter:
    def __init__(self, leaf, acc, land, load, send_sem, recv_sem, r_size):
        self.leaf, self.acc, self.land, self.load = leaf, acc, land, load
        self.send_sem, self.recv_sem = send_sem, recv_sem
        self.levels = [tree_of(order, r_size) for order in chip_orders(r_size)]

    def copy(self, part, transfer):
        offset, _, axis, bit = transfer
        src = self.acc(offset, part) if self.children(part, offset) else self.leaf(offset, part)
        return remote(
            src,
            self.land(offset, part),
            self.send_sem.at[part, offset],
            self.recv_sem.at[part, offset],
            **partner(axis, bit),
        )

    def children(self, part, offset):
        return [t for level in self.levels[part] for t in level if t[1] == offset]

    def start_leaves(self):
        for level in range(len(self.levels[0]) - 1, -1, -1):
            for i in range(len(self.levels[0][level])):
                for part in range(2):
                    t = self.levels[part][level][i]
                    if not self.children(part, t[0]):
                        self.copy(part, t).start()

    def total(self, part, offset):
        value = self.acc(offset, part)[...].astype(F32)
        for t in self.children(part, offset)[::-1]:
            self.copy(part, t).wait_recv()
            value = value + self.load(t[0], part).astype(F32)
        return value

    def start_inner(self):
        for level in range(len(self.levels[0]) - 1, -1, -1):
            for i in range(len(self.levels[0][level])):
                for part in range(2):
                    t = self.levels[part][level][i]
                    if self.children(part, t[0]):
                        self.acc(t[0], part)[...] = self.total(part, t[0]).astype(BF16)
                        self.copy(part, t).start()

    def finish(self):
        return jnp.concatenate([self.total(part, 0) for part in range(2)], axis=0)

    def close(self):
        for part in range(2):
            for level in self.levels[part]:
                for t in level:
                    self.copy(part, t).wait_send()


class LineSum:
    def __init__(self, jobs, land, rs_send, rs_recv, ag_send, ag_recv, home):
        self.jobs, self.land = jobs, land
        self.rs_send, self.rs_recv, self.ag_send, self.ag_recv = rs_send, rs_recv, ag_send, ag_recv
        self.home = home
        self.n = jobs.shape[1]
        self.z = lax.axis_index("z")
        self.last = lax.axis_size("z") - 1
        self.first_dir = jnp.where(self.z * 2 > self.last, 1, 0)
        self.outer = jnp.logical_or(self.z == 0, self.z == self.last)

    def place(self, d):
        return jnp.where(d == 0, self.z, self.last - self.z)

    def up(self, d, j):
        return remote(
            self.jobs.at[d, j], self.land.at[d, j], self.rs_send.at[d, j], self.rs_recv.at[d, j], z=self.z + 1 - 2 * d
        )

    def down(self, d, j):
        return remote(
            self.land.at[d, j], self.land.at[d, j], self.ag_send.at[d, j], self.ag_recv.at[d, j], z=self.z - 1 + 2 * d
        )

    def add(self, d, j):
        place = self.place(d)

        @pl.when(place > 0)
        def _():
            self.up(d, j).wait_recv()
            total = (self.jobs[d, j].astype(F32) + self.land[d, j].astype(F32)).astype(BF16)

            @pl.when(place < self.last)
            def _():
                self.jobs[d, j] = total

            @pl.when(place == self.last)
            def _():
                self.land[d, j] = total

        @pl.when(place < self.last)
        def _():
            self.up(d, j).start()

        @pl.when(place == self.last)
        def _():
            self.down(d, j).start()
            self.home(d, j)

    def back(self, d, j):
        place = self.place(d)

        @pl.when(place < self.last)
        def _():
            self.down(d, j).wait_recv()

            @pl.when(place > 0)
            def _():
                self.down(d, j).start()

            self.home(d, j)

    def add_ticks(self, lo, hi):
        def tick(t, carry):
            @pl.when(t < self.n)
            def _():
                self.add(self.first_dir, t)

            u = t - jnp.where(self.outer, 3, 1)

            @pl.when(jnp.logical_and(u >= 0, u < self.n))
            def _():
                self.add(1 - self.first_dir, u)

            return carry

        lax.fori_loop(lo, hi, tick, 0)

    def back_ticks(self, lo, hi):
        def tick(t, carry):
            @pl.when(t < self.n)
            def _():
                self.back(1 - self.first_dir, t)

            u = t - jnp.where(self.outer, 2, 1)

            @pl.when(jnp.logical_and(u >= 0, u < self.n))
            def _():
                self.back(self.first_dir, u)

            return carry

        lax.fori_loop(lo, hi, tick, 0)

    def close(self):
        def one(i, carry):
            d, j = i // self.n, i % self.n
            place = self.place(d)

            @pl.when(place < self.last)
            def _():
                self.up(d, j).wait_send()

            @pl.when(place > 0)
            def _():
                self.down(d, j).wait_send()

            return carry

        lax.fori_loop(0, 2 * self.n, one, 0)


def job_rows(n, most=80):
    for rows in range(most, 15, -16):
        if n % rows == 0:
            return rows
    return n


def norm_backward_rows(grad, normed, inverse, gain):
    scaled = grad * gain
    mean_scaled = jnp.mean(scaled, axis=-1, keepdims=True)
    mean_product = jnp.mean(scaled * normed, axis=-1, keepdims=True)
    grad_in = inverse * (scaled - mean_scaled - normed * mean_product)
    return (
        grad_in,
        jnp.sum(grad * normed, axis=0, keepdims=True),
        jnp.sum(grad, axis=0, keepdims=True),
    )


def backward_kernel(
    part2, partp, gproj, gfc, h1, wq, wo, q_ref, k_ref, v_ref, att_ref, lse_ref, code_ref, middle_ref, x_ref, cot_in,
    small_ref, fcb_ref,
    out_home, ig_home, home_proj, home_fc, home_qkv, home_out, small_out, landp, gb,
    acc2, accp, land, tmp, jp, jf, jq, jo, lp, lf, lq, lo_, own_q, own_o, cot_v, chunk, gq_acc, do_ref, gp,
    dk_acc, dv_acc, go_acc, vec, vec_land, gb_own, out_v, ig_v,
    load_sem, s2_send, s2_recv, sp_send, sp_recv, s1_send, s1_recv, g_send, g_recv, tmp_sem, home_sem, mv_sem,
    vec_send, vec_recv,
    p_rs, p_rr, p_as, p_ar, f_rs, f_rr, f_as, f_ar, q_rs, q_rr, q_as, q_ar, o_rs, o_rr, o_as, o_ar,
    ph_send, ph_recv, fh_send, fh_recv, qh_send, qh_recv, oh_send, oh_recv,
):
    s, r, z = (lax.axis_index(a) for a in ("s", "r", "z"))
    s_size, r_size, z_size = (lax.axis_size(a) for a in ("s", "r", "z"))
    devices = s_size * r_size
    me = s * r_size + r
    rows, width = x_ref.shape
    tokens = rows * devices
    half = rows // 2
    own_cols = q_ref.shape[1]
    own_ff = gfc.shape[3]
    heads = own_cols // HEAD_DIM
    shard_rows = width // s_size

    barrier = pltpu.get_barrier_semaphore()
    for offset in range(1, devices):
        pl.semaphore_signal(barrier, inc=1, device_id=plane_device(offset, r_size), device_id_type=MESH_ID)
    for bit in bits_of(z_size):
        pl.semaphore_signal(barrier, inc=1, device_id={"z": z ^ bit}, device_id_type=MESH_ID)
    inner = jnp.logical_and(z > 0, z < z_size - 1)

    @pl.when(s != z)
    def _():
        pl.semaphore_signal(barrier, inc=1, device_id={"z": s, "s": z}, device_id_type=MESH_ID)

    @pl.when(inner)
    def _():
        pl.semaphore_signal(
            barrier, inc=1, device_id={"z": jnp.where(z % 2 == 1, z + 1, z - 1)}, device_id_type=MESH_ID
        )

    peers = devices - 1 + len(bits_of(z_size))
    pl.semaphore_wait(barrier, peers + jnp.where(s != z, 1, 0) + jnp.where(inner, 1, 0))

    def core_of(offset):
        return (offset // r_size) % 2

    def slot(offset):
        return (offset // r_size) // 2 * r_size + offset % r_size

    def block(ref):
        return lambda o, part: ref.at[pl.ds(o * rows + part * half, half)]

    def packed_block(ref):
        return lambda o, part: ref.at[pl.ds(slot(o) * rows + part * half, half)]

    loads = []
    plain = [(gproj, jp), (gfc, jf), (wq, own_q), (wo, own_o), (cot_in.at[pl.ds(0, rows)], cot_v)]
    for i, (src, dst) in enumerate(plain):
        loads.append(pltpu.make_async_copy(src, dst, load_sem.at[i]))
    acc_loads = []
    for i, (src, dst) in enumerate(((part2, acc2), (partp, accp))):
        for so in range(0, s_size, 2):
            n = r_size * rows
            acc_loads.append(
                pltpu.make_async_copy(
                    src.at[pl.ds(so * n, n)], dst.at[pl.ds(so // 2 * n, n)], load_sem.at[len(plain) + 2 * i + so // 2]
                )
            )
    scatter_two = Scatter(
        block(part2), packed_block(acc2), block(land), lambda o, part: block(land)(o, part)[...], s2_send, s2_recv, r_size
    )

    def load_from_far(o, part):
        copy = pltpu.make_async_copy(block(landp)(o, part), tmp, tmp_sem.at[0])
        copy.start()
        copy.wait()
        return tmp[...]

    scatter_proj = Scatter(
        block(partp), packed_block(accp), block(landp), load_from_far, sp_send, sp_recv, r_size
    )
    scatter_two.start_leaves()
    for copy in acc_loads[:2] + loads + acc_loads[2:]:
        copy.start()
    scatter_proj.start_leaves()

    def to_home(src, dst, send, recv, s_to, m):
        far = remote(src, dst, send, recv, s=s_to, r=r ^ m)
        if m:
            far.start()
        else:
            near = pltpu.make_async_copy(src, dst, recv)

            @pl.when(s_to == s)
            def _():
                near.start()

            @pl.when(s_to != s)
            def _():
                far.start()

    def home_of_proj(d, j):
        for m in range(r_size):
            src, dst = lp.at[d, j], home_proj.at[r, d, j]
            if m:
                remote(src, dst, ph_send.at[m], ph_recv.at[r], r=r ^ m).start()
            else:
                pltpu.make_async_copy(src, dst, ph_recv.at[r]).start()

    def home_of_columns(landing, home, send, recv):
        per = landing.shape[1] // (s_size // 2)

        def go(d, j):
            s_to = d * (s_size // 2) + j // per
            for m in range(r_size):
                to_home(landing.at[d, j], home.at[me, j % per], send.at[s_to, m], recv.at[me], s_to, m)

        return go

    def out_targets():
        a = (me * own_cols) // shard_rows
        b = (me * own_cols + own_cols - 1) // shard_rows
        return ((a, a < s_size), (b, jnp.logical_and(b != a, b < s_size)))

    def home_of_out(d, j):
        for i, (s_to, valid) in enumerate(out_targets()):

            @pl.when(valid)
            def _(i=i, s_to=s_to):
                for m in range(r_size):
                    to_home(lo_.at[d, j], home_out.at[me, d, j], oh_send.at[i, m], oh_recv.at[me], s_to, m)

    sum_proj = LineSum(jp, lp, p_rs, p_rr, p_as, p_ar, home_of_proj)
    sum_fc = LineSum(jf, lf, f_rs, f_rr, f_as, f_ar, home_of_columns(lf, home_fc, fh_send, fh_recv))
    sum_qkv = LineSum(jq, lq, q_rs, q_rr, q_as, q_ar, home_of_columns(lq, home_qkv, qh_send, qh_recv))
    sum_out = LineSum(jo, lo_, o_rs, o_rr, o_as, o_ar, home_of_out)

    for copy in loads + acc_loads:
        copy.wait()

    scatter_two.start_inner()
    vec[...] = jnp.zeros_like(vec)
    gain_one, gain_two, proj_bias = (small_ref[i : i + 1, :] for i in (0, 3, 5))
    cot = cot_v[...].astype(F32)
    middle = middle_ref[...]
    normed, inverse = norm_parts(middle)
    grad_in, grad_gain, grad_bias = norm_backward_rows(scatter_two.finish(), normed, inverse, gain_two)
    grad_middle = cot + grad_in
    branch = grad_middle.astype(BF16)
    gb_own[...] = branch
    ig_keep = grad_middle
    gather = Gather(block(gb), g_send, g_recv, r_size, own=lambda o, part: gb_own.at[pl.ds(part * half, half)])
    gather.start(0)
    save_gb = pltpu.make_async_copy(gb_own, gb.at[pl.ds(0, rows)], tmp_sem.at[1])
    save_gb.start()
    vec[2:3, :] = jnp.sum(branch.astype(F32), axis=0, keepdims=True)
    vec[3:4, :] = grad_gain
    vec[4:5, :] = grad_bias
    vec[5:6, :] = jnp.sum(cot, axis=0, keepdims=True)
    gather.start_rest()
    scatter_proj.start_inner()
    out_v[...] = (middle + (scatter_proj.finish() + proj_bias)).astype(BF16)

    def moved(src, dst, sem):
        far = remote(src, dst, sem.at[0], sem.at[1], z=s, s=z)
        near = pltpu.make_async_copy(src, dst, sem.at[1])

        @pl.when(s != z)
        def _():
            far.start()

        @pl.when(s == z)
        def _():
            near.start()

        def done():
            @pl.when(s != z)
            def _():
                far.wait()

            @pl.when(s == z)
            def _():
                near.wait()

        return done

    out_done = moved(out_v, out_home, mv_sem.at[0])
    gather.need_all()
    save_gb.wait()

    step = chunk.shape[0]
    go_acc[...] = jnp.zeros_like(go_acc)

    def branch_rows(i, carry):
        at = pl.ds(pl.multiple_of(i * step, step), step)
        copy = pltpu.make_async_copy(gb.at[at], chunk, tmp_sem.at[2])
        copy.start()
        copy.wait()
        do_ref[at, :] = lax.dot_general(
            chunk[...], own_o[...], (((1,), (1,)), ((), ())), preferred_element_type=F32
        ).astype(BF16)
        go_acc[...] += lax.dot_general(
            att_ref[at, :], chunk[...], (((0,), (0,)), ((), ())), preferred_element_type=F32
        )
        return carry

    lax.fori_loop(0, tokens // step, branch_rows, 0)
    out_rows = jo.shape[2]
    for i in range(2 * jo.shape[1]):
        jo[i // jo.shape[1], i % jo.shape[1]] = go_acc[i * out_rows : (i + 1) * out_rows, :].astype(BF16)

    code_row = jnp.concatenate([code_ref[i : i + 1, :] for i in range(devices)], axis=1)
    q_rows = min(rows if tokens > 2048 else 256, tokens)
    dk_acc[...] = jnp.zeros_like(dk_acc)
    dv_acc[...] = jnp.zeros_like(dv_acc)
    contract_last = (((1,), (1,)), ((), ()))
    contract_first = (((0,), (0,)), ((), ()))

    def attend(i, carry):
        at = pl.ds(pl.multiple_of(i * q_rows, q_rows), q_rows)
        per = q_rows // rows
        code_q = jnp.concatenate(
            [
                jnp.transpose(jnp.broadcast_to(code_ref[pl.ds(i * per + j, 1), :], (8, rows)))[:, 0:1]
                for j in range(per)
            ],
            axis=0,
        )
        low_q = (code_q // SEG_STEP) * SEG_STEP
        allowed = jnp.logical_and(code_row >= low_q, code_row <= code_q)
        dqs, dks, dvs = [], [], []
        for h in range(heads):
            cols = slice(h * HEAD_DIM, (h + 1) * HEAD_DIM)
            q, do, k = q_ref[at, cols], do_ref[at, cols], k_ref[:, cols]
            scores = lax.dot_general(q, k, contract_last, preferred_element_type=F32)
            scores = jnp.where(allowed, scores, NEGATIVE)
            probs = jnp.exp(scores - lse_ref[at, h : h + 1])
            dp = lax.dot_general(do, v_ref[:, cols], contract_last, preferred_element_type=F32)
            delta = jnp.sum(probs * dp, axis=-1, keepdims=True)
            ds = (probs * (dp - delta)).astype(BF16)
            dqs.append(jnp.dot(ds, k, preferred_element_type=F32))
            dks.append(lax.dot_general(ds, q, contract_first, preferred_element_type=F32))
            dvs.append(lax.dot_general(probs.astype(BF16), do, contract_first, preferred_element_type=F32))
        gp[at, 0:own_cols] = (jnp.concatenate(dqs, axis=1) * (1.0 / math.sqrt(HEAD_DIM))).astype(BF16)
        dk_acc[...] += jnp.concatenate(dks, axis=1)
        dv_acc[...] += jnp.concatenate(dvs, axis=1)
        return carry

    lax.fori_loop(0, tokens // q_rows, attend, 0)
    gp[:, own_cols : 2 * own_cols] = dk_acc[...].astype(BF16)
    gp[:, 2 * own_cols :] = dv_acc[...].astype(BF16)

    n = r_size * rows
    leaf1 = accp
    scatter_one = Scatter(
        packed_block(leaf1), packed_block(acc2), block(land), lambda o, part: block(land)(o, part)[...],
        s1_send, s1_recv, r_size,
    )
    scatter_two.close()
    scatter_proj.close()
    for dst, odd in ((leaf1, 1), (acc2, 0)):

        def partial(i, carry, dst=dst, odd=odd):
            dst[pl.ds(pl.multiple_of(i * n, n), n), :] = lax.dot_general(
                gp[pl.ds(pl.multiple_of((2 * i + odd) * n, n), n), :], own_q[...], contract_last,
                preferred_element_type=F32,
            ).astype(BF16)
            return carry

        lax.fori_loop(0, s_size // 2, partial, 0)
        if odd:
            scatter_one.start_leaves()
    scatter_one.start_inner()

    gq_acc[...] = jnp.zeros_like(gq_acc)

    def hidden_rows(i, carry):
        at = pl.ds(pl.multiple_of(i * step, step), step)
        copy = pltpu.make_async_copy(h1.at[at], chunk, tmp_sem.at[2])
        copy.start()
        copy.wait()
        gq_acc[...] += lax.dot_general(chunk[...], gp[at, :], contract_first, preferred_element_type=F32)
        return carry

    lax.fori_loop(0, tokens // step, hidden_rows, 0)
    per, q_job = jq.shape[1:3]
    for i in range(2 * per):
        jq[i // per, i % per] = gq_acc[i * q_job : (i + 1) * q_job, :].astype(BF16)

    resid = x_ref[...].astype(F32)
    normed, inverse = norm_parts(resid)
    grad_in, grad_gain, grad_bias = norm_backward_rows(scatter_one.finish(), normed, inverse, gain_one)
    ig_v[...] = (ig_keep + grad_in).astype(BF16)
    ig_done = moved(ig_v, ig_home, mv_sem.at[1])
    vec[0:1, :] = grad_gain
    vec[1:2, :] = grad_bias
    ff_lanes = -(-own_ff // 128) * 128
    q_lanes = -(-own_cols // 128) * 128
    vec[7:8, 0:own_ff] = fcb_ref[...]
    vec[7:8, ff_lanes : ff_lanes + own_cols] = jnp.sum(gp[:, :own_cols].astype(F32), axis=0, keepdims=True)
    vec[7:8, ff_lanes + q_lanes : ff_lanes + q_lanes + own_cols] = jnp.sum(
        gp[:, 2 * own_cols :].astype(F32), axis=0, keepdims=True
    )
    vec[pl.ds(8 + me, 1), :] = vec[7:8, :]

    sum_proj.add_ticks(0, sum_proj.n + 3)
    sum_fc.add_ticks(0, sum_fc.n + 3)
    sum_proj.back_ticks(0, sum_proj.n + 2)
    sum_fc.back_ticks(0, sum_fc.n + 2)
    sum_out.add_ticks(0, sum_out.n + 3)
    sum_qkv.add_ticks(0, sum_qkv.n + 3)

    hops = [("s", 1), ("s", 2)] + [("r", bit) for bit in bits_of(r_size)] + [("z", bit) for bit in bits_of(z_size)]
    for i, (axis, bit) in enumerate(hops):
        copy = remote(vec, vec_land.at[i], vec_send.at[i], vec_recv.at[i], **partner(axis, bit))
        copy.start()
        copy.wait()
        vec[...] = vec[...] + vec_land[i]
    small_out[...] = vec[...]

    sum_out.back_ticks(0, sum_out.n + 2)
    sum_qkv.back_ticks(0, sum_qkv.n + 2)

    scatter_one.close()
    gather.close()
    out_done()
    ig_done()
    for total in (sum_proj, sum_fc, sum_qkv, sum_out):
        total.close()
    for i in range(r_size):
        pltpu.make_async_copy(home_proj.at[i], home_proj.at[i], ph_recv.at[i]).wait()
    for m in range(1, r_size):
        pltpu.make_async_copy(home_proj.at[0], home_proj.at[0], ph_send.at[m]).wait()
    for home, send, recv in ((home_fc, fh_send, fh_recv), (home_qkv, qh_send, qh_recv)):
        for i in range(devices):
            pltpu.make_async_copy(home.at[i], home.at[i], recv.at[i]).wait()
        for s_to in range(s_size):
            for m in range(r_size):
                sent = pltpu.make_async_copy(home.at[0], home.at[0], send.at[s_to, m])
                if m:
                    sent.wait()
                else:

                    @pl.when(s != s_to)
                    def _(sent=sent):
                        sent.wait()

    for i in range(devices):
        a, b = (i * own_cols) // shard_rows, (i * own_cols + own_cols - 1) // shard_rows

        @pl.when(jnp.logical_or(s == a, s == b))
        def _(i=i):
            pltpu.make_async_copy(home_out.at[i], home_out.at[i], oh_recv.at[i]).wait()

    for i, (s_to, valid) in enumerate(out_targets()):
        for m in range(r_size):
            far = valid if m else jnp.logical_and(valid, s_to != s)

            @pl.when(far)
            def _(i=i, m=m):
                pltpu.make_async_copy(home_out.at[0], home_out.at[0], oh_send.at[i, m]).wait()


def backward_part(
    part2, partp, grad_proj, grad_fc, h1, wq, wo, q, k, v, att, lse, code, middle, x_own, cot, small, fcb
):
    s_size, r_size, z_size = (lax.axis_size(a) for a in ("s", "r", "z"))
    devices = s_size * r_size
    rows, width = x_own.shape
    tokens = rows * devices
    own_cols = q.shape[1]
    heads = own_cols // HEAD_DIM
    own_ff = grad_proj.shape[0]
    shard_rows = width // s_size
    p_rows = job_rows(own_ff // 2)
    p_n = own_ff // 2 // p_rows
    c_rows = job_rows(shard_rows)
    c_per = shard_rows // c_rows
    c_n = c_per * s_size // 2
    o_rows = job_rows(own_cols // 2)
    o_n = own_cols // 2 // o_rows
    hops = 2 + len(bits_of(r_size)) + len(bits_of(z_size))
    vec_rows = 8 + devices
    anywhere = pl.BlockSpec(memory_space=pl.ANY)
    vmem = pl.BlockSpec(memory_space=pltpu.VMEM)
    shape = jax.ShapeDtypeStruct
    dma = pltpu.SemaphoreType.DMA
    tree = [dma((2, devices))] * 2
    jobs = [(2, p_n, p_rows, width), (2, c_n, c_rows, own_ff), (2, c_n, c_rows, 3 * own_cols), (2, o_n, o_rows, width)]
    line = [dma(j[:2]) for j in jobs for _ in range(4)]
    return pl.pallas_call(
        backward_kernel,
        in_specs=[anywhere] * 7 + [vmem] * 8 + [anywhere, vmem, vmem],
        out_specs=[anywhere] * 6 + [vmem] + [anywhere] * 2,
        out_shape=[
            shape((rows, width), BF16),
            shape((rows, width), BF16),
            shape((r_size,) + jobs[0], BF16),
            shape((devices, c_per, c_rows, own_ff), BF16),
            shape((devices, c_per, c_rows, 3 * own_cols), BF16),
            shape((devices,) + jobs[3], BF16),
            shape((vec_rows, width), F32),
            shape((tokens, width), BF16),
            shape((tokens, width), BF16),
        ],
        scratch_shapes=[
            pltpu.VMEM((tokens // 2, width), BF16),
            pltpu.VMEM((tokens // 2, width), BF16),
            pltpu.VMEM((tokens, width), BF16),
            pltpu.VMEM((rows // 2, width), BF16),
        ]
        + [pltpu.VMEM(j, BF16) for j in jobs]
        + [pltpu.VMEM(j, BF16) for j in jobs]
        + [
            pltpu.VMEM((width, 3 * own_cols), BF16),
            pltpu.VMEM((own_cols, width), BF16),
            pltpu.VMEM((rows, width), BF16),
            pltpu.VMEM((256 if tokens > 2048 else min(512, tokens), width), BF16),
            pltpu.VMEM((width, 3 * own_cols), F32),
            pltpu.VMEM((tokens, own_cols), BF16),
            pltpu.VMEM((tokens, 3 * own_cols), BF16),
            pltpu.VMEM((tokens, own_cols), F32),
            pltpu.VMEM((tokens, own_cols), F32),
            pltpu.VMEM((own_cols, width), F32),
            pltpu.VMEM((vec_rows, width), F32),
            pltpu.VMEM((hops, vec_rows, width), F32),
            pltpu.VMEM((rows, width), BF16),
            pltpu.VMEM((rows, width), BF16),
            pltpu.VMEM((rows, width), BF16),
            dma((10,)),
        ]
        + tree * 4
        + [dma((3,)), dma((1,)), dma((2, 2)), dma((hops,)), dma((hops,))]
        + line
        + [
            dma((r_size,)), dma((r_size,)),
            dma((s_size, r_size)), dma((devices,)),
            dma((s_size, r_size)), dma((devices,)),
            dma((2, r_size)), dma((devices,)),
        ],
        compiler_params=pltpu.CompilerParams(
            collective_id=1, has_side_effects=True, vmem_limit_bytes=62 << 20
        ),
        cost_estimate=pl.CostEstimate(
            flops=10 * heads * tokens * tokens * HEAD_DIM, bytes_accessed=40 << 20, transcendentals=0
        ),
        name="backward_part",
    )(
        part2, partp, grad_proj.reshape(jobs[0]), grad_fc.reshape(jobs[1]), h1, wq, wo, q, k, v, att, lse, code, middle,
        x_own, cot, small, fcb,
    )


def columns_out_kernel(parts, blocks_ref, out_ref):
    devices = blocks_ref.shape[0]
    each = blocks_ref.shape[3] // len(parts)
    for i, (first, width) in enumerate(parts):
        for device in range(devices):
            n = max(0, min(each, width - device * each))
            if n:
                lo = first + device * each
                out_ref[:, lo : lo + n] = blocks_ref[device, 0, :, i * each : i * each + n].astype(F32)


def columns_out(blocks, parts):
    devices, chunks, rows, columns = blocks.shape
    total = parts[-1][0] + parts[-1][1]
    step = 16 if rows % 16 == 0 else rows
    per = rows // step
    return pl.pallas_call(
        lambda *refs: columns_out_kernel(parts, *refs),
        grid=(chunks, per),
        in_specs=[pl.BlockSpec((devices, 1, step, columns), lambda i, j: (0, i, j, 0))],
        out_specs=pl.BlockSpec((step, total), lambda i, j: (i * per + j, 0)),
        out_shape=jax.ShapeDtypeStruct((chunks * rows, total), F32),
        compiler_params=pltpu.CompilerParams(vmem_limit_bytes=32 << 20),
        name="columns_out",
    )(blocks)


def rows_out_kernel(rows_ref, out_ref):
    out_ref[...] = rows_ref[...].astype(F32)


def rows_out(x):
    rows, width = x.shape
    step = job_rows(rows, 160)
    return pl.pallas_call(
        rows_out_kernel,
        grid=(rows // step,),
        in_specs=[pl.BlockSpec((step, width), lambda i: (i, 0))],
        out_specs=pl.BlockSpec((step, width), lambda i: (i, 0)),
        out_shape=jax.ShapeDtypeStruct((rows, width), F32),
        compiler_params=pltpu.CompilerParams(vmem_limit_bytes=32 << 20),
        name="rows_out",
    )(x)


def place(values_in, total, offset):
    return lax.dynamic_update_slice_in_dim(jnp.zeros((total,), F32), values_in.astype(F32), offset, axis=0)


def local(
    inputs,
    positions,
    segments,
    cotangent,
    ln1_gain,
    ln1_bias,
    w_qkv,
    qv_bias,
    w_out,
    out_bias,
    ln2_gain,
    ln2_bias,
    w_fc,
    fc_bias,
    w_proj,
    proj_bias,
):
    s = lax.axis_index("s")
    r = lax.axis_index("r")
    s_size = lax.axis_size("s")
    r_size = lax.axis_size("r")
    devices = s_size * r_size
    me = s * r_size + r
    rows, width = inputs.shape
    heads = width // HEAD_DIM
    own_heads = -(-heads // devices)
    own_cols = own_heads * HEAD_DIM
    head_total = own_cols * devices
    ff = w_fc.shape[1]
    own_ff = ff // devices
    shard_rows = width // s_size

    def head_pad(a):
        return jnp.pad(a, (0, head_total - width)).reshape(devices, own_cols)

    code = jnp.broadcast_to(segments * SEG_STEP + positions // BLOCK, (8, rows))
    small = jnp.stack(
        [place(a, width, s * shard_rows) for a in (ln1_gain, ln1_bias, out_bias, ln2_gain, ln2_bias, proj_bias)]
        + [jnp.zeros((width,), F32)] * 2
    )
    qv = place(qv_bias, 2 * width, s * 2 * shard_rows)
    smallh = jnp.concatenate([head_pad(qv[:width]), head_pad(qv[width:])])

    (
        hidden_one, hidden_two, cot, own_fc, own_qkv, own_out, queries, keys, values, attended, lse, code_all,
        middle, x_own, small, smallh,
    ) = forward_part(inputs, cotangent, code, small, smallh, w_qkv, w_fc, w_out)
    own_fcb = lax.dynamic_slice_in_dim(fc_bias, r * own_ff, own_ff).astype(F32)
    own_proj = lax.dynamic_slice_in_dim(w_proj, r * own_ff, own_ff, axis=0)
    pre_act = dot(hidden_two, own_fc) + own_fcb
    activated, slope = gelu_parts(pre_act)
    activated = activated.astype(BF16)
    grad_act = dot(cot, own_proj, ON_LAST)
    grad_pre = (grad_act * slope).astype(BF16)
    grad_w_proj = dot(activated, cot, ACROSS_TOKENS).astype(BF16)
    partial_two = dot(grad_pre, own_fc, ON_LAST).astype(BF16)
    grad_w_fc = dot(hidden_two, grad_pre, ACROSS_TOKENS).astype(BF16)
    partial_proj = dot(activated, own_proj).astype(BF16)
    grad_fcb = jnp.sum(grad_pre.astype(F32), axis=0)
    out_home, ig_home, home_proj, home_fc, home_qkv, home_out, sums, _, _ = backward_part(
        partial_two, partial_proj, grad_w_proj, grad_w_fc, hidden_one, own_qkv, own_out, queries, keys, values,
        attended, lse, code_all, middle, x_own, cot, small, grad_fcb.reshape(1, own_ff),
    )

    def own_slice(vector):
        size = vector.shape[0] // s_size
        return lax.dynamic_slice_in_dim(vector, s * size, size)

    ff_lanes = -(-own_ff // 128) * 128
    q_lanes = -(-own_cols // 128) * 128
    by_device = sums[8:]
    g_fcb = by_device[:, :own_ff].reshape(ff)
    g_qb = by_device[:, ff_lanes : ff_lanes + own_cols].reshape(-1)[:width]
    g_vb = by_device[:, ff_lanes + q_lanes : ff_lanes + q_lanes + own_cols].reshape(-1)[:width]
    g_fc = columns_out(home_fc, [(0, ff)])
    g_qkv = columns_out(home_qkv, [(i * width, width) for i in range(3)])
    g_out = lax.dynamic_slice_in_dim(home_out.reshape(head_total, width), s * shard_rows, shard_rows)
    g_proj = rows_out(home_proj.reshape(ff // s_size, width))
    return (
        out_home,
        ig_home.astype(F32),
        own_slice(sums[0]),
        own_slice(sums[1]),
        g_qkv,
        own_slice(jnp.concatenate([g_qb, g_vb])),
        g_out.astype(F32),
        own_slice(sums[2]),
        own_slice(sums[3]),
        own_slice(sums[4]),
        g_fc,
        own_slice(g_fcb),
        g_proj,
        own_slice(sums[5]),
    )


def solution(mesh):
    ctx, shard = mesh.devices.shape
    fine = Mesh(mesh.devices.reshape(shard, ctx // shard, shard), ("z", "r", "s"))
    tokens = ("s", "z", "r")
    arg_specs = (
        P(tokens, None),
        P(tokens),
        P(tokens),
        P(tokens, None),
        P("s"),
        P("s"),
        P("s", None),
        P("s"),
        P("s", None),
        P("s"),
        P("s"),
        P("s"),
        P("s", None),
        P("s"),
        P("s", None),
        P("s"),
    )
    out_specs = (P(tokens, None), P(tokens, None)) + arg_specs[4:]
    return jax.shard_map(local, mesh=fine, in_specs=arg_specs, out_specs=out_specs, check_vma=False)
```

```python
import math

import jax
import jax.numpy as jnp
from jax import lax
from jax.experimental import pallas as pl
from jax.experimental.pallas import tpu as pltpu
from jax.sharding import Mesh, PartitionSpec as P

HEAD_DIM = 64
BLOCK = 256
EPSILON = 1e-05
NEGATIVE = -1e30
SEG_STEP = 65536
BF16 = jnp.bfloat16
F32 = jnp.float32


def bits_of(size):
    return [1 << i for i in range(size.bit_length() - 1)]


def norm_parts(values):
    centre = jnp.mean(values, axis=-1, keepdims=True)
    centred = values - centre
    spread = jnp.mean(centred * centred, axis=-1, keepdims=True)
    inverse = lax.rsqrt(spread + EPSILON)
    return centred * inverse, inverse


def gelu_parts(u):
    c = math.sqrt(2.0 / math.pi)
    squared = u * u
    t = jnp.tanh(c * (u + 0.044715 * (u * squared)))
    half = 0.5 * (1.0 + t)
    slope = half + 0.5 * u * (1.0 - t * t) * (c * (1.0 + 3.0 * 0.044715 * squared))
    return u * half, slope


def dot(a, b, contract=((1,), (0,))):
    return lax.dot_general(a, b, (contract, ((), ())), preferred_element_type=F32)


ACROSS_TOKENS = ((0,), (0,))
ON_LAST = ((1,), (1,))


MESH_ID = pl.DeviceIdType.MESH


def remote(src, dst, send_sem, recv_sem, **device):
    return pltpu.make_async_remote_copy(
        src_ref=src,
        dst_ref=dst,
        send_sem=send_sem,
        recv_sem=recv_sem,
        device_id=device,
        device_id_type=MESH_ID,
    )


def partner(axis, bit):
    return {axis: lax.axis_index(axis) ^ bit}


def plane_device(offset, r_size):
    found = {}
    if offset // r_size:
        found["s"] = lax.axis_index("s") ^ (offset // r_size)
    if offset % r_size:
        found["r"] = lax.axis_index("r") ^ (offset % r_size)
    return found


def tree_of(order, r_size):
    levels = []
    known = [(0, 0)]
    for axis, bit in order:
        step = bit * r_size if axis == "s" else bit
        known = known + [(o ^ step, depth + 1) for o, depth in known]
    found = {}
    for o, depth in known:
        if o == 0:
            continue
        for axis, bit in order[::-1]:
            step = bit * r_size if axis == "s" else bit
            if o & step:
                found.setdefault(depth, []).append((o, o ^ step, axis, bit))
                break
    for depth in sorted(found):
        levels.append(found[depth])
    return levels


def chip_orders(r_size):
    chips = [("s", 2)] + [("r", bit) for bit in bits_of(r_size)]
    return [chips + [("s", 1)], chips[::-1] + [("s", 1)]]


class Gather:
    def __init__(self, block, send_sem, recv_sem, r_size, parts=2, own=None):
        self.block = block
        self.own = own or block
        self.send_sem = send_sem
        self.recv_sem = recv_sem
        self.levels = [tree_of(order, r_size) for order in chip_orders(r_size)[:parts]]
        self.parts = parts
        self.arrived = set()

    def copy(self, part, transfer):
        offset, source, axis, bit = transfer
        src = self.own(0, part) if source == 0 else self.block(source, part)
        return remote(
            src,
            self.block(offset, part),
            self.send_sem.at[part, offset],
            self.recv_sem.at[part, offset],
            **partner(axis, bit),
        )

    def transfers(self):
        for level in range(len(self.levels[0])):
            for i in range(len(self.levels[0][level])):
                for part in range(self.parts):
                    yield level, part, self.levels[part][level][i]

    def find(self, part, offset):
        for _, p, t in self.transfers():
            if p == part and t[0] == offset:
                return t

    def need(self, part, offset):
        if offset and (part, offset) not in self.arrived:
            self.arrived.add((part, offset))
            self.copy(part, self.find(part, offset)).wait_recv()

    def start(self, level):
        for lv, part, t in self.transfers():
            if lv == level:
                self.need(part, t[1])
                self.copy(part, t).start()

    def start_rest(self):
        for level in range(1, len(self.levels[0])):
            self.start(level)

    def need_all(self):
        for _, part, t in self.transfers():
            self.need(part, t[0])

    def close(self):
        self.need_all()
        for _, part, t in self.transfers():
            self.copy(part, t).wait_send()


def attention_rows(rows, first, q_ref, k_ref, v_ref, code_q, code_k):
    heads = q_ref.shape[1] // HEAD_DIM
    low_q = (code_q // SEG_STEP) * SEG_STEP
    allowed = jnp.logical_and(code_k >= low_q, code_k <= code_q)
    outs = []
    sums = []
    for h in range(heads):
        cols = slice(h * HEAD_DIM, (h + 1) * HEAD_DIM)
        scores = lax.dot_general(
            q_ref[pl.ds(first, rows), cols],
            k_ref[:, cols],
            (((1,), (1,)), ((), ())),
            preferred_element_type=F32,
        )
        scores = jnp.where(allowed, scores, NEGATIVE)
        top = jnp.max(scores, axis=-1, keepdims=True)
        unnorm = jnp.exp(scores - top)
        total = jnp.sum(unnorm, axis=-1, keepdims=True)
        mixed = jnp.dot(unnorm.astype(BF16), v_ref[:, cols], preferred_element_type=F32)
        outs.append((mixed / total).astype(BF16))
        sums.append(top + jnp.log(total))
    return jnp.concatenate(outs, axis=1), jnp.concatenate(sums, axis=1)


def split_rows(n):
    first = -(-n // 32) * 16
    return ((0, first), (first, n - first))


class WeightPush:
    def __init__(self, source, dest, rows, send_sem, recv_sem, across):
        self.source, self.dest, self.rows = source, dest, rows
        self.send_sem, self.recv_sem = send_sem, recv_sem
        self.across = across

    def core_copy(self):
        s = lax.axis_index("s")
        return remote(
            self.source(s ^ 1),
            self.dest(s, 0, self.rows),
            self.send_sem.at[0],
            self.recv_sem.at[0],
            s=s ^ 1,
        )

    def chip_copy(self, m, part, landed=None):
        s = lax.axis_index("s")
        first, count = split_rows(self.rows)[part]
        return remote(
            self.source(s ^ m).at[pl.ds(first, count)],
            self.dest(s, first, count),
            self.send_sem.at[m],
            self.recv_sem.at[m],
            s=s ^ m,
        )

    def relay_copy(self, m, part):
        s = lax.axis_index("s")
        first, count = split_rows(self.rows)[part]
        ref = self.dest(s ^ m, first, count)
        return remote(
            ref, ref, self.send_sem.at[2 + m], self.recv_sem.at[2 + m], z=lax.axis_index("z") ^ 1
        )

    def per_part(self, act):
        odd = lax.axis_index("z") % 2
        for part in range(2):

            @pl.when(odd == part)
            def _(part=part):
                act(part)

    def start(self):
        if 1 in self.across:
            self.core_copy().start()

        def act(part):
            for m in self.across:
                if m != 1:
                    self.chip_copy(m, part).start()

        self.per_part(act)

    def relay(self):
        def act(part):
            for m in self.across:
                if m != 1:
                    self.chip_copy(m, part).wait_recv()
                    self.relay_copy(m, part).start()

        self.per_part(act)

    def need(self):
        if 1 in self.across:
            self.core_copy().wait_recv()

        def act(part):
            for m in self.across:
                if m != 1:
                    self.relay_copy(m, 1 - part).wait_recv()

        self.per_part(act)

    def close(self):
        if 1 in self.across:
            self.core_copy().wait_send()

        def act(part):
            for m in self.across:
                if m != 1:
                    self.chip_copy(m, part).wait_send()
                    self.relay_copy(m, part).wait_send()

        self.per_part(act)


def forward_kernel(
    x_in, cot_in, code_in, small_in, smallh_in, wq_in, wf_in, wo_in,
    h1_out, h2_out, cot_out, wf_out, wq_out, wo_out, q_ref, k_ref, v_ref, att_ref, lse_ref, code_out,
    middle_out, x_own, small_ref, smallh_ref,
    code_land, small_land, smallh_land, h1, wq_vm, stage_q, wf_vm, stage_f, own_q, full_out, att_land, h2_own,
    x_sem, code_sem, cot_sem, small_sem, load_sem, h1_send, h1_recv, cd_send, cd_recv, ct_send, ct_recv, h2_send,
    h2_recv, wq_send, wq_recv, wf_send, wf_recv, wo_send, wo_recv, at_send, at_recv, out_sem,
):
    s, r, z = (lax.axis_index(a) for a in ("s", "r", "z"))
    s_size, r_size = lax.axis_size("s"), lax.axis_size("r")
    devices = s_size * r_size
    me = s * r_size + r
    rows, width = x_in.shape
    tokens = rows * devices
    own_cols = q_ref.shape[1]
    own_ff = wf_out.shape[1]
    shard_rows = wq_in.shape[0]

    def shard_at(i, first=0, count=shard_rows):
        return pl.ds(pl.multiple_of(i * shard_rows + first, 16), count)

    barrier = pltpu.get_barrier_semaphore()
    for offset in range(1, devices):
        pl.semaphore_signal(barrier, inc=1, device_id=plane_device(offset, r_size), device_id_type=MESH_ID)
    pl.semaphore_signal(barrier, inc=1, device_id={"z": z ^ 1}, device_id_type=MESH_ID)

    @pl.when(s != z)
    def _():
        pl.semaphore_signal(barrier, inc=1, device_id={"z": s, "s": z}, device_id_type=MESH_ID)

    pl.semaphore_wait(barrier, devices + jnp.where(s != z, 1, 0))

    def moved(src, dst, sem):
        far = remote(src, dst, sem.at[0], sem.at[1], z=s, s=z)
        near = pltpu.make_async_copy(src, dst, sem.at[1])

        @pl.when(s != z)
        def _():
            far.start()

        @pl.when(s == z)
        def _():
            near.start()

        def arrived():
            @pl.when(s != z)
            def _():
                far.wait_recv()

            @pl.when(s == z)
            def _():
                near.wait()

        def sent():
            @pl.when(s != z)
            def _():
                far.wait_send()

        return arrived, sent

    x_arrived, x_sent = moved(x_in, x_own, x_sem)
    code_arrived, code_sent = moved(code_in, code_land.at[0], code_sem)
    loads = [
        pltpu.make_async_copy(wq_in, wq_vm, load_sem.at[0]),
        pltpu.make_async_copy(wf_in, wf_vm, load_sem.at[1]),
        pltpu.make_async_copy(wo_in, full_out.at[shard_at(s)], load_sem.at[2]),
    ]
    for load in loads:
        load.start()
    small_copies = []
    for m in range(1, s_size):
        small_copies.append(
            remote(small_in, small_land.at[m], small_sem.at[0, m], small_sem.at[1, m], s=s ^ m)
        )
        small_copies.append(
            remote(smallh_in, smallh_land.at[m], small_sem.at[2, m], small_sem.at[3, m], s=s ^ m)
        )
    for copy in small_copies:
        copy.start()
    if full_out.shape[0] > width:
        full_out[width:, :] = jnp.zeros((full_out.shape[0] - width, width), BF16)

    loads[0].wait()
    for s2 in range(s_size):
        for r2 in range(r_size):

            @pl.when(r == r2)
            def _(s2=s2, r2=r2):
                device = s2 * r_size + r2
                for part in range(3):
                    lo = device * own_cols
                    n = max(0, min(own_cols, width - lo))
                    if n:
                        stage_q[s2, :, part * own_cols : part * own_cols + n] = wq_vm[
                            :, part * width + lo : part * width + lo + n
                        ]
                    if n < own_cols:
                        stage_q[s2, :, part * own_cols + n : (part + 1) * own_cols] = jnp.zeros(
                            (shard_rows, own_cols - n), BF16
                        )

    push_q = WeightPush(
        lambda i: stage_q.at[i],
        lambda i, first, count: own_q.at[shard_at(i, first, count)],
        shard_rows, wq_send, wq_recv, (1, 2, 3),
    )
    push_q.start()
    own_q[shard_at(s), :] = stage_q[s]

    for copy in small_copies:
        copy.wait_recv()
    small = small_in[...]
    smallh = smallh_in[...]
    for m in range(1, s_size):
        small = small + small_land[m]
        smallh = smallh + smallh_land[m]
    small_ref[...] = small
    smallh_ref[...] = smallh
    gain_one, bias_one, out_bias, gain_two, bias_two = (small_ref[i : i + 1, :] for i in range(5))
    x_arrived()
    cot_arrived, cot_sent = moved(cot_in, cot_out.at[pl.ds(0, rows)], cot_sem)
    resid = x_own[...].astype(F32)
    normed, _ = norm_parts(resid)
    h1[0:rows, :] = (normed * gain_one + bias_one).astype(BF16)
    half = rows // 2

    def block_of(ref):
        return lambda offset, part: ref.at[pl.ds(offset * rows + part * half, half)]

    gather_one = Gather(block_of(h1), h1_send, h1_recv, r_size)
    gather_one.start(0)
    code_arrived()
    gather_code = Gather(lambda offset, part: code_land.at[offset], cd_send, cd_recv, r_size, parts=1)
    gather_code.start(0)

    loads[1].wait()
    for s2 in range(s_size):
        for r2 in range(r_size):

            @pl.when(r == r2)
            def _(s2=s2, r2=r2):
                lo = (s2 * r_size + r2) * own_ff
                stage_f[s2] = wf_vm[:, lo : lo + own_ff]

    gather_one.start(1)
    gather_code.start(1)
    push_q.relay()
    for level in range(2, len(gather_one.levels[0])):
        gather_one.start(level)
        gather_code.start(level)

    push_o = WeightPush(
        lambda i: full_out.at[shard_at(s)],
        lambda i, first, count: full_out.at[shard_at(i, first, count)],
        shard_rows, wo_send, wo_recv, (1, 2),
    )
    push_f = WeightPush(
        lambda i: stage_f.at[i],
        lambda i, first, count: wf_out.at[shard_at(i, first, count)],
        shard_rows, wf_send, wf_recv, (1, 2, 3),
    )
    own_f = pltpu.make_async_copy(
        stage_f.at[s], wf_out.at[shard_at(s)], load_sem.at[1]
    )
    own_f.start()
    gather_one.need_all()
    loads[2].wait()
    push_o.start()
    push_f.start()

    push_q.need()
    save_q = pltpu.make_async_copy(own_q, wq_out, out_sem.at[0])
    save_q.start()
    save_h = pltpu.make_async_copy(h1, h1_out, out_sem.at[1])
    save_h.start()
    q_bias = smallh_ref[pl.ds(me, 1), :]
    v_bias = smallh_ref[pl.ds(devices + me, 1), :]
    step = min(512, tokens)
    score_scale = jnp.asarray(1.0 / math.sqrt(HEAD_DIM), BF16)

    def project(i, carry):
        at = pl.ds(pl.multiple_of(i * step, step), step)
        packed = jnp.dot(h1[at, :], own_q[...], preferred_element_type=F32)
        q_ref[at, :] = (packed[:, :own_cols] + q_bias).astype(BF16) * score_scale
        k_ref[at, :] = packed[:, own_cols : 2 * own_cols].astype(BF16)
        v_ref[at, :] = (packed[:, 2 * own_cols :] + v_bias).astype(BF16)
        return carry

    lax.fori_loop(0, tokens // step, project, 0)
    cot_arrived()
    gather_cot = Gather(block_of(cot_out), ct_send, ct_recv, r_size)
    gather_cot.start(0)
    gather_code.need_all()
    code_out[...] = code_land[:, 0, :]
    code_row = jnp.concatenate([code_land[i, 0:1, :] for i in range(devices)], axis=1)

    q_rows = min(rows if tokens > 2048 else 256, tokens)

    def attend(i, carry):
        first = pl.multiple_of(i * q_rows, q_rows)
        per = q_rows // rows
        code_col = jnp.concatenate(
            [jnp.transpose(code_land[i * per + j])[:, 0:1] for j in range(per)], axis=0
        )
        out, sums = attention_rows(q_rows, first, q_ref, k_ref, v_ref, code_col, code_row)
        att_ref[pl.ds(first, q_rows), :] = out
        lse_ref[pl.ds(first, q_rows), :] = sums
        return carry

    lax.fori_loop(0, tokens // q_rows, attend, 0)

    at_copies = []
    for offset in range(1, devices):
        at_copies.append(
            remote(
                att_ref.at[pl.ds(offset * rows, rows)],
                att_land.at[me],
                at_send.at[offset],
                at_recv.at[offset],
                **plane_device(offset, r_size),
            )
        )
    for copy in at_copies:
        copy.start()
    att_land[me] = att_ref[0:rows, :]
    push_o.relay()
    push_o.need()
    far = full_out.at[shard_at(s ^ 2)]
    out_core = remote(far, far, wo_send.at[5], wo_recv.at[5], s=s ^ 1)
    out_core.start()
    gather_cot.start(1)
    for copy in at_copies:
        copy.wait_recv()
    out_core.wait_recv()
    middle = resid + out_bias
    for device in range(devices):
        middle = middle + jnp.dot(
            att_land[device],
            full_out[device * own_cols : (device + 1) * own_cols, :],
            preferred_element_type=F32,
        )
    middle_out[...] = middle
    normed, _ = norm_parts(middle)
    h2_own[...] = (normed * gain_two + bias_two).astype(BF16)
    save_h2 = pltpu.make_async_copy(h2_own, h2_out.at[pl.ds(0, rows)], out_sem.at[2])
    save_h2.start()
    gather_two = Gather(
        block_of(h2_out), h2_send, h2_recv, r_size, own=lambda o, part: h2_own.at[pl.ds(part * half, half)]
    )
    gather_two.start(0)
    save_o = pltpu.make_async_copy(
        full_out.at[pl.ds(pl.multiple_of(me * own_cols, own_cols), own_cols)], wo_out, out_sem.at[3]
    )
    save_o.start()
    for level in range(2, len(gather_cot.levels[0])):
        gather_cot.start(level)
    push_f.relay()
    gather_two.start_rest()
    gather_two.close()
    gather_cot.close()
    gather_one.close()
    gather_code.close()
    push_f.need()
    for push in (push_q, push_o, push_f):
        push.close()
    out_core.wait_send()
    for copy in at_copies + small_copies:
        copy.wait_send()
    x_sent()
    code_sent()
    cot_sent()
    own_f.wait()
    for save in (save_q, save_h, save_h2, save_o):
        save.wait()


def forward_part(x, cot, code, small, smallh, w_qkv, w_fc, w_out):
    s_size, r_size = lax.axis_size("s"), lax.axis_size("r")
    devices = s_size * r_size
    rows, width = x.shape
    tokens = rows * devices
    shard_rows = w_qkv.shape[0]
    heads = width // HEAD_DIM
    own_heads = -(-heads // devices)
    own_cols = own_heads * HEAD_DIM
    own_ff = w_fc.shape[1] // devices
    anywhere = pl.BlockSpec(memory_space=pl.ANY)
    vmem = pl.BlockSpec(memory_space=pltpu.VMEM)
    shape = jax.ShapeDtypeStruct
    dma = pltpu.SemaphoreType.DMA
    flops = 2 * tokens * width * 3 * own_cols + 4 * own_heads * tokens * tokens * HEAD_DIM
    return pl.pallas_call(
        forward_kernel,
        in_specs=[anywhere, anywhere, anywhere, vmem, vmem, anywhere, anywhere, anywhere],
        out_specs=[anywhere] * 6 + [vmem] * 10,
        out_shape=[
            shape((tokens, width), BF16),
            shape((tokens, width), BF16),
            shape((tokens, width), BF16),
            shape((width, own_ff), BF16),
            shape((width, 3 * own_cols), BF16),
            shape((own_cols, width), BF16),
            shape((tokens, own_cols), BF16),
            shape((tokens, own_cols), BF16),
            shape((tokens, own_cols), BF16),
            shape((tokens, own_cols), BF16),
            shape((tokens, own_heads), F32),
            shape((devices, rows), jnp.int32),
            shape((rows, width), F32),
            shape((rows, width), BF16),
            shape(small.shape, F32),
            shape(smallh.shape, F32),
        ],
        scratch_shapes=[
            pltpu.VMEM((devices, 8, rows), jnp.int32),
            pltpu.VMEM((s_size,) + small.shape, F32),
            pltpu.VMEM((s_size,) + smallh.shape, F32),
            pltpu.VMEM((tokens, width), BF16),
            pltpu.VMEM(w_qkv.shape, BF16),
            pltpu.VMEM((s_size, shard_rows, 3 * own_cols), BF16),
            pltpu.VMEM(w_fc.shape, BF16),
            pltpu.VMEM((s_size, shard_rows, own_ff), BF16),
            pltpu.VMEM((width, 3 * own_cols), BF16),
            pltpu.VMEM((devices * own_cols, width), BF16),
            pltpu.VMEM((devices, rows, own_cols), BF16),
            pltpu.VMEM((rows, width), BF16),
            dma((2,)), dma((2,)), dma((2,)), dma((4, s_size)), dma((3,)),
            dma((2, devices)), dma((2, devices)), dma((1, devices)), dma((1, devices)),
            dma((2, devices)), dma((2, devices)), dma((2, devices)), dma((2, devices)),
            dma((6,)), dma((6,)), dma((6,)), dma((6,)), dma((6,)), dma((6,)),
            dma((devices,)), dma((devices,)), dma((4,)),
        ],
        compiler_params=pltpu.CompilerParams(
            collective_id=0, has_side_effects=True, vmem_limit_bytes=60 << 20
        ),
        cost_estimate=pl.CostEstimate(flops=flops, bytes_accessed=40 << 20, transcendentals=0),
        name="forward_part",
    )(x, cot, code, small, smallh, w_qkv, w_fc, w_out)


class Scatter:
    def __init__(self, leaf, acc, land, load, send_sem, recv_sem, r_size):
        self.leaf, self.acc, self.land, self.load = leaf, acc, land, load
        self.send_sem, self.recv_sem = send_sem, recv_sem
        self.levels = [tree_of(order, r_size) for order in chip_orders(r_size)]

    def copy(self, part, transfer):
        offset, _, axis, bit = transfer
        src = self.acc(offset, part) if self.children(part, offset) else self.leaf(offset, part)
        return remote(
            src,
            self.land(offset, part),
            self.send_sem.at[part, offset],
            self.recv_sem.at[part, offset],
            **partner(axis, bit),
        )

    def children(self, part, offset):
        return [t for level in self.levels[part] for t in level if t[1] == offset]

    def start_leaves(self):
        for level in range(len(self.levels[0]) - 1, -1, -1):
            for i in range(len(self.levels[0][level])):
                for part in range(2):
                    t = self.levels[part][level][i]
                    if not self.children(part, t[0]):
                        self.copy(part, t).start()

    def total(self, part, offset):
        value = self.acc(offset, part)[...].astype(F32)
        for t in self.children(part, offset)[::-1]:
            self.copy(part, t).wait_recv()
            value = value + self.load(t[0], part).astype(F32)
        return value

    def start_inner(self):
        for level in range(len(self.levels[0]) - 1, -1, -1):
            for i in range(len(self.levels[0][level])):
                for part in range(2):
                    t = self.levels[part][level][i]
                    if self.children(part, t[0]):
                        self.acc(t[0], part)[...] = self.total(part, t[0]).astype(BF16)
                        self.copy(part, t).start()

    def finish(self):
        return jnp.concatenate([self.total(part, 0) for part in range(2)], axis=0)

    def close(self):
        for part in range(2):
            for level in self.levels[part]:
                for t in level:
                    self.copy(part, t).wait_send()


class LineSum:
    def __init__(self, jobs, land, rs_send, rs_recv, ag_send, ag_recv, home, start):
        self.jobs, self.land = jobs, land
        self.rs_send, self.rs_recv, self.ag_send, self.ag_recv = rs_send, rs_recv, ag_send, ag_recv
        self.home = home
        self.n = jobs.shape[1]
        self.z = lax.axis_index("z")
        self.last = lax.axis_size("z") - 1
        self.start = start
        self.end = start + self.n + 2 * self.last

    def place(self, d):
        return self.z if d == 0 else self.last - self.z

    def up(self, d, j):
        return remote(
            self.jobs.at[d, j], self.land.at[d, j], self.rs_send.at[d, j], self.rs_recv.at[d, j], z=self.z + 1 - 2 * d
        )

    def down(self, d, j):
        return remote(
            self.land.at[d, j], self.land.at[d, j], self.ag_send.at[d, j], self.ag_recv.at[d, j], z=self.z - 1 + 2 * d
        )

    def add(self, d, j):
        place = self.place(d)

        @pl.when(place > 0)
        def _():
            self.up(d, j).wait_recv()
            total = (self.jobs[d, j].astype(F32) + self.land[d, j].astype(F32)).astype(BF16)

            @pl.when(place < self.last)
            def _():
                self.jobs[d, j] = total

            @pl.when(place == self.last)
            def _():
                self.land[d, j] = total

        @pl.when(place < self.last)
        def _():
            self.up(d, j).start()

        @pl.when(place == self.last)
        def _():
            self.down(d, j).start()
            self.home(d, j)

    def back(self, d, j):
        place = self.place(d)
        self.down(d, j).wait_recv()

        @pl.when(place > 0)
        def _():
            self.down(d, j).start()

        self.home(d, j)

    def tick(self, k):
        for d in range(2):
            j = k - self.start - self.place(d)

            @pl.when(jnp.logical_and(j >= 0, j < self.n))
            def _(d=d, j=j):
                self.add(d, j)

        for d in range(2):
            place = self.place(d)
            j = k - self.start - 2 * self.last + place

            @pl.when(jnp.logical_and(place < self.last, jnp.logical_and(j >= 0, j < self.n)))
            def _(d=d, j=j):
                self.back(d, j)

    def close(self):
        def one(j, carry):
            for d in range(2):
                place = self.place(d)

                @pl.when(place < self.last)
                def _(d=d):
                    self.up(d, j).wait_send()

                @pl.when(place > 0)
                def _(d=d):
                    self.down(d, j).wait_send()

            return carry

        lax.fori_loop(0, self.n, one, 0)


class Clock:
    def __init__(self, sums):
        self.sums = sums
        self.now = 0
        self.end = max(one.end for one in sums)

    def ticks(self, first, lo, hi):
        for one in self.sums:
            if one.start < hi and one.end > lo:
                one.tick(first)

    def run(self, count):
        lo, hi = self.now, min(self.now + count, self.end)
        self.now = hi
        if hi - lo == 1:
            self.ticks(lo, lo, hi)
        elif hi > lo:

            def step(k, carry):
                self.ticks(k, lo, hi)
                return carry

            lax.fori_loop(lo, hi, step, 0)

    def loop(self, count, body):
        lo, hi = self.now, min(self.now + count, self.end)
        self.now = hi

        def step(i, carry):
            body(i)
            self.ticks(lo + i, lo, lo + count)
            return carry

        lax.fori_loop(0, count, step, 0)


def product_rows(lhs, rhs, write):
    for lo in range(0, lhs.shape[1], 256):
        hi = min(lhs.shape[1], lo + 256)
        value = lax.dot_general(
            lhs[:, lo:hi], rhs[...], (((0,), (0,)), ((), ())), preferred_element_type=F32
        )
        write(lo, hi, value)


def into_jobs(jobs):
    n, size = jobs.shape[1:3]

    def write(lo, hi, value):
        value = value.astype(BF16)
        for job in range(lo // size, -(-hi // size)):
            a, b = max(lo, job * size), min(hi, (job + 1) * size)
            jobs[job // n, job % n, a - job * size : b - job * size, :] = value[a - lo : b - lo, :]

    return write


def into_sum(acc):
    def write(lo, hi, value):
        acc[lo:hi, :] += value

    return write


def job_rows(n, most=80):
    for rows in range(most, 15, -16):
        if n % rows == 0:
            return rows
    return n


def norm_backward_rows(grad, normed, inverse, gain):
    scaled = grad * gain
    mean_scaled = jnp.mean(scaled, axis=-1, keepdims=True)
    mean_product = jnp.mean(scaled * normed, axis=-1, keepdims=True)
    grad_in = inverse * (scaled - mean_scaled - normed * mean_product)
    return (
        grad_in,
        jnp.sum(grad * normed, axis=0, keepdims=True),
        jnp.sum(grad, axis=0, keepdims=True),
    )


def backward_kernel(
    h2, cot_in, wf, wp, h1, wq, wo, q_ref, k_ref, v_ref, att_ref, lse_ref, code_ref, middle_ref, x_ref,
    small_ref, fcb_ref,
    out_home, ig_home, home_proj, home_fc, home_qkv, home_out, small_out, landp, land_far, gb,
    acc, leaf, land_near, tmp, jp, jf, jq, jo, lp, lf, lq, lo_, own_f, own_p, own_q, own_o, cot_v, chunk, chunk2,
    gp_acc, gf_acc, gq_acc, act, gpre, do_ref, gp, dk_acc, dv_acc, go_acc, vec, vec_land, gb_own, out_v, ig_v,
    load_sem, s2_send, s2_recv, sp_send, sp_recv, s1_send, s1_recv, g_send, g_recv, tmp_sem, mv_sem,
    vec_send, vec_recv,
    p_rs, p_rr, p_as, p_ar, f_rs, f_rr, f_as, f_ar, q_rs, q_rr, q_as, q_ar, o_rs, o_rr, o_as, o_ar,
    ph_send, ph_recv, fh_send, fh_recv, qh_send, qh_recv, oh_send, oh_recv,
):
    s, r, z = (lax.axis_index(a) for a in ("s", "r", "z"))
    s_size, r_size, z_size = (lax.axis_size(a) for a in ("s", "r", "z"))
    devices = s_size * r_size
    me = s * r_size + r
    rows, width = x_ref.shape
    tokens = rows * devices
    half = rows // 2
    own_cols = q_ref.shape[1]
    own_ff = wf.shape[1]
    heads = own_cols // HEAD_DIM
    shard_rows = width // s_size
    step = chunk.shape[0]
    contract_last = (((1,), (1,)), ((), ()))
    contract_first = (((0,), (0,)), ((), ()))

    barrier = pltpu.get_barrier_semaphore()
    for offset in range(1, devices):
        pl.semaphore_signal(barrier, inc=1, device_id=plane_device(offset, r_size), device_id_type=MESH_ID)
    for bit in bits_of(z_size):
        pl.semaphore_signal(barrier, inc=1, device_id={"z": z ^ bit}, device_id_type=MESH_ID)
    inner = jnp.logical_and(z > 0, z < z_size - 1)

    @pl.when(s != z)
    def _():
        pl.semaphore_signal(barrier, inc=1, device_id={"z": s, "s": z}, device_id_type=MESH_ID)

    @pl.when(inner)
    def _():
        pl.semaphore_signal(
            barrier, inc=1, device_id={"z": jnp.where(z % 2 == 1, z + 1, z - 1)}, device_id_type=MESH_ID
        )

    loads = [
        pltpu.make_async_copy(src, dst, load_sem.at[i])
        for i, (src, dst) in enumerate(
            (
                (wf, own_f),
                (wp.at[pl.ds(pl.multiple_of(r * own_ff, 8), own_ff)], own_p),
                (wo, own_o),
                (cot_in.at[pl.ds(0, rows)], cot_v),
            )
        )
    ]
    for load in loads:
        load.start()
    if own_q.shape[0] != width:
        own_q = own_f.at[:, : 3 * own_cols]
    load_q = pltpu.make_async_copy(wq, own_q, load_sem.at[4])

    loads[0].wait()
    loads[1].wait()
    chunks = tokens // step
    if chunks > 1:
        gp_acc[...] = jnp.zeros_like(gp_acc)
        gf_acc[...] = jnp.zeros_like(gf_acc)
        gq_acc[...] = jnp.zeros_like(gq_acc)

    def fetch(src, at, dst, i):
        copy = pltpu.make_async_copy(src.at[at], dst, tmp_sem.at[i])
        copy.start()
        return copy

    piece = min(256, step)

    def feed_forward(i, carry):
        at = pl.ds(pl.multiple_of(i * step, step), step)
        first = fetch(h2, at, chunk, 2)
        second = fetch(cot_in, at, chunk2, 3)
        first.wait()
        second.wait()

        def one(j, inner_carry):
            here = pl.ds(pl.multiple_of(j * piece, piece), piece)
            there = pl.ds(pl.multiple_of(i * step + j * piece, piece), piece)
            pre = jnp.dot(chunk[here, :], own_f[...], preferred_element_type=F32) + fcb_ref[...]
            value, slope = gelu_parts(pre)
            act[there, :] = value.astype(BF16)
            back = lax.dot_general(chunk2[here, :], own_p[...], contract_last, preferred_element_type=F32)
            gpre[there, :] = (back * slope).astype(BF16)
            return inner_carry

        lax.fori_loop(0, step // piece, one, 0)
        product_rows(act.at[at], chunk2, into_jobs(jp) if chunks == 1 else into_sum(gp_acc))
        if chunks > 1:
            product_rows(chunk, gpre.at[at], into_sum(gf_acc))
        return carry

    if chunks == 1:
        feed_forward(0, 0)
    else:
        lax.fori_loop(0, chunks, feed_forward, 0)
        into_jobs(jp)(0, own_ff, gp_acc[...])
        into_jobs(jf)(0, width, gf_acc[...])

    peers = devices - 1 + len(bits_of(z_size))
    pl.semaphore_wait(barrier, peers + jnp.where(s != z, 1, 0) + jnp.where(inner, 1, 0))

    def to_home(src, dst, send, recv, s_to, m):
        far = remote(src, dst, send, recv, s=s_to, r=r ^ m)
        if m:
            far.start()
        else:
            near = pltpu.make_async_copy(src, dst, recv)

            @pl.when(s_to == s)
            def _():
                near.start()

            @pl.when(s_to != s)
            def _():
                far.start()

    def home_of_proj(d, j):
        for m in range(r_size):
            src, dst = lp.at[d, j], home_proj.at[r, d, j]
            if m:
                remote(src, dst, ph_send.at[m], ph_recv.at[r], r=r ^ m).start()
            else:
                pltpu.make_async_copy(src, dst, ph_recv.at[r]).start()

    def home_of_columns(landing, home, send, recv):
        per = landing.shape[1] // (s_size // 2)

        def go(d, j):
            s_to = d * (s_size // 2) + j // per
            for m in range(r_size):
                to_home(landing.at[d, j], home.at[me, j % per], send.at[s_to, m], recv.at[me], s_to, m)

        return go

    def out_targets():
        a = (me * own_cols) // shard_rows
        b = (me * own_cols + own_cols - 1) // shard_rows
        return ((a, a < s_size), (b, jnp.logical_and(b != a, b < s_size)))

    def home_of_out(d, j):
        for i, (s_to, valid) in enumerate(out_targets()):

            @pl.when(valid)
            def _(i=i, s_to=s_to):
                for m in range(r_size):
                    to_home(lo_.at[d, j], home_out.at[me, d, j], oh_send.at[i, m], oh_recv.at[me], s_to, m)

    sum_proj = LineSum(jp, lp, p_rs, p_rr, p_as, p_ar, home_of_proj, 0)
    start = sum_proj.n
    sum_fc = LineSum(jf, lf, f_rs, f_rr, f_as, f_ar, home_of_columns(lf, home_fc, fh_send, fh_recv), start)
    start += sum_fc.n
    sum_out = LineSum(jo, lo_, o_rs, o_rr, o_as, o_ar, home_of_out, start)
    start += sum_out.n
    sum_qkv = LineSum(jq, lq, q_rs, q_rr, q_as, q_ar, home_of_columns(lq, home_qkv, qh_send, qh_recv), start)
    clock = Clock([sum_proj, sum_fc, sum_out, sum_qkv])
    clock.run(1)

    def slot(offset):
        return (offset // r_size) // 2 * r_size + offset % r_size

    def block(ref):
        return lambda o, part: ref.at[pl.ds(o * rows + part * half, half)]

    def packed_block(ref):
        return lambda o, part: ref.at[pl.ds(slot(o) * rows + part * half, half)]

    def far_load(ref):
        def load(o, part):
            copy = pltpu.make_async_copy(block(ref)(o, part), tmp, tmp_sem.at[0])
            copy.start()
            copy.wait()
            return tmp[...]

        return load

    if land_near.shape[0] == tokens:
        land, load_land = block(land_near), lambda o, part: block(land_near)(o, part)[...]
    else:
        land, load_land = block(land_far), far_load(land_far)
    scatter_two = Scatter(packed_block(leaf), packed_block(acc), land, load_land, s2_send, s2_recv, r_size)
    scatter_proj = Scatter(
        packed_block(leaf), packed_block(acc), block(landp), far_load(landp), sp_send, sp_recv, r_size
    )
    scatter_one = Scatter(packed_block(leaf), packed_block(acc), land, load_land, s1_send, s1_recv, r_size)
    n = r_size * rows

    def partial_sums(dst, odd, lhs, rhs, contract):
        def one(i, carry):
            dst[pl.ds(pl.multiple_of(i * n, n), n), :] = lax.dot_general(
                lhs[pl.ds(pl.multiple_of((2 * i + odd) * n, n), n), :], rhs[...], contract, preferred_element_type=F32
            ).astype(BF16)
            return carry

        lax.fori_loop(0, s_size // 2, one, 0)

    partial_sums(leaf, 1, gpre, own_f, contract_last)
    scatter_two.start_leaves()
    clock.run(1)
    partial_sums(acc, 0, gpre, own_f, contract_last)
    load_q.start()
    if chunks == 1:
        product_rows(chunk, gpre, into_jobs(jf))
    clock.run(1)

    scatter_two.start_inner()
    clock.run(1)
    vec[...] = jnp.zeros_like(vec)
    gain_one, gain_two, proj_bias = (small_ref[i : i + 1, :] for i in (0, 3, 5))
    for load in loads[2:]:
        load.wait()
    cot = cot_v[...].astype(F32)
    middle = middle_ref[...]
    normed, inverse = norm_parts(middle)
    grad_in, grad_gain, grad_bias = norm_backward_rows(scatter_two.finish(), normed, inverse, gain_two)
    grad_middle = cot + grad_in
    branch = grad_middle.astype(BF16)
    gb_own[...] = branch
    gather = Gather(block(gb), g_send, g_recv, r_size, own=lambda o, part: gb_own.at[pl.ds(part * half, half)])
    gather.start(0)
    save_gb = pltpu.make_async_copy(gb_own, gb.at[pl.ds(0, rows)], tmp_sem.at[1])
    save_gb.start()
    vec[2:3, :] = jnp.sum(branch.astype(F32), axis=0, keepdims=True)
    vec[3:4, :] = grad_gain
    vec[4:5, :] = grad_bias
    vec[5:6, :] = jnp.sum(cot, axis=0, keepdims=True)
    clock.run(1)
    gather.start_rest()
    scatter_two.close()
    partial_sums(leaf, 1, act, own_p, (((1,), (0,)), ((), ())))
    scatter_proj.start_leaves()
    clock.run(1)
    partial_sums(acc, 0, act, own_p, (((1,), (0,)), ((), ())))
    gather.need_all()
    save_gb.wait()
    scatter_proj.start_inner()
    clock.run(1)

    if chunks > 1:
        go_acc[...] = jnp.zeros_like(go_acc)

    def branch_rows(i, carry):
        at = pl.ds(pl.multiple_of(i * step, step), step)
        fetch(gb, at, chunk2, 3).wait()
        do_ref[at, :] = lax.dot_general(
            chunk2[...], own_o[...], contract_last, preferred_element_type=F32
        ).astype(BF16)
        product_rows(att_ref.at[at], chunk2, into_jobs(jo) if chunks == 1 else into_sum(go_acc))
        return carry

    if chunks == 1:
        branch_rows(0, 0)
    else:
        lax.fori_loop(0, chunks, branch_rows, 0)
        into_jobs(jo)(0, own_cols, go_acc[...])
    clock.run(1)
    out_v[...] = (middle + (scatter_proj.finish() + proj_bias)).astype(BF16)

    def moved(src, dst, sem):
        far = remote(src, dst, sem.at[0], sem.at[1], z=s, s=z)
        near = pltpu.make_async_copy(src, dst, sem.at[1])

        @pl.when(s != z)
        def _():
            far.start()

        @pl.when(s == z)
        def _():
            near.start()

        def done():
            @pl.when(s != z)
            def _():
                far.wait()

            @pl.when(s == z)
            def _():
                near.wait()

        return done

    out_done = moved(out_v, out_home, mv_sem.at[0])

    code_row = jnp.concatenate([code_ref[i : i + 1, :] for i in range(devices)], axis=1)
    q_rows = min(rows if tokens > 2048 else 256, tokens)
    dk_acc[...] = jnp.zeros_like(dk_acc)
    dv_acc[...] = jnp.zeros_like(dv_acc)

    def attend(i):
        at = pl.ds(pl.multiple_of(i * q_rows, q_rows), q_rows)
        per = q_rows // rows
        code_q = jnp.concatenate(
            [
                jnp.transpose(jnp.broadcast_to(code_ref[pl.ds(i * per + j, 1), :], (8, rows)))[:, 0:1]
                for j in range(per)
            ],
            axis=0,
        )
        low_q = (code_q // SEG_STEP) * SEG_STEP
        allowed = jnp.logical_and(code_row >= low_q, code_row <= code_q)
        dqs, dks, dvs = [], [], []
        for h in range(heads):
            cols = slice(h * HEAD_DIM, (h + 1) * HEAD_DIM)
            q, do, k = q_ref[at, cols], do_ref[at, cols], k_ref[:, cols]
            scores = lax.dot_general(q, k, contract_last, preferred_element_type=F32)
            scores = jnp.where(allowed, scores, NEGATIVE)
            probs = jnp.exp(scores - lse_ref[at, h : h + 1])
            dp = lax.dot_general(do, v_ref[:, cols], contract_last, preferred_element_type=F32)
            delta = jnp.sum(probs * dp, axis=-1, keepdims=True)
            ds = (probs * (dp - delta)).astype(BF16)
            dqs.append(jnp.dot(ds, k, preferred_element_type=F32))
            dks.append(lax.dot_general(ds, q, contract_first, preferred_element_type=F32))
            dvs.append(lax.dot_general(probs.astype(BF16), do, contract_first, preferred_element_type=F32))
        gp[at, 0:own_cols] = (jnp.concatenate(dqs, axis=1) * (1.0 / math.sqrt(HEAD_DIM))).astype(BF16)
        dk_acc[...] += jnp.concatenate(dks, axis=1)
        dv_acc[...] += jnp.concatenate(dvs, axis=1)

    if chunks == 1:
        clock.loop(tokens // q_rows, attend)
    else:

        def attend_step(i, carry):
            attend(i)
            return carry

        lax.fori_loop(0, tokens // q_rows, attend_step, 0)
    gp[:, own_cols : 2 * own_cols] = dk_acc[...].astype(BF16)
    gp[:, 2 * own_cols :] = dv_acc[...].astype(BF16)

    scatter_proj.close()
    load_q.wait()
    partial_sums(leaf, 1, gp, own_q, contract_last)
    scatter_one.start_leaves()
    partial_sums(acc, 0, gp, own_q, contract_last)
    clock.run(1)

    def hidden_rows(i, carry):
        at = pl.ds(pl.multiple_of(i * step, step), step)
        fetch(h1, at, chunk, 2).wait()
        product_rows(chunk, gp.at[at], into_jobs(jq) if chunks == 1 else into_sum(gq_acc))
        return carry

    if chunks == 1:
        hidden_rows(0, 0)
    else:
        lax.fori_loop(0, chunks, hidden_rows, 0)
        into_jobs(jq)(0, width, gq_acc[...])
    scatter_one.start_inner()
    clock.run(2)

    resid = x_ref[...].astype(F32)
    normed, inverse = norm_parts(resid)
    grad_in, grad_gain, grad_bias = norm_backward_rows(scatter_one.finish(), normed, inverse, gain_one)
    ig_v[...] = (grad_middle + grad_in).astype(BF16)
    ig_done = moved(ig_v, ig_home, mv_sem.at[1])
    vec[0:1, :] = grad_gain
    vec[1:2, :] = grad_bias
    ff_lanes = -(-own_ff // 128) * 128
    q_lanes = -(-own_cols // 128) * 128
    vec[7:8, 0:own_ff] = jnp.sum(gpre[...].astype(F32), axis=0, keepdims=True)
    vec[7:8, ff_lanes : ff_lanes + own_cols] = jnp.sum(gp[:, :own_cols].astype(F32), axis=0, keepdims=True)
    vec[7:8, ff_lanes + q_lanes : ff_lanes + q_lanes + own_cols] = jnp.sum(
        gp[:, 2 * own_cols :].astype(F32), axis=0, keepdims=True
    )
    vec[pl.ds(8 + me, 1), :] = vec[7:8, :]

    hops = [("s", 1), ("s", 2)] + [("r", bit) for bit in bits_of(r_size)] + [("z", bit) for bit in bits_of(z_size)]
    for i, (axis, bit) in enumerate(hops):
        copy = remote(vec, vec_land.at[i], vec_send.at[i], vec_recv.at[i], **partner(axis, bit))
        copy.start()
        clock.run(1)
        copy.wait()
        vec[...] = vec[...] + vec_land[i]
    small_out[...] = vec[...]
    clock.run(clock.end)

    scatter_one.close()
    gather.close()
    out_done()
    ig_done()
    for total in (sum_proj, sum_fc, sum_qkv, sum_out):
        total.close()
    for i in range(r_size):
        pltpu.make_async_copy(home_proj.at[i], home_proj.at[i], ph_recv.at[i]).wait()
    for m in range(1, r_size):
        pltpu.make_async_copy(home_proj.at[0], home_proj.at[0], ph_send.at[m]).wait()
    for home, send, recv in ((home_fc, fh_send, fh_recv), (home_qkv, qh_send, qh_recv)):
        for i in range(devices):
            pltpu.make_async_copy(home.at[i], home.at[i], recv.at[i]).wait()
        for s_to in range(s_size):
            for m in range(r_size):
                sent = pltpu.make_async_copy(home.at[0], home.at[0], send.at[s_to, m])
                if m:
                    sent.wait()
                else:

                    @pl.when(s != s_to)
                    def _(sent=sent):
                        sent.wait()

    for i in range(devices):
        a, b = (i * own_cols) // shard_rows, (i * own_cols + own_cols - 1) // shard_rows

        @pl.when(jnp.logical_or(s == a, s == b))
        def _(i=i):
            pltpu.make_async_copy(home_out.at[i], home_out.at[i], oh_recv.at[i]).wait()

    for i, (s_to, valid) in enumerate(out_targets()):
        for m in range(r_size):
            far = valid if m else jnp.logical_and(valid, s_to != s)

            @pl.when(far)
            def _(i=i, m=m):
                pltpu.make_async_copy(home_out.at[0], home_out.at[0], oh_send.at[i, m]).wait()


def backward_part(h2, cot, wf, wp, h1, wq, wo, q, k, v, att, lse, code, middle, x_own, small, fcb):
    s_size, r_size, z_size = (lax.axis_size(a) for a in ("s", "r", "z"))
    devices = s_size * r_size
    rows, width = x_own.shape
    tokens = rows * devices
    own_cols = q.shape[1]
    heads = own_cols // HEAD_DIM
    own_ff = wf.shape[1]
    shard_rows = width // s_size
    p_rows = job_rows(own_ff // 2)
    p_n = own_ff // 2 // p_rows
    c_rows = job_rows(shard_rows)
    c_per = shard_rows // c_rows
    c_n = c_per * s_size // 2
    o_rows = job_rows(own_cols // 2)
    o_n = own_cols // 2 // o_rows
    hops = 2 + len(bits_of(r_size)) + len(bits_of(z_size))
    vec_rows = 8 + devices
    small_plane = tokens <= 1024
    step = tokens if small_plane else 256
    anywhere = pl.BlockSpec(memory_space=pl.ANY)
    vmem = pl.BlockSpec(memory_space=pltpu.VMEM)
    shape = jax.ShapeDtypeStruct
    dma = pltpu.SemaphoreType.DMA
    tree = [dma((2, devices))] * 2
    jobs = [(2, p_n, p_rows, width), (2, c_n, c_rows, own_ff), (2, c_n, c_rows, 3 * own_cols), (2, o_n, o_rows, width)]
    line = [dma(j[:2]) for j in jobs for _ in range(4)]

    def sums(*dims):
        return pltpu.VMEM((8, 128) if small_plane else dims, F32)

    return pl.pallas_call(
        backward_kernel,
        in_specs=[anywhere] * 7 + [vmem] * 10,
        out_specs=[anywhere] * 6 + [vmem] + [anywhere] * 3,
        out_shape=[
            shape((rows, width), BF16),
            shape((rows, width), BF16),
            shape((r_size,) + jobs[0], BF16),
            shape((devices, c_per, c_rows, own_ff), BF16),
            shape((devices, c_per, c_rows, 3 * own_cols), BF16),
            shape((devices,) + jobs[3], BF16),
            shape((vec_rows, width), F32),
            shape((tokens, width), BF16),
            shape((tokens, width), BF16),
            shape((tokens, width), BF16),
        ],
        scratch_shapes=[
            pltpu.VMEM((tokens // 2, width), BF16),
            pltpu.VMEM((tokens // 2, width), BF16),
            pltpu.VMEM((tokens if small_plane else 16, width), BF16),
            pltpu.VMEM((rows // 2, width), BF16),
        ]
        + [pltpu.VMEM(j, BF16) for j in jobs]
        + [pltpu.VMEM(j, BF16) for j in jobs]
        + [
            pltpu.VMEM((width, own_ff), BF16),
            pltpu.VMEM((own_ff, width), BF16),
            pltpu.VMEM((16, 128) if small_plane else (width, 3 * own_cols), BF16),
            pltpu.VMEM((own_cols, width), BF16),
            pltpu.VMEM((rows, width), BF16),
            pltpu.VMEM((step, width), BF16),
            pltpu.VMEM((step, width), BF16),
            sums(own_ff, width),
            sums(width, own_ff),
            sums(width, 3 * own_cols),
            pltpu.VMEM((tokens, own_ff), BF16),
            pltpu.VMEM((tokens, own_ff), BF16),
            pltpu.VMEM((tokens, own_cols), BF16),
            pltpu.VMEM((tokens, 3 * own_cols), BF16),
            pltpu.VMEM((tokens, own_cols), F32),
            pltpu.VMEM((tokens, own_cols), F32),
            sums(own_cols, width),
            pltpu.VMEM((vec_rows, width), F32),
            pltpu.VMEM((hops, vec_rows, width), F32),
            pltpu.VMEM((rows, width), BF16),
            pltpu.VMEM((rows, width), BF16),
            pltpu.VMEM((rows, width), BF16),
            dma((5,)),
        ]
        + tree * 4
        + [dma((4,)), dma((2, 2)), dma((hops,)), dma((hops,))]
        + line
        + [
            dma((r_size,)), dma((r_size,)),
            dma((s_size, r_size)), dma((devices,)),
            dma((s_size, r_size)), dma((devices,)),
            dma((2, r_size)), dma((devices,)),
        ],
        compiler_params=pltpu.CompilerParams(
            collective_id=1, has_side_effects=True, vmem_limit_bytes=62 << 20
        ),
        cost_estimate=pl.CostEstimate(
            flops=10 * heads * tokens * tokens * HEAD_DIM + 12 * tokens * width * own_ff,
            bytes_accessed=40 << 20,
            transcendentals=0,
        ),
        name="backward_part",
    )(h2, cot, wf, wp, h1, wq, wo, q, k, v, att, lse, code, middle, x_own, small, fcb)


def columns_out_kernel(parts, blocks_ref, out_ref):
    devices = blocks_ref.shape[0]
    each = blocks_ref.shape[3] // len(parts)
    for i, (first, width) in enumerate(parts):
        for device in range(devices):
            n = max(0, min(each, width - device * each))
            if n:
                lo = first + device * each
                out_ref[:, lo : lo + n] = blocks_ref[device, 0, :, i * each : i * each + n].astype(F32)


def columns_out(blocks, parts):
    devices, chunks, rows, columns = blocks.shape
    total = parts[-1][0] + parts[-1][1]
    step = 16 if rows % 16 == 0 else rows
    per = rows // step
    return pl.pallas_call(
        lambda *refs: columns_out_kernel(parts, *refs),
        grid=(chunks, per),
        in_specs=[pl.BlockSpec((devices, 1, step, columns), lambda i, j: (0, i, j, 0))],
        out_specs=pl.BlockSpec((step, total), lambda i, j: (i * per + j, 0)),
        out_shape=jax.ShapeDtypeStruct((chunks * rows, total), F32),
        compiler_params=pltpu.CompilerParams(vmem_limit_bytes=32 << 20),
        name="columns_out",
    )(blocks)


def rows_out_kernel(rows_ref, out_ref):
    out_ref[...] = rows_ref[...].astype(F32)


def rows_out(x):
    rows, width = x.shape
    step = job_rows(rows, 160)
    return pl.pallas_call(
        rows_out_kernel,
        grid=(rows // step,),
        in_specs=[pl.BlockSpec((step, width), lambda i: (i, 0))],
        out_specs=pl.BlockSpec((step, width), lambda i: (i, 0)),
        out_shape=jax.ShapeDtypeStruct((rows, width), F32),
        compiler_params=pltpu.CompilerParams(vmem_limit_bytes=32 << 20),
        name="rows_out",
    )(x)


def place(values_in, total, offset):
    return lax.dynamic_update_slice_in_dim(jnp.zeros((total,), F32), values_in.astype(F32), offset, axis=0)


def local(
    inputs,
    positions,
    segments,
    cotangent,
    ln1_gain,
    ln1_bias,
    w_qkv,
    qv_bias,
    w_out,
    out_bias,
    ln2_gain,
    ln2_bias,
    w_fc,
    fc_bias,
    w_proj,
    proj_bias,
):
    s = lax.axis_index("s")
    r = lax.axis_index("r")
    s_size = lax.axis_size("s")
    r_size = lax.axis_size("r")
    devices = s_size * r_size
    me = s * r_size + r
    rows, width = inputs.shape
    heads = width // HEAD_DIM
    own_heads = -(-heads // devices)
    own_cols = own_heads * HEAD_DIM
    head_total = own_cols * devices
    ff = w_fc.shape[1]
    own_ff = ff // devices
    shard_rows = width // s_size

    def head_pad(a):
        return jnp.pad(a, (0, head_total - width)).reshape(devices, own_cols)

    code = jnp.broadcast_to(segments * SEG_STEP + positions // BLOCK, (8, rows))
    small = jnp.stack(
        [place(a, width, s * shard_rows) for a in (ln1_gain, ln1_bias, out_bias, ln2_gain, ln2_bias, proj_bias)]
        + [jnp.zeros((width,), F32)] * 2
    )
    qv = place(qv_bias, 2 * width, s * 2 * shard_rows)
    smallh = jnp.concatenate([head_pad(qv[:width]), head_pad(qv[width:])])

    (
        hidden_one, hidden_two, cot, own_fc, own_qkv, own_out, queries, keys, values, attended, lse, code_all,
        middle, x_own, small, smallh,
    ) = forward_part(inputs, cotangent, code, small, smallh, w_qkv, w_fc, w_out)
    own_fcb = lax.dynamic_slice_in_dim(fc_bias, r * own_ff, own_ff).astype(F32).reshape(1, own_ff)
    out_home, ig_home, home_proj, home_fc, home_qkv, home_out, sums = backward_part(
        hidden_two, cot, own_fc, w_proj, hidden_one, own_qkv, own_out, queries, keys, values, attended, lse, code_all,
        middle, x_own, small, own_fcb,
    )[:7]

    def own_slice(vector):
        size = vector.shape[0] // s_size
        return lax.dynamic_slice_in_dim(vector, s * size, size)

    ff_lanes = -(-own_ff // 128) * 128
    q_lanes = -(-own_cols // 128) * 128
    by_device = sums[8:]
    g_fcb = by_device[:, :own_ff].reshape(ff)
    g_qb = by_device[:, ff_lanes : ff_lanes + own_cols].reshape(-1)[:width]
    g_vb = by_device[:, ff_lanes + q_lanes : ff_lanes + q_lanes + own_cols].reshape(-1)[:width]
    g_fc = columns_out(home_fc, [(0, ff)])
    g_qkv = columns_out(home_qkv, [(i * width, width) for i in range(3)])
    g_out = lax.dynamic_slice_in_dim(home_out.reshape(head_total, width), s * shard_rows, shard_rows)
    g_proj = rows_out(home_proj.reshape(ff // s_size, width))
    return (
        out_home,
        ig_home.astype(F32),
        own_slice(sums[0]),
        own_slice(sums[1]),
        g_qkv,
        own_slice(jnp.concatenate([g_qb, g_vb])),
        g_out.astype(F32),
        own_slice(sums[2]),
        own_slice(sums[3]),
        own_slice(sums[4]),
        g_fc,
        own_slice(g_fcb),
        g_proj,
        own_slice(sums[5]),
    )


def solution(mesh):
    ctx, shard = mesh.devices.shape
    fine = Mesh(mesh.devices.reshape(shard, ctx // shard, shard), ("z", "r", "s"))
    tokens = ("s", "z", "r")
    arg_specs = (
        P(tokens, None),
        P(tokens),
        P(tokens),
        P(tokens, None),
        P("s"),
        P("s"),
        P("s", None),
        P("s"),
        P("s", None),
        P("s"),
        P("s"),
        P("s"),
        P("s", None),
        P("s"),
        P("s", None),
        P("s"),
    )
    out_specs = (P(tokens, None), P(tokens, None)) + arg_specs[4:]
    return jax.shard_map(local, mesh=fine, in_specs=arg_specs, out_specs=out_specs, check_vma=False)
```

```python
import math

import jax
import jax.numpy as jnp
from jax import lax
from jax.experimental import pallas as pl
from jax.experimental.pallas import tpu as pltpu
from jax.sharding import Mesh, PartitionSpec as P

HEAD_DIM = 64
BLOCK = 256
EPSILON = 1e-05
NEGATIVE = -1e30
SEG_STEP = 65536
BF16 = jnp.bfloat16
F32 = jnp.float32


def bits_of(size):
    return [1 << i for i in range(size.bit_length() - 1)]


def norm_parts(values):
    centre = jnp.mean(values, axis=-1, keepdims=True)
    centred = values - centre
    spread = jnp.mean(centred * centred, axis=-1, keepdims=True)
    inverse = lax.rsqrt(spread + EPSILON)
    return centred * inverse, inverse


def gelu_parts(u):
    c = math.sqrt(2.0 / math.pi)
    squared = u * u
    t = jnp.tanh(c * (u + 0.044715 * (u * squared)))
    half = 0.5 * (1.0 + t)
    slope = half + 0.5 * u * (1.0 - t * t) * (c * (1.0 + 3.0 * 0.044715 * squared))
    return u * half, slope


def dot(a, b, contract=((1,), (0,))):
    return lax.dot_general(a, b, (contract, ((), ())), preferred_element_type=F32)


ACROSS_TOKENS = ((0,), (0,))
ON_LAST = ((1,), (1,))


MESH_ID = pl.DeviceIdType.MESH


def remote(src, dst, send_sem, recv_sem, **device):
    return pltpu.make_async_remote_copy(
        src_ref=src,
        dst_ref=dst,
        send_sem=send_sem,
        recv_sem=recv_sem,
        device_id=device,
        device_id_type=MESH_ID,
    )


def partner(axis, bit):
    return {axis: lax.axis_index(axis) ^ bit}


def plane_device(offset, r_size):
    found = {}
    if offset // r_size:
        found["s"] = lax.axis_index("s") ^ (offset // r_size)
    if offset % r_size:
        found["r"] = lax.axis_index("r") ^ (offset % r_size)
    return found


def tree_of(order, r_size):
    levels = []
    known = [(0, 0)]
    for axis, bit in order:
        step = bit * r_size if axis == "s" else bit
        known = known + [(o ^ step, depth + 1) for o, depth in known]
    found = {}
    for o, depth in known:
        if o == 0:
            continue
        for axis, bit in order[::-1]:
            step = bit * r_size if axis == "s" else bit
            if o & step:
                found.setdefault(depth, []).append((o, o ^ step, axis, bit))
                break
    for depth in sorted(found):
        levels.append(found[depth])
    return levels


def chip_orders(r_size):
    chips = [("s", 2)] + [("r", bit) for bit in bits_of(r_size)]
    return [chips + [("s", 1)], chips[::-1] + [("s", 1)]]


class Gather:
    def __init__(self, block, send_sem, recv_sem, r_size, parts=2, own=None):
        self.block = block
        self.own = own or block
        self.send_sem = send_sem
        self.recv_sem = recv_sem
        self.levels = [tree_of(order, r_size) for order in chip_orders(r_size)[:parts]]
        self.parts = parts
        self.arrived = set()

    def copy(self, part, transfer):
        offset, source, axis, bit = transfer
        src = self.own(0, part) if source == 0 else self.block(source, part)
        return remote(
            src,
            self.block(offset, part),
            self.send_sem.at[part, offset],
            self.recv_sem.at[part, offset],
            **partner(axis, bit),
        )

    def transfers(self):
        for level in range(len(self.levels[0])):
            for i in range(len(self.levels[0][level])):
                for part in range(self.parts):
                    yield level, part, self.levels[part][level][i]

    def find(self, part, offset):
        for _, p, t in self.transfers():
            if p == part and t[0] == offset:
                return t

    def need(self, part, offset):
        if offset and (part, offset) not in self.arrived:
            self.arrived.add((part, offset))
            self.copy(part, self.find(part, offset)).wait_recv()

    def start(self, level):
        for lv, part, t in self.transfers():
            if lv == level:
                self.need(part, t[1])
                self.copy(part, t).start()

    def start_rest(self):
        for level in range(1, len(self.levels[0])):
            self.start(level)

    def need_all(self):
        for _, part, t in self.transfers():
            self.need(part, t[0])

    def close(self):
        self.need_all()
        for _, part, t in self.transfers():
            self.copy(part, t).wait_send()


def attention_rows(rows, first, q_ref, k_ref, v_ref, code_q, code_k):
    heads = q_ref.shape[1] // HEAD_DIM
    low_q = (code_q // SEG_STEP) * SEG_STEP
    allowed = jnp.logical_and(code_k >= low_q, code_k <= code_q)
    outs = []
    sums = []
    for h in range(heads):
        cols = slice(h * HEAD_DIM, (h + 1) * HEAD_DIM)
        scores = lax.dot_general(
            q_ref[pl.ds(first, rows), cols],
            k_ref[:, cols],
            (((1,), (1,)), ((), ())),
            preferred_element_type=F32,
        )
        scores = jnp.where(allowed, scores, NEGATIVE)
        top = jnp.max(scores, axis=-1, keepdims=True)
        unnorm = jnp.exp(scores - top)
        total = jnp.sum(unnorm, axis=-1, keepdims=True)
        mixed = jnp.dot(unnorm.astype(BF16), v_ref[:, cols], preferred_element_type=F32)
        outs.append((mixed / total).astype(BF16))
        sums.append(top + jnp.log(total))
    return jnp.concatenate(outs, axis=1), jnp.concatenate(sums, axis=1)


def split_rows(n):
    first = -(-n // 32) * 16
    return ((0, first), (first, n - first))


class WeightPush:
    def __init__(self, source, dest, rows, send_sem, recv_sem, across):
        self.source, self.dest, self.rows = source, dest, rows
        self.send_sem, self.recv_sem = send_sem, recv_sem
        self.across = across

    def core_copy(self):
        s = lax.axis_index("s")
        return remote(
            self.source(s ^ 1),
            self.dest(s, 0, self.rows),
            self.send_sem.at[0],
            self.recv_sem.at[0],
            s=s ^ 1,
        )

    def chip_copy(self, m, part, landed=None):
        s = lax.axis_index("s")
        first, count = split_rows(self.rows)[part]
        return remote(
            self.source(s ^ m).at[pl.ds(first, count)],
            self.dest(s, first, count),
            self.send_sem.at[m],
            self.recv_sem.at[m],
            s=s ^ m,
        )

    def relay_copy(self, m, part):
        s = lax.axis_index("s")
        first, count = split_rows(self.rows)[part]
        ref = self.dest(s ^ m, first, count)
        return remote(
            ref, ref, self.send_sem.at[2 + m], self.recv_sem.at[2 + m], z=lax.axis_index("z") ^ 1
        )

    def per_part(self, act):
        odd = lax.axis_index("z") % 2
        for part in range(2):

            @pl.when(odd == part)
            def _(part=part):
                act(part)

    def start(self):
        if 1 in self.across:
            self.core_copy().start()

        def act(part):
            for m in self.across:
                if m != 1:
                    self.chip_copy(m, part).start()

        self.per_part(act)

    def relay(self):
        def act(part):
            for m in self.across:
                if m != 1:
                    self.chip_copy(m, part).wait_recv()
                    self.relay_copy(m, part).start()

        self.per_part(act)

    def need(self):
        if 1 in self.across:
            self.core_copy().wait_recv()

        def act(part):
            for m in self.across:
                if m != 1:
                    self.relay_copy(m, 1 - part).wait_recv()

        self.per_part(act)

    def close(self):
        if 1 in self.across:
            self.core_copy().wait_send()

        def act(part):
            for m in self.across:
                if m != 1:
                    self.chip_copy(m, part).wait_send()
                    self.relay_copy(m, part).wait_send()

        self.per_part(act)


def forward_kernel(
    x_in, cot_in, code_in, g1_in, b1_in, ob_in, g2_in, b2_in, pb_in, qv_in, fcb_in, wq_in, wf_in, wo_in,
    h1_out, h2_out, cot_out, wf_out, wq_out, wo_out, q_ref, k_ref, v_ref, att_ref, lse_ref, code_out,
    middle_out, x_own, small_ref, fcb_out,
    xt_vm, ct_vm, x_vm, cot_vm, vec_in, code_land, vec_land, bias_ref, h1, wq_vm, stage_q, wf_vm, stage_f, own_q, full_out, att_land, h2_own,
    x_sem, code_sem, cot_sem, small_sem, load_sem, h1_send, h1_recv, cd_send, cd_recv, ct_send, ct_recv, h2_send,
    h2_recv, wq_send, wq_recv, wf_send, wf_recv, wo_send, wo_recv, at_send, at_recv, out_sem,
):
    s, r, z = (lax.axis_index(a) for a in ("s", "r", "z"))
    s_size, r_size = lax.axis_size("s"), lax.axis_size("r")
    devices = s_size * r_size
    me = s * r_size + r
    width, rows = x_in.shape
    tokens = rows * devices
    own_cols = q_ref.shape[1]
    own_ff = wf_out.shape[1]
    shard_rows = wq_in.shape[0]

    def shard_at(i, first=0, count=shard_rows):
        return pl.ds(pl.multiple_of(i * shard_rows + first, 16), count)

    x_loads = [
        pltpu.make_async_copy(x_in, xt_vm, load_sem.at[3]),
        pltpu.make_async_copy(cot_in, ct_vm, load_sem.at[4]),
    ]
    for load in x_loads:
        load.start()

    barrier = pltpu.get_barrier_semaphore()
    for offset in range(1, devices):
        pl.semaphore_signal(barrier, inc=1, device_id=plane_device(offset, r_size), device_id_type=MESH_ID)
    pl.semaphore_signal(barrier, inc=1, device_id={"z": z ^ 1}, device_id_type=MESH_ID)

    @pl.when(s != z)
    def _():
        pl.semaphore_signal(barrier, inc=1, device_id={"z": s, "s": z}, device_id_type=MESH_ID)

    at = 0
    for ref in (g1_in, b1_in, ob_in, g2_in, b2_in, pb_in, qv_in, fcb_in):
        vec_in[0:1, at : at + ref.shape[0]] = ref[...].astype(F32).reshape(1, ref.shape[0])
        at += ref.shape[0]
    for load, src, dst in zip(x_loads, (xt_vm, ct_vm), (x_vm, cot_vm)):
        load.wait()
        dst[...] = jnp.transpose(src[...])
    pl.semaphore_wait(barrier, devices + jnp.where(s != z, 1, 0))

    def moved(src, dst, sem):
        far = remote(src, dst, sem.at[0], sem.at[1], z=s, s=z)
        near = pltpu.make_async_copy(src, dst, sem.at[1])

        @pl.when(s != z)
        def _():
            far.start()

        @pl.when(s == z)
        def _():
            near.start()

        def arrived():
            @pl.when(s != z)
            def _():
                far.wait_recv()

            @pl.when(s == z)
            def _():
                near.wait()

        def sent():
            @pl.when(s != z)
            def _():
                far.wait_send()

        return arrived, sent

    x_arrived, x_sent = moved(x_vm, x_own, x_sem)
    code_arrived, code_sent = moved(code_in, code_land.at[0], code_sem)
    loads = [
        pltpu.make_async_copy(wq_in, wq_vm, load_sem.at[0]),
        pltpu.make_async_copy(wf_in, wf_vm, load_sem.at[1]),
        pltpu.make_async_copy(wo_in, full_out.at[shard_at(s)], load_sem.at[2]),
    ]
    for load in loads:
        load.start()
    small_copies = [
        remote(vec_in, vec_land.at[s], small_sem.at[0, m], small_sem.at[1, m], s=s ^ m) for m in range(1, s_size)
    ]
    for copy in small_copies:
        copy.start()
    vec_land[s] = vec_in[...]
    if full_out.shape[0] > width:
        full_out[width:, :] = jnp.zeros((full_out.shape[0] - width, width), BF16)

    loads[0].wait()
    for s2 in range(s_size):
        for r2 in range(r_size):

            @pl.when(r == r2)
            def _(s2=s2, r2=r2):
                device = s2 * r_size + r2
                for part in range(3):
                    lo = device * own_cols
                    n = max(0, min(own_cols, width - lo))
                    if n:
                        stage_q[s2, :, part * own_cols : part * own_cols + n] = wq_vm[
                            :, part * width + lo : part * width + lo + n
                        ]
                    if n < own_cols:
                        stage_q[s2, :, part * own_cols + n : (part + 1) * own_cols] = jnp.zeros(
                            (shard_rows, own_cols - n), BF16
                        )

    push_q = WeightPush(
        lambda i: stage_q.at[i],
        lambda i, first, count: own_q.at[shard_at(i, first, count)],
        shard_rows, wq_send, wq_recv, (1, 2, 3),
    )
    push_q.start()
    own_q[shard_at(s), :] = stage_q[s]

    for copy in small_copies:
        copy.wait_recv()
    per = shard_rows
    small_ref[...] = jnp.zeros_like(small_ref)
    for s2 in range(s_size):
        for i in range(6):
            small_ref[i : i + 1, s2 * per : (s2 + 1) * per] = vec_land[s2, :, i * per : (i + 1) * per]
    for part in range(2):
        q_or_v = jnp.concatenate(
            [vec_land[part * s_size // 2 + i, :, 6 * per : 8 * per] for i in range(s_size // 2)], axis=1
        )
        for device in range(devices):
            n = max(0, min(own_cols, width - device * own_cols))
            if n:
                bias_ref[part, device : device + 1, 0:n] = q_or_v[:, device * own_cols : device * own_cols + n]
            if n < own_cols:
                bias_ref[part, device : device + 1, n:] = jnp.zeros((1, own_cols - n), F32)
    for r2 in range(r_size):

        @pl.when(r == r2)
        def _(r2=r2):
            fcb_out[...] = vec_in[:, 8 * per + r2 * own_ff : 8 * per + (r2 + 1) * own_ff]

    gain_one, bias_one, out_bias, gain_two, bias_two = (small_ref[i : i + 1, :] for i in range(5))
    x_arrived()
    cot_arrived, cot_sent = moved(cot_vm, cot_out.at[pl.ds(0, rows)], cot_sem)
    resid = x_own[...].astype(F32)
    normed, _ = norm_parts(resid)
    h1[0:rows, :] = (normed * gain_one + bias_one).astype(BF16)
    half = rows // 2

    def block_of(ref):
        return lambda offset, part: ref.at[pl.ds(offset * rows + part * half, half)]

    gather_one = Gather(block_of(h1), h1_send, h1_recv, r_size)
    gather_one.start(0)
    code_arrived()
    gather_code = Gather(lambda offset, part: code_land.at[offset], cd_send, cd_recv, r_size, parts=1)
    gather_code.start(0)

    loads[1].wait()
    for s2 in range(s_size):
        for r2 in range(r_size):

            @pl.when(r == r2)
            def _(s2=s2, r2=r2):
                lo = (s2 * r_size + r2) * own_ff
                stage_f[s2] = wf_vm[:, lo : lo + own_ff]

    gather_one.start(1)
    gather_code.start(1)
    push_q.relay()
    for level in range(2, len(gather_one.levels[0])):
        gather_one.start(level)
        gather_code.start(level)

    push_o = WeightPush(
        lambda i: full_out.at[shard_at(s)],
        lambda i, first, count: full_out.at[shard_at(i, first, count)],
        shard_rows, wo_send, wo_recv, (1, 2),
    )
    push_f = WeightPush(
        lambda i: stage_f.at[i],
        lambda i, first, count: wf_out.at[shard_at(i, first, count)],
        shard_rows, wf_send, wf_recv, (1, 2, 3),
    )
    own_f = pltpu.make_async_copy(
        stage_f.at[s], wf_out.at[shard_at(s)], load_sem.at[1]
    )
    own_f.start()
    gather_one.need_all()
    loads[2].wait()
    push_o.start()
    push_f.start()

    push_q.need()
    save_q = pltpu.make_async_copy(own_q, wq_out, out_sem.at[0])
    save_q.start()
    save_h = pltpu.make_async_copy(h1, h1_out, out_sem.at[1])
    save_h.start()
    q_bias = bias_ref[0, pl.ds(me, 1), :]
    v_bias = bias_ref[1, pl.ds(me, 1), :]
    step = min(512, tokens)
    score_scale = jnp.asarray(1.0 / math.sqrt(HEAD_DIM), BF16)

    def project(i, carry):
        at = pl.ds(pl.multiple_of(i * step, step), step)
        packed = jnp.dot(h1[at, :], own_q[...], preferred_element_type=F32)
        q_ref[at, :] = (packed[:, :own_cols] + q_bias).astype(BF16) * score_scale
        k_ref[at, :] = packed[:, own_cols : 2 * own_cols].astype(BF16)
        v_ref[at, :] = (packed[:, 2 * own_cols :] + v_bias).astype(BF16)
        return carry

    lax.fori_loop(0, tokens // step, project, 0)
    cot_arrived()
    gather_cot = Gather(block_of(cot_out), ct_send, ct_recv, r_size)
    gather_cot.start(0)
    gather_code.need_all()
    code_out[...] = code_land[:, 0, :]
    code_row = jnp.concatenate([code_land[i, 0:1, :] for i in range(devices)], axis=1)

    q_rows = min(rows if tokens > 2048 else 256, tokens)

    def attend(i, carry):
        first = pl.multiple_of(i * q_rows, q_rows)
        per = q_rows // rows
        code_col = jnp.concatenate(
            [jnp.transpose(code_land[i * per + j])[:, 0:1] for j in range(per)], axis=0
        )
        out, sums = attention_rows(q_rows, first, q_ref, k_ref, v_ref, code_col, code_row)
        att_ref[pl.ds(first, q_rows), :] = out
        lse_ref[pl.ds(first, q_rows), :] = sums
        return carry

    lax.fori_loop(0, tokens // q_rows, attend, 0)

    at_copies = []
    for offset in range(1, devices):
        at_copies.append(
            remote(
                att_ref.at[pl.ds(offset * rows, rows)],
                att_land.at[me],
                at_send.at[offset],
                at_recv.at[offset],
                **plane_device(offset, r_size),
            )
        )
    for copy in at_copies:
        copy.start()
    att_land[me] = att_ref[0:rows, :]
    push_o.relay()
    push_o.need()
    far = full_out.at[shard_at(s ^ 2)]
    out_core = remote(far, far, wo_send.at[5], wo_recv.at[5], s=s ^ 1)
    out_core.start()
    gather_cot.start(1)
    for copy in at_copies:
        copy.wait_recv()
    out_core.wait_recv()
    middle = resid + out_bias
    for device in range(devices):
        middle = middle + jnp.dot(
            att_land[device],
            full_out[device * own_cols : (device + 1) * own_cols, :],
            preferred_element_type=F32,
        )
    middle_out[...] = middle
    normed, _ = norm_parts(middle)
    h2_own[...] = (normed * gain_two + bias_two).astype(BF16)
    save_h2 = pltpu.make_async_copy(h2_own, h2_out.at[pl.ds(0, rows)], out_sem.at[2])
    save_h2.start()
    gather_two = Gather(
        block_of(h2_out), h2_send, h2_recv, r_size, own=lambda o, part: h2_own.at[pl.ds(part * half, half)]
    )
    gather_two.start(0)
    save_o = pltpu.make_async_copy(
        full_out.at[pl.ds(pl.multiple_of(me * own_cols, own_cols), own_cols)], wo_out, out_sem.at[3]
    )
    save_o.start()
    for level in range(2, len(gather_cot.levels[0])):
        gather_cot.start(level)
    push_f.relay()
    gather_two.start_rest()
    gather_two.close()
    gather_cot.close()
    gather_one.close()
    gather_code.close()
    push_f.need()
    for push in (push_q, push_o, push_f):
        push.close()
    out_core.wait_send()
    for copy in at_copies + small_copies:
        copy.wait_send()
    x_sent()
    code_sent()
    cot_sent()
    own_f.wait()
    for save in (save_q, save_h, save_h2, save_o):
        save.wait()


def forward_part(x, cot, code, small, w_qkv, w_fc, w_out):
    s_size, r_size = lax.axis_size("s"), lax.axis_size("r")
    devices = s_size * r_size
    width, rows = x.shape
    tokens = rows * devices
    shard_rows = w_qkv.shape[0]
    heads = width // HEAD_DIM
    own_heads = -(-heads // devices)
    own_cols = own_heads * HEAD_DIM
    own_ff = w_fc.shape[1] // devices
    anywhere = pl.BlockSpec(memory_space=pl.ANY)
    vmem = pl.BlockSpec(memory_space=pltpu.VMEM)
    shape = jax.ShapeDtypeStruct
    dma = pltpu.SemaphoreType.DMA
    flops = 2 * tokens * width * 3 * own_cols + 4 * own_heads * tokens * tokens * HEAD_DIM
    return pl.pallas_call(
        forward_kernel,
        in_specs=[anywhere] * 3 + [vmem] * 8 + [anywhere] * 3,
        out_specs=[anywhere] * 6 + [vmem] * 10,
        out_shape=[
            shape((tokens, width), BF16),
            shape((tokens, width), BF16),
            shape((tokens, width), BF16),
            shape((width, own_ff), BF16),
            shape((width, 3 * own_cols), BF16),
            shape((own_cols, width), BF16),
            shape((tokens, own_cols), BF16),
            shape((tokens, own_cols), BF16),
            shape((tokens, own_cols), BF16),
            shape((tokens, own_cols), BF16),
            shape((tokens, own_heads), F32),
            shape((devices, rows), jnp.int32),
            shape((rows, width), F32),
            shape((rows, width), BF16),
            shape((8, width), F32),
            shape((1, own_ff), F32),
        ],
        scratch_shapes=[
            pltpu.VMEM((width, rows), BF16),
            pltpu.VMEM((width, rows), BF16),
            pltpu.VMEM((rows, width), BF16),
            pltpu.VMEM((rows, width), BF16),
            pltpu.VMEM((1, sum(a.shape[0] for a in small)), F32),
            pltpu.VMEM((devices, 8, rows), jnp.int32),
            pltpu.VMEM((s_size, 1, sum(a.shape[0] for a in small)), F32),
            pltpu.VMEM((2, devices, own_cols), F32),
            pltpu.VMEM((tokens, width), BF16),
            pltpu.VMEM(w_qkv.shape, BF16),
            pltpu.VMEM((s_size, shard_rows, 3 * own_cols), BF16),
            pltpu.VMEM(w_fc.shape, BF16),
            pltpu.VMEM((s_size, shard_rows, own_ff), BF16),
            pltpu.VMEM((width, 3 * own_cols), BF16),
            pltpu.VMEM((devices * own_cols, width), BF16),
            pltpu.VMEM((devices, rows, own_cols), BF16),
            pltpu.VMEM((rows, width), BF16),
            dma((2,)), dma((2,)), dma((2,)), dma((2, s_size)), dma((5,)),
            dma((2, devices)), dma((2, devices)), dma((1, devices)), dma((1, devices)),
            dma((2, devices)), dma((2, devices)), dma((2, devices)), dma((2, devices)),
            dma((6,)), dma((6,)), dma((6,)), dma((6,)), dma((6,)), dma((6,)),
            dma((devices,)), dma((devices,)), dma((4,)),
        ],
        compiler_params=pltpu.CompilerParams(
            collective_id=0, has_side_effects=True, vmem_limit_bytes=60 << 20
        ),
        cost_estimate=pl.CostEstimate(flops=flops, bytes_accessed=40 << 20, transcendentals=0),
        name="forward_part",
    )(x, cot, code, *small, w_qkv, w_fc, w_out)


class Scatter:
    def __init__(self, leaf, acc, land, load, send_sem, recv_sem, r_size):
        self.leaf, self.acc, self.land, self.load = leaf, acc, land, load
        self.send_sem, self.recv_sem = send_sem, recv_sem
        self.levels = [tree_of(order, r_size) for order in chip_orders(r_size)]

    def copy(self, part, transfer):
        offset, _, axis, bit = transfer
        src = self.acc(offset, part) if self.children(part, offset) else self.leaf(offset, part)
        return remote(
            src,
            self.land(offset, part),
            self.send_sem.at[part, offset],
            self.recv_sem.at[part, offset],
            **partner(axis, bit),
        )

    def children(self, part, offset):
        return [t for level in self.levels[part] for t in level if t[1] == offset]

    def start_leaves(self):
        for level in range(len(self.levels[0]) - 1, -1, -1):
            for i in range(len(self.levels[0][level])):
                for part in range(2):
                    t = self.levels[part][level][i]
                    if not self.children(part, t[0]):
                        self.copy(part, t).start()

    def total(self, part, offset):
        value = self.acc(offset, part)[...].astype(F32)
        for t in self.children(part, offset)[::-1]:
            self.copy(part, t).wait_recv()
            value = value + self.load(t[0], part).astype(F32)
        return value

    def start_inner(self):
        for level in range(len(self.levels[0]) - 1, -1, -1):
            for i in range(len(self.levels[0][level])):
                for part in range(2):
                    t = self.levels[part][level][i]
                    if self.children(part, t[0]):
                        self.acc(t[0], part)[...] = self.total(part, t[0]).astype(BF16)
                        self.copy(part, t).start()

    def finish(self):
        return jnp.concatenate([self.total(part, 0) for part in range(2)], axis=0)

    def close(self):
        for part in range(2):
            for level in self.levels[part]:
                for t in level:
                    self.copy(part, t).wait_send()


class LineSum:
    def __init__(self, jobs, land, rs_send, rs_recv, ag_send, ag_recv, home, start):
        self.jobs, self.land = jobs, land
        self.rs_send, self.rs_recv, self.ag_send, self.ag_recv = rs_send, rs_recv, ag_send, ag_recv
        self.home = home
        self.n = jobs.shape[1]
        self.z = lax.axis_index("z")
        self.last = lax.axis_size("z") - 1
        self.start = start
        self.end = start + self.n + 2 * self.last

    def place(self, d):
        return self.z if d == 0 else self.last - self.z

    def up(self, d, j):
        return remote(
            self.jobs.at[d, j], self.land.at[d, j], self.rs_send.at[d, j], self.rs_recv.at[d, j], z=self.z + 1 - 2 * d
        )

    def down(self, d, j):
        return remote(
            self.land.at[d, j], self.land.at[d, j], self.ag_send.at[d, j], self.ag_recv.at[d, j], z=self.z - 1 + 2 * d
        )

    def add(self, d, j):
        place = self.place(d)

        @pl.when(place > 0)
        def _():
            self.up(d, j).wait_recv()
            total = (self.jobs[d, j].astype(F32) + self.land[d, j].astype(F32)).astype(BF16)

            @pl.when(place < self.last)
            def _():
                self.jobs[d, j] = total

            @pl.when(place == self.last)
            def _():
                self.land[d, j] = total

        @pl.when(place < self.last)
        def _():
            self.up(d, j).start()

        @pl.when(place == self.last)
        def _():
            self.down(d, j).start()
            self.home(d, j)

    def back(self, d, j):
        place = self.place(d)
        self.down(d, j).wait_recv()

        @pl.when(place > 0)
        def _():
            self.down(d, j).start()

        self.home(d, j)

    def tick(self, k):
        for d in range(2):
            j = k - self.start - self.place(d)

            @pl.when(jnp.logical_and(j >= 0, j < self.n))
            def _(d=d, j=j):
                self.add(d, j)

        for d in range(2):
            place = self.place(d)
            j = k - self.start - 2 * self.last + place

            @pl.when(jnp.logical_and(place < self.last, jnp.logical_and(j >= 0, j < self.n)))
            def _(d=d, j=j):
                self.back(d, j)

    def close(self):
        def one(j, carry):
            for d in range(2):
                place = self.place(d)

                @pl.when(place < self.last)
                def _(d=d):
                    self.up(d, j).wait_send()

                @pl.when(place > 0)
                def _(d=d):
                    self.down(d, j).wait_send()

            return carry

        lax.fori_loop(0, self.n, one, 0)


class Clock:
    def __init__(self, sums):
        self.sums = sums
        self.now = 0
        self.end = max(one.end for one in sums)

    def ticks(self, first, lo, hi):
        for one in self.sums:
            if one.start < hi and one.end > lo:
                one.tick(first)

    def run(self, count):
        lo, hi = self.now, min(self.now + count, self.end)
        self.now = hi
        if hi - lo == 1:
            self.ticks(lo, lo, hi)
        elif hi > lo:

            def step(k, carry):
                self.ticks(k, lo, hi)
                return carry

            lax.fori_loop(lo, hi, step, 0)

    def loop(self, count, body):
        lo, hi = self.now, min(self.now + count, self.end)
        self.now = hi

        def step(i, carry):
            body(i)
            self.ticks(lo + i, lo, lo + count)
            return carry

        lax.fori_loop(0, count, step, 0)


def product_rows(lhs, rhs, write):
    for lo in range(0, lhs.shape[1], 256):
        hi = min(lhs.shape[1], lo + 256)
        value = lax.dot_general(
            lhs[:, lo:hi], rhs[...], (((0,), (0,)), ((), ())), preferred_element_type=F32
        )
        write(lo, hi, value)


def into_jobs(jobs):
    n, size = jobs.shape[1:3]

    def write(lo, hi, value):
        value = value.astype(BF16)
        for job in range(lo // size, -(-hi // size)):
            a, b = max(lo, job * size), min(hi, (job + 1) * size)
            jobs[job // n, job % n, a - job * size : b - job * size, :] = value[a - lo : b - lo, :]

    return write


def into_sum(acc):
    def write(lo, hi, value):
        acc[lo:hi, :] += value

    return write


def job_rows(n, most=80):
    for rows in range(most, 15, -16):
        if n % rows == 0:
            return rows
    return n


def norm_backward_rows(grad, normed, inverse, gain):
    scaled = grad * gain
    mean_scaled = jnp.mean(scaled, axis=-1, keepdims=True)
    mean_product = jnp.mean(scaled * normed, axis=-1, keepdims=True)
    grad_in = inverse * (scaled - mean_scaled - normed * mean_product)
    return (
        grad_in,
        jnp.sum(grad * normed, axis=0, keepdims=True),
        jnp.sum(grad, axis=0, keepdims=True),
    )


def backward_kernel(
    h2, cot_in, wf, wp, h1, wq, wo, q_ref, k_ref, v_ref, att_ref, lse_ref, code_ref, middle_ref, x_ref,
    small_ref, fcb_ref,
    out_home, ig_home, home_proj, home_fc, home_qkv, home_out, small_out, landp, land_far, gb,
    acc, leaf, land_near, tmp, jp, jf, jq, jo, lp, lf, lq, lo_, own_f, own_p, own_q, own_o, cot_v, chunk, chunk2,
    gp_acc, gf_acc, gq_acc, act, gpre, do_ref, gp, dk_acc, dv_acc, go_acc, vec, vec_land, gb_own, out_v, ig_v,
    load_sem, s2_send, s2_recv, sp_send, sp_recv, s1_send, s1_recv, g_send, g_recv, tmp_sem, mv_sem,
    vec_send, vec_recv,
    p_rs, p_rr, p_as, p_ar, f_rs, f_rr, f_as, f_ar, q_rs, q_rr, q_as, q_ar, o_rs, o_rr, o_as, o_ar,
    ph_send, ph_recv, fh_send, fh_recv, qh_send, qh_recv, oh_send, oh_recv,
):
    s, r, z = (lax.axis_index(a) for a in ("s", "r", "z"))
    s_size, r_size, z_size = (lax.axis_size(a) for a in ("s", "r", "z"))
    devices = s_size * r_size
    me = s * r_size + r
    rows, width = x_ref.shape
    tokens = rows * devices
    half = rows // 2
    own_cols = q_ref.shape[1]
    own_ff = wf.shape[1]
    heads = own_cols // HEAD_DIM
    shard_rows = width // s_size
    step = chunk.shape[0]
    contract_last = (((1,), (1,)), ((), ()))
    contract_first = (((0,), (0,)), ((), ()))

    barrier = pltpu.get_barrier_semaphore()
    for offset in range(1, devices):
        pl.semaphore_signal(barrier, inc=1, device_id=plane_device(offset, r_size), device_id_type=MESH_ID)
    for bit in bits_of(z_size):
        pl.semaphore_signal(barrier, inc=1, device_id={"z": z ^ bit}, device_id_type=MESH_ID)
    inner = jnp.logical_and(z > 0, z < z_size - 1)

    @pl.when(s != z)
    def _():
        pl.semaphore_signal(barrier, inc=1, device_id={"z": s, "s": z}, device_id_type=MESH_ID)

    @pl.when(inner)
    def _():
        pl.semaphore_signal(
            barrier, inc=1, device_id={"z": jnp.where(z % 2 == 1, z + 1, z - 1)}, device_id_type=MESH_ID
        )

    loads = [
        pltpu.make_async_copy(src, dst, load_sem.at[i])
        for i, (src, dst) in enumerate(
            (
                (wf, own_f),
                (wp.at[pl.ds(pl.multiple_of(r * own_ff, 8), own_ff)], own_p),
                (wo, own_o),
                (cot_in.at[pl.ds(0, rows)], cot_v),
            )
        )
    ]
    for load in loads:
        load.start()
    if own_q.shape[0] != width:
        own_q = own_f.at[:, : 3 * own_cols]
    load_q = pltpu.make_async_copy(wq, own_q, load_sem.at[4])

    loads[0].wait()
    loads[1].wait()
    chunks = tokens // step
    if chunks > 1:
        gp_acc[...] = jnp.zeros_like(gp_acc)
        gf_acc[...] = jnp.zeros_like(gf_acc)
        gq_acc[...] = jnp.zeros_like(gq_acc)

    def fetch(src, at, dst, i):
        copy = pltpu.make_async_copy(src.at[at], dst, tmp_sem.at[i])
        copy.start()
        return copy

    piece = min(256, step)

    def feed_forward(i, carry):
        at = pl.ds(pl.multiple_of(i * step, step), step)
        first = fetch(h2, at, chunk, 2)
        second = fetch(cot_in, at, chunk2, 3)
        first.wait()
        second.wait()

        def one(j, inner_carry):
            here = pl.ds(pl.multiple_of(j * piece, piece), piece)
            there = pl.ds(pl.multiple_of(i * step + j * piece, piece), piece)
            pre = jnp.dot(chunk[here, :], own_f[...], preferred_element_type=F32) + fcb_ref[...]
            value, slope = gelu_parts(pre)
            act[there, :] = value.astype(BF16)
            back = lax.dot_general(chunk2[here, :], own_p[...], contract_last, preferred_element_type=F32)
            gpre[there, :] = (back * slope).astype(BF16)
            return inner_carry

        lax.fori_loop(0, step // piece, one, 0)
        product_rows(act.at[at], chunk2, into_jobs(jp) if chunks == 1 else into_sum(gp_acc))
        if chunks > 1:
            product_rows(chunk, gpre.at[at], into_sum(gf_acc))
        return carry

    if chunks == 1:
        feed_forward(0, 0)
    else:
        lax.fori_loop(0, chunks, feed_forward, 0)
        into_jobs(jp)(0, own_ff, gp_acc[...])
        into_jobs(jf)(0, width, gf_acc[...])

    peers = devices - 1 + len(bits_of(z_size))
    pl.semaphore_wait(barrier, peers + jnp.where(s != z, 1, 0) + jnp.where(inner, 1, 0))

    def to_home(src, dst, send, recv, s_to, m):
        far = remote(src, dst, send, recv, s=s_to, r=r ^ m)
        if m:
            far.start()
        else:
            near = pltpu.make_async_copy(src, dst, recv)

            @pl.when(s_to == s)
            def _():
                near.start()

            @pl.when(s_to != s)
            def _():
                far.start()

    def home_of_proj(d, j):
        for m in range(r_size):
            src, dst = lp.at[d, j], home_proj.at[r, d, j]
            if m:
                remote(src, dst, ph_send.at[m], ph_recv.at[r], r=r ^ m).start()
            else:
                pltpu.make_async_copy(src, dst, ph_recv.at[r]).start()

    def home_of_columns(landing, home, send, recv):
        per = landing.shape[1] // (s_size // 2)

        def go(d, j):
            s_to = d * (s_size // 2) + j // per
            for m in range(r_size):
                to_home(landing.at[d, j], home.at[me, j % per], send.at[s_to, m], recv.at[me], s_to, m)

        return go

    def out_targets():
        a = (me * own_cols) // shard_rows
        b = (me * own_cols + own_cols - 1) // shard_rows
        return ((a, a < s_size), (b, jnp.logical_and(b != a, b < s_size)))

    margin = (home_out.shape[0] - shard_rows) // 2

    def out_at(s_to, d, j):
        n_out, size = lo_.shape[1:3]
        first = margin + me * own_cols - s_to * shard_rows + (d * n_out + j) * size
        return pl.ds(pl.multiple_of(first, 16), size)

    def home_of_out(d, j):
        for i, (s_to, valid) in enumerate(out_targets()):

            @pl.when(valid)
            def _(i=i, s_to=s_to):
                for m in range(r_size):
                    to_home(lo_.at[d, j], home_out.at[out_at(s_to, d, j)], oh_send.at[i, m], oh_recv.at[me], s_to, m)

    sum_proj = LineSum(jp, lp, p_rs, p_rr, p_as, p_ar, home_of_proj, 0)
    start = sum_proj.n
    sum_fc = LineSum(jf, lf, f_rs, f_rr, f_as, f_ar, home_of_columns(lf, home_fc, fh_send, fh_recv), start)
    start += sum_fc.n
    sum_out = LineSum(jo, lo_, o_rs, o_rr, o_as, o_ar, home_of_out, start)
    start += sum_out.n
    sum_qkv = LineSum(jq, lq, q_rs, q_rr, q_as, q_ar, home_of_columns(lq, home_qkv, qh_send, qh_recv), start)
    clock = Clock([sum_proj, sum_fc, sum_out, sum_qkv])
    clock.run(1)

    def slot(offset):
        return (offset // r_size) // 2 * r_size + offset % r_size

    def block(ref):
        return lambda o, part: ref.at[pl.ds(o * rows + part * half, half)]

    def packed_block(ref):
        return lambda o, part: ref.at[pl.ds(slot(o) * rows + part * half, half)]

    def far_load(ref):
        def load(o, part):
            copy = pltpu.make_async_copy(block(ref)(o, part), tmp, tmp_sem.at[0])
            copy.start()
            copy.wait()
            return tmp[...]

        return load

    if land_near.shape[0] == tokens:
        land, load_land = block(land_near), lambda o, part: block(land_near)(o, part)[...]
    else:
        land, load_land = block(land_far), far_load(land_far)
    scatter_two = Scatter(packed_block(leaf), packed_block(acc), land, load_land, s2_send, s2_recv, r_size)
    scatter_proj = Scatter(
        packed_block(leaf), packed_block(acc), block(landp), far_load(landp), sp_send, sp_recv, r_size
    )
    scatter_one = Scatter(packed_block(leaf), packed_block(acc), land, load_land, s1_send, s1_recv, r_size)
    n = r_size * rows

    def partial_sums(dst, odd, lhs, rhs, contract):
        def one(i, carry):
            dst[pl.ds(pl.multiple_of(i * n, n), n), :] = lax.dot_general(
                lhs[pl.ds(pl.multiple_of((2 * i + odd) * n, n), n), :], rhs[...], contract, preferred_element_type=F32
            ).astype(BF16)
            return carry

        lax.fori_loop(0, s_size // 2, one, 0)

    partial_sums(leaf, 1, gpre, own_f, contract_last)
    scatter_two.start_leaves()
    clock.run(1)
    partial_sums(acc, 0, gpre, own_f, contract_last)
    load_q.start()
    if chunks == 1:
        product_rows(chunk, gpre, into_jobs(jf))
    clock.run(1)

    scatter_two.start_inner()
    clock.run(1)
    vec[...] = jnp.zeros_like(vec)
    gain_one, gain_two, proj_bias = (small_ref[i : i + 1, :] for i in (0, 3, 5))
    for load in loads[2:]:
        load.wait()
    cot = cot_v[...].astype(F32)
    middle = middle_ref[...]
    normed, inverse = norm_parts(middle)
    grad_in, grad_gain, grad_bias = norm_backward_rows(scatter_two.finish(), normed, inverse, gain_two)
    grad_middle = cot + grad_in
    branch = grad_middle.astype(BF16)
    gb_own[...] = branch
    gather = Gather(block(gb), g_send, g_recv, r_size, own=lambda o, part: gb_own.at[pl.ds(part * half, half)])
    gather.start(0)
    save_gb = pltpu.make_async_copy(gb_own, gb.at[pl.ds(0, rows)], tmp_sem.at[1])
    save_gb.start()
    vec[2:3, :] = jnp.sum(branch.astype(F32), axis=0, keepdims=True)
    vec[3:4, :] = grad_gain
    vec[4:5, :] = grad_bias
    vec[5:6, :] = jnp.sum(cot, axis=0, keepdims=True)
    clock.run(1)
    gather.start_rest()
    scatter_two.close()
    partial_sums(leaf, 1, act, own_p, (((1,), (0,)), ((), ())))
    scatter_proj.start_leaves()
    clock.run(1)
    partial_sums(acc, 0, act, own_p, (((1,), (0,)), ((), ())))
    gather.need_all()
    save_gb.wait()
    scatter_proj.start_inner()
    clock.run(1)

    if chunks > 1:
        go_acc[...] = jnp.zeros_like(go_acc)

    def branch_rows(i, carry):
        at = pl.ds(pl.multiple_of(i * step, step), step)
        fetch(gb, at, chunk2, 3).wait()
        do_ref[at, :] = lax.dot_general(
            chunk2[...], own_o[...], contract_last, preferred_element_type=F32
        ).astype(BF16)
        product_rows(att_ref.at[at], chunk2, into_jobs(jo) if chunks == 1 else into_sum(go_acc))
        return carry

    if chunks == 1:
        branch_rows(0, 0)
    else:
        lax.fori_loop(0, chunks, branch_rows, 0)
        into_jobs(jo)(0, own_cols, go_acc[...])
    clock.run(1)
    out_v[...] = (middle + (scatter_proj.finish() + proj_bias)).astype(BF16)

    def moved(src, dst, sem):
        far = remote(src, dst, sem.at[0], sem.at[1], z=s, s=z)
        near = pltpu.make_async_copy(src, dst, sem.at[1])

        @pl.when(s != z)
        def _():
            far.start()

        @pl.when(s == z)
        def _():
            near.start()

        def done():
            @pl.when(s != z)
            def _():
                far.wait()

            @pl.when(s == z)
            def _():
                near.wait()

        return done

    out_done = moved(out_v, out_home, mv_sem.at[0])

    code_row = jnp.concatenate([code_ref[i : i + 1, :] for i in range(devices)], axis=1)
    q_rows = min(rows if tokens > 2048 else 256, tokens)
    dk_acc[...] = jnp.zeros_like(dk_acc)
    dv_acc[...] = jnp.zeros_like(dv_acc)

    def attend(i):
        at = pl.ds(pl.multiple_of(i * q_rows, q_rows), q_rows)
        per = q_rows // rows
        code_q = jnp.concatenate(
            [
                jnp.transpose(jnp.broadcast_to(code_ref[pl.ds(i * per + j, 1), :], (8, rows)))[:, 0:1]
                for j in range(per)
            ],
            axis=0,
        )
        low_q = (code_q // SEG_STEP) * SEG_STEP
        allowed = jnp.logical_and(code_row >= low_q, code_row <= code_q)
        dqs, dks, dvs = [], [], []
        for h in range(heads):
            cols = slice(h * HEAD_DIM, (h + 1) * HEAD_DIM)
            q, do, k = q_ref[at, cols], do_ref[at, cols], k_ref[:, cols]
            scores = lax.dot_general(q, k, contract_last, preferred_element_type=F32)
            scores = jnp.where(allowed, scores, NEGATIVE)
            probs = jnp.exp(scores - lse_ref[at, h : h + 1])
            dp = lax.dot_general(do, v_ref[:, cols], contract_last, preferred_element_type=F32)
            delta = jnp.sum(probs * dp, axis=-1, keepdims=True)
            ds = (probs * (dp - delta)).astype(BF16)
            dqs.append(jnp.dot(ds, k, preferred_element_type=F32))
            dks.append(lax.dot_general(ds, q, contract_first, preferred_element_type=F32))
            dvs.append(lax.dot_general(probs.astype(BF16), do, contract_first, preferred_element_type=F32))
        gp[at, 0:own_cols] = (jnp.concatenate(dqs, axis=1) * (1.0 / math.sqrt(HEAD_DIM))).astype(BF16)
        dk_acc[...] += jnp.concatenate(dks, axis=1)
        dv_acc[...] += jnp.concatenate(dvs, axis=1)

    if chunks == 1:
        clock.loop(tokens // q_rows, attend)
    else:

        def attend_step(i, carry):
            attend(i)
            return carry

        lax.fori_loop(0, tokens // q_rows, attend_step, 0)
    gp[:, own_cols : 2 * own_cols] = dk_acc[...].astype(BF16)
    gp[:, 2 * own_cols :] = dv_acc[...].astype(BF16)

    scatter_proj.close()
    load_q.wait()
    partial_sums(leaf, 1, gp, own_q, contract_last)
    scatter_one.start_leaves()
    partial_sums(acc, 0, gp, own_q, contract_last)
    clock.run(1)

    def hidden_rows(i, carry):
        at = pl.ds(pl.multiple_of(i * step, step), step)
        fetch(h1, at, chunk, 2).wait()
        product_rows(chunk, gp.at[at], into_jobs(jq) if chunks == 1 else into_sum(gq_acc))
        return carry

    if chunks == 1:
        hidden_rows(0, 0)
    else:
        lax.fori_loop(0, chunks, hidden_rows, 0)
        into_jobs(jq)(0, width, gq_acc[...])
    scatter_one.start_inner()
    clock.run(2)

    resid = x_ref[...].astype(F32)
    normed, inverse = norm_parts(resid)
    grad_in, grad_gain, grad_bias = norm_backward_rows(scatter_one.finish(), normed, inverse, gain_one)
    ig_v[...] = (grad_middle + grad_in).astype(BF16)
    ig_done = moved(ig_v, ig_home, mv_sem.at[1])
    vec[0:1, :] = grad_gain
    vec[1:2, :] = grad_bias
    ff_lanes = -(-own_ff // 128) * 128
    q_lanes = -(-own_cols // 128) * 128
    vec[7:8, 0:own_ff] = jnp.sum(gpre[...].astype(F32), axis=0, keepdims=True)
    vec[7:8, ff_lanes : ff_lanes + own_cols] = jnp.sum(gp[:, :own_cols].astype(F32), axis=0, keepdims=True)
    vec[7:8, ff_lanes + q_lanes : ff_lanes + q_lanes + own_cols] = jnp.sum(
        gp[:, 2 * own_cols :].astype(F32), axis=0, keepdims=True
    )
    vec[pl.ds(8 + me, 1), :] = vec[7:8, :]

    hops = [("s", 1), ("s", 2)] + [("r", bit) for bit in bits_of(r_size)] + [("z", bit) for bit in bits_of(z_size)]
    for i, (axis, bit) in enumerate(hops):
        copy = remote(vec, vec_land.at[i], vec_send.at[i], vec_recv.at[i], **partner(axis, bit))
        copy.start()
        clock.run(1)
        copy.wait()
        vec[...] = vec[...] + vec_land[i]
    small_out[...] = vec[...]
    clock.run(clock.end)

    scatter_one.close()
    gather.close()
    out_done()
    ig_done()
    for total in (sum_proj, sum_fc, sum_qkv, sum_out):
        total.close()
    for i in range(r_size):
        pltpu.make_async_copy(home_proj.at[i], home_proj.at[i], ph_recv.at[i]).wait()
    for m in range(1, r_size):
        pltpu.make_async_copy(home_proj.at[0], home_proj.at[0], ph_send.at[m]).wait()
    for home, send, recv in ((home_fc, fh_send, fh_recv), (home_qkv, qh_send, qh_recv)):
        for i in range(devices):
            pltpu.make_async_copy(home.at[i], home.at[i], recv.at[i]).wait()
        for s_to in range(s_size):
            for m in range(r_size):
                sent = pltpu.make_async_copy(home.at[0], home.at[0], send.at[s_to, m])
                if m:
                    sent.wait()
                else:

                    @pl.when(s != s_to)
                    def _(sent=sent):
                        sent.wait()

    out_block = home_out.at[pl.ds(0, own_cols)]
    for i in range(devices):
        a, b = (i * own_cols) // shard_rows, (i * own_cols + own_cols - 1) // shard_rows

        @pl.when(jnp.logical_or(s == a, s == b))
        def _(i=i):
            pltpu.make_async_copy(out_block, out_block, oh_recv.at[i]).wait()

    for i, (s_to, valid) in enumerate(out_targets()):
        for m in range(r_size):
            far = valid if m else jnp.logical_and(valid, s_to != s)

            @pl.when(far)
            def _(i=i, m=m):
                pltpu.make_async_copy(out_block, out_block, oh_send.at[i, m]).wait()


def backward_part(h2, cot, wf, wp, h1, wq, wo, q, k, v, att, lse, code, middle, x_own, small, fcb):
    s_size, r_size, z_size = (lax.axis_size(a) for a in ("s", "r", "z"))
    devices = s_size * r_size
    rows, width = x_own.shape
    tokens = rows * devices
    own_cols = q.shape[1]
    heads = own_cols // HEAD_DIM
    own_ff = wf.shape[1]
    shard_rows = width // s_size
    p_rows = job_rows(own_ff // 2)
    p_n = own_ff // 2 // p_rows
    c_rows = job_rows(shard_rows)
    c_per = shard_rows // c_rows
    c_n = c_per * s_size // 2
    o_rows = job_rows(own_cols // 2)
    o_n = own_cols // 2 // o_rows
    hops = 2 + len(bits_of(r_size)) + len(bits_of(z_size))
    vec_rows = 8 + devices
    small_plane = tokens <= 1024
    step = tokens if small_plane else 256
    anywhere = pl.BlockSpec(memory_space=pl.ANY)
    vmem = pl.BlockSpec(memory_space=pltpu.VMEM)
    shape = jax.ShapeDtypeStruct
    dma = pltpu.SemaphoreType.DMA
    tree = [dma((2, devices))] * 2
    jobs = [(2, p_n, p_rows, width), (2, c_n, c_rows, own_ff), (2, c_n, c_rows, 3 * own_cols), (2, o_n, o_rows, width)]
    line = [dma(j[:2]) for j in jobs for _ in range(4)]

    def sums(*dims):
        return pltpu.VMEM((8, 128) if small_plane else dims, F32)

    return pl.pallas_call(
        backward_kernel,
        in_specs=[anywhere] * 7 + [vmem] * 10,
        out_specs=[anywhere] * 6 + [vmem] + [anywhere] * 3,
        out_shape=[
            shape((rows, width), BF16),
            shape((rows, width), BF16),
            shape((r_size,) + jobs[0], BF16),
            shape((devices, c_per, c_rows, own_ff), BF16),
            shape((devices, c_per, c_rows, 3 * own_cols), BF16),
            shape((2 * (-(-own_cols // c_rows)) * c_rows + shard_rows, width), BF16),
            shape((vec_rows, width), F32),
            shape((tokens, width), BF16),
            shape((tokens, width), BF16),
            shape((tokens, width), BF16),
        ],
        scratch_shapes=[
            pltpu.VMEM((tokens // 2, width), BF16),
            pltpu.VMEM((tokens // 2, width), BF16),
            pltpu.VMEM((tokens if small_plane else 16, width), BF16),
            pltpu.VMEM((rows // 2, width), BF16),
        ]
        + [pltpu.VMEM(j, BF16) for j in jobs]
        + [pltpu.VMEM(j, BF16) for j in jobs]
        + [
            pltpu.VMEM((width, own_ff), BF16),
            pltpu.VMEM((own_ff, width), BF16),
            pltpu.VMEM((16, 128) if small_plane else (width, 3 * own_cols), BF16),
            pltpu.VMEM((own_cols, width), BF16),
            pltpu.VMEM((rows, width), BF16),
            pltpu.VMEM((step, width), BF16),
            pltpu.VMEM((step, width), BF16),
            sums(own_ff, width),
            sums(width, own_ff),
            sums(width, 3 * own_cols),
            pltpu.VMEM((tokens, own_ff), BF16),
            pltpu.VMEM((tokens, own_ff), BF16),
            pltpu.VMEM((tokens, own_cols), BF16),
            pltpu.VMEM((tokens, 3 * own_cols), BF16),
            pltpu.VMEM((tokens, own_cols), F32),
            pltpu.VMEM((tokens, own_cols), F32),
            sums(own_cols, width),
            pltpu.VMEM((vec_rows, width), F32),
            pltpu.VMEM((hops, vec_rows, width), F32),
            pltpu.VMEM((rows, width), BF16),
            pltpu.VMEM((rows, width), BF16),
            pltpu.VMEM((rows, width), BF16),
            dma((5,)),
        ]
        + tree * 4
        + [dma((4,)), dma((2, 2)), dma((hops,)), dma((hops,))]
        + line
        + [
            dma((r_size,)), dma((r_size,)),
            dma((s_size, r_size)), dma((devices,)),
            dma((s_size, r_size)), dma((devices,)),
            dma((2, r_size)), dma((devices,)),
        ],
        compiler_params=pltpu.CompilerParams(
            collective_id=1, has_side_effects=True, vmem_limit_bytes=62 << 20
        ),
        cost_estimate=pl.CostEstimate(
            flops=10 * heads * tokens * tokens * HEAD_DIM + 12 * tokens * width * own_ff,
            bytes_accessed=40 << 20,
            transcendentals=0,
        ),
        name="backward_part",
    )(h2, cot, wf, wp, h1, wq, wo, q, k, v, att, lse, code, middle, x_own, small, fcb)


def results_kernel(
    out_in, ig_in, proj_in, fc_in, qkv_in, wo_in, sums,
    out, ig, g1, b1, qkv, qv, wo, ob, g2, b2, fc, fcb, proj, pb,
):
    devices = fc_in.shape[0]
    own_ff, own_cols = fc_in.shape[3], qkv_in.shape[3] // 3
    width = wo.shape[1]
    proj[...] = proj_in[...].astype(F32)
    wo[...] = wo_in[...].astype(F32)
    fc[...] = jnp.concatenate([fc_in[device, 0] for device in range(devices)], axis=1).astype(F32)
    parts = []
    for part in range(3):
        for device in range(devices):
            n = max(0, min(own_cols, width - device * own_cols))
            if n:
                parts.append(qkv_in[device, 0, :, part * own_cols : part * own_cols + n])
    qkv[...] = jnp.concatenate(parts, axis=1).astype(F32)

    @pl.when(pl.program_id(0) == 0)
    def _():
        out[...] = jnp.transpose(out_in[...])
        ig[...] = jnp.transpose(ig_in[...].astype(F32))
        s = lax.axis_index("s")
        s_size = lax.axis_size("s")
        ff_lanes = -(-own_ff // 128) * 128
        q_lanes = -(-own_cols // 128) * 128
        by_device = devices // s_size

        def heads_of(first):
            return jnp.concatenate(
                [sums[8 + d : 9 + d, first : first + own_cols] for d in range(devices)], axis=1
            )[:, :width]

        qv_all = jnp.concatenate([heads_of(ff_lanes), heads_of(ff_lanes + q_lanes)], axis=1)
        for s2 in range(s_size):

            @pl.when(s == s2)
            def _(s2=s2):
                n = width // s_size
                for i, ref in enumerate((g1, b1, ob, g2, b2, pb)):
                    ref[...] = sums[i, s2 * n : (s2 + 1) * n]
                qv[...] = qv_all[0, 2 * s2 * n : 2 * (s2 + 1) * n]
                fcb[...] = jnp.concatenate(
                    [sums[8 + d : 9 + d, 0:own_ff] for d in range(s2 * by_device, (s2 + 1) * by_device)], axis=1
                )[0]


def results(out_home, ig_home, home_proj, home_fc, home_qkv, home_out, sums):
    devices, c_per, c_rows, own_ff = home_fc.shape
    rows, width = out_home.shape
    shard_rows = c_per * c_rows
    own_cols = home_qkv.shape[3] // 3
    proj = home_proj.reshape(-1, width)
    ff = devices * own_ff
    steps = c_per
    proj_rows = proj.shape[0] // steps
    first = (home_out.shape[0] - shard_rows) // 2 // c_rows
    whole = lambda *dims: pl.BlockSpec(dims, lambda i: (0,) * len(dims))
    by_rows = lambda n, columns: pl.BlockSpec((n, columns), lambda i: (i, 0))
    by_device = lambda columns: pl.BlockSpec((devices, 1, c_rows, columns), lambda i: (0, i, 0, 0))
    shape = lambda *dims: jax.ShapeDtypeStruct(dims, F32)
    vector = whole(shard_rows)
    return pl.pallas_call(
        results_kernel,
        grid=(steps,),
        in_specs=[
            whole(rows, width),
            whole(rows, width),
            by_rows(proj_rows, width),
            by_device(own_ff),
            by_device(3 * own_cols),
            pl.BlockSpec((c_rows, width), lambda i: (first + i, 0)),
            whole(*sums.shape),
        ],
        out_specs=[
            whole(width, rows),
            whole(width, rows),
            vector,
            vector,
            by_rows(c_rows, 3 * width),
            whole(2 * shard_rows),
            by_rows(c_rows, width),
            vector,
            vector,
            vector,
            by_rows(c_rows, ff),
            whole(proj.shape[0]),
            by_rows(proj_rows, width),
            vector,
        ],
        out_shape=[
            jax.ShapeDtypeStruct((width, rows), BF16),
            shape(width, rows),
            shape(shard_rows),
            shape(shard_rows),
            shape(shard_rows, 3 * width),
            shape(2 * shard_rows),
            shape(shard_rows, width),
            shape(shard_rows),
            shape(shard_rows),
            shape(shard_rows),
            shape(shard_rows, ff),
            shape(proj.shape[0]),
            shape(*proj.shape),
            shape(shard_rows),
        ],
        compiler_params=pltpu.CompilerParams(vmem_limit_bytes=61 << 20),
        name="results",
    )(out_home, ig_home, proj, home_fc, home_qkv, home_out, sums)


def local(
    inputs,
    positions,
    segments,
    cotangent,
    ln1_gain,
    ln1_bias,
    w_qkv,
    qv_bias,
    w_out,
    out_bias,
    ln2_gain,
    ln2_bias,
    w_fc,
    fc_bias,
    w_proj,
    proj_bias,
):
    rows = inputs.shape[0]
    code = jnp.broadcast_to(segments * SEG_STEP + positions // BLOCK, (8, rows))
    vectors = (ln1_gain, ln1_bias, out_bias, ln2_gain, ln2_bias, proj_bias, qv_bias, fc_bias)

    (
        hidden_one, hidden_two, cot, own_fc, own_qkv, own_out, queries, keys, values, attended, lse, code_all,
        middle, x_own, small, own_fcb,
    ) = forward_part(inputs.T, cotangent.T, code, vectors, w_qkv, w_fc, w_out)
    found = backward_part(
        hidden_two, cot, own_fc, w_proj, hidden_one, own_qkv, own_out, queries, keys, values, attended, lse, code_all,
        middle, x_own, small, own_fcb,
    )
    out, input_grad, *grads = results(*found[:7])
    return (out.T, input_grad.T, *grads)


def solution(mesh):
    ctx, shard = mesh.devices.shape
    fine = Mesh(mesh.devices.reshape(shard, ctx // shard, shard), ("z", "r", "s"))
    tokens = ("s", "z", "r")
    arg_specs = (
        P(tokens, None),
        P(tokens),
        P(tokens),
        P(tokens, None),
        P("s"),
        P("s"),
        P("s", None),
        P("s"),
        P("s", None),
        P("s"),
        P("s"),
        P("s"),
        P("s", None),
        P("s"),
        P("s", None),
        P("s"),
    )
    out_specs = (P(tokens, None), P(tokens, None)) + arg_specs[4:]
    return jax.shard_map(local, mesh=fine, in_specs=arg_specs, out_specs=out_specs, check_vma=False)
```

```python
import math

import jax
import jax.numpy as jnp
from jax import lax
from jax.experimental import pallas as pl
from jax.experimental.pallas import tpu as pltpu
from jax.sharding import Mesh, PartitionSpec as P

HEAD_DIM = 64
BLOCK = 256
EPSILON = 1e-05
NEGATIVE = -1e30
SEG_STEP = 65536
BF16 = jnp.bfloat16
F32 = jnp.float32


def bits_of(size):
    return [1 << i for i in range(size.bit_length() - 1)]


def norm_parts(values):
    centre = jnp.mean(values, axis=-1, keepdims=True)
    centred = values - centre
    spread = jnp.mean(centred * centred, axis=-1, keepdims=True)
    inverse = lax.rsqrt(spread + EPSILON)
    return centred * inverse, inverse


def gelu_parts(u):
    c = math.sqrt(2.0 / math.pi)
    squared = u * u
    t = jnp.tanh(c * (u + 0.044715 * (u * squared)))
    half = 0.5 * (1.0 + t)
    slope = half + 0.5 * u * (1.0 - t * t) * (c * (1.0 + 3.0 * 0.044715 * squared))
    return u * half, slope


def dot(a, b, contract=((1,), (0,))):
    return lax.dot_general(a, b, (contract, ((), ())), preferred_element_type=F32)


ACROSS_TOKENS = ((0,), (0,))
ON_LAST = ((1,), (1,))


MESH_ID = pl.DeviceIdType.MESH


def remote(src, dst, send_sem, recv_sem, **device):
    return pltpu.make_async_remote_copy(
        src_ref=src,
        dst_ref=dst,
        send_sem=send_sem,
        recv_sem=recv_sem,
        device_id=device,
        device_id_type=MESH_ID,
    )


def partner(axis, bit):
    return {axis: lax.axis_index(axis) ^ bit}


def plane_device(offset, r_size):
    found = {}
    if offset // r_size:
        found["s"] = lax.axis_index("s") ^ (offset // r_size)
    if offset % r_size:
        found["r"] = lax.axis_index("r") ^ (offset % r_size)
    return found


def tree_of(order, r_size):
    levels = []
    known = [(0, 0)]
    for axis, bit in order:
        step = bit * r_size if axis == "s" else bit
        known = known + [(o ^ step, depth + 1) for o, depth in known]
    found = {}
    for o, depth in known:
        if o == 0:
            continue
        for axis, bit in order[::-1]:
            step = bit * r_size if axis == "s" else bit
            if o & step:
                found.setdefault(depth, []).append((o, o ^ step, axis, bit))
                break
    for depth in sorted(found):
        levels.append(found[depth])
    return levels


def chip_orders(r_size):
    chips = [("s", 2)] + [("r", bit) for bit in bits_of(r_size)]
    return [chips + [("s", 1)], chips[::-1] + [("s", 1)]]


class Gather:
    def __init__(self, block, send_sem, recv_sem, r_size, parts=2, own=None):
        self.block = block
        self.own = own or block
        self.send_sem = send_sem
        self.recv_sem = recv_sem
        self.levels = [tree_of(order, r_size) for order in chip_orders(r_size)[:parts]]
        self.parts = parts
        self.arrived = set()

    def copy(self, part, transfer):
        offset, source, axis, bit = transfer
        src = self.own(0, part) if source == 0 else self.block(source, part)
        return remote(
            src,
            self.block(offset, part),
            self.send_sem.at[part, offset],
            self.recv_sem.at[part, offset],
            **partner(axis, bit),
        )

    def transfers(self):
        for level in range(len(self.levels[0])):
            for i in range(len(self.levels[0][level])):
                for part in range(self.parts):
                    yield level, part, self.levels[part][level][i]

    def find(self, part, offset):
        for _, p, t in self.transfers():
            if p == part and t[0] == offset:
                return t

    def need(self, part, offset):
        if offset and (part, offset) not in self.arrived:
            self.arrived.add((part, offset))
            self.copy(part, self.find(part, offset)).wait_recv()

    def start(self, level):
        for lv, part, t in self.transfers():
            if lv == level:
                self.need(part, t[1])
                self.copy(part, t).start()

    def start_rest(self):
        for level in range(1, len(self.levels[0])):
            self.start(level)

    def need_all(self):
        for _, part, t in self.transfers():
            self.need(part, t[0])

    def close(self):
        self.need_all()
        for _, part, t in self.transfers():
            self.copy(part, t).wait_send()


def attention_rows(rows, first, q_ref, k_ref, v_ref, code_q, code_k):
    heads = q_ref.shape[1] // HEAD_DIM
    low_q = (code_q // SEG_STEP) * SEG_STEP
    allowed = jnp.logical_and(code_k >= low_q, code_k <= code_q)
    outs = []
    sums = []
    for h in range(heads):
        cols = slice(h * HEAD_DIM, (h + 1) * HEAD_DIM)
        scores = lax.dot_general(
            q_ref[pl.ds(first, rows), cols],
            k_ref[:, cols],
            (((1,), (1,)), ((), ())),
            preferred_element_type=F32,
        )
        scores = jnp.where(allowed, scores, NEGATIVE)
        top = jnp.max(scores, axis=-1, keepdims=True)
        unnorm = jnp.exp(scores - top)
        total = jnp.sum(unnorm, axis=-1, keepdims=True)
        mixed = jnp.dot(unnorm.astype(BF16), v_ref[:, cols], preferred_element_type=F32)
        outs.append((mixed / total).astype(BF16))
        sums.append(top + jnp.log(total))
    return jnp.concatenate(outs, axis=1), jnp.concatenate(sums, axis=1)


def split_rows(n):
    first = -(-n // 32) * 16
    return ((0, first), (first, n - first))


class WeightPush:
    def __init__(self, source, dest, rows, send_sem, recv_sem, across):
        self.source, self.dest, self.rows = source, dest, rows
        self.send_sem, self.recv_sem = send_sem, recv_sem
        self.across = across

    def core_copy(self):
        s = lax.axis_index("s")
        return remote(
            self.source(s ^ 1),
            self.dest(s, 0, self.rows),
            self.send_sem.at[0],
            self.recv_sem.at[0],
            s=s ^ 1,
        )

    def chip_copy(self, m, part, landed=None):
        s = lax.axis_index("s")
        first, count = split_rows(self.rows)[part]
        return remote(
            self.source(s ^ m).at[pl.ds(first, count)],
            self.dest(s, first, count),
            self.send_sem.at[m],
            self.recv_sem.at[m],
            s=s ^ m,
        )

    def relay_copy(self, m, part):
        s = lax.axis_index("s")
        first, count = split_rows(self.rows)[part]
        ref = self.dest(s ^ m, first, count)
        return remote(
            ref, ref, self.send_sem.at[2 + m], self.recv_sem.at[2 + m], z=lax.axis_index("z") ^ 1
        )

    def per_part(self, act):
        odd = lax.axis_index("z") % 2
        for part in range(2):

            @pl.when(odd == part)
            def _(part=part):
                act(part)

    def start(self):
        if 1 in self.across:
            self.core_copy().start()

        def act(part):
            for m in self.across:
                if m != 1:
                    self.chip_copy(m, part).start()

        self.per_part(act)

    def relay(self):
        def act(part):
            for m in self.across:
                if m != 1:
                    self.chip_copy(m, part).wait_recv()
                    self.relay_copy(m, part).start()

        self.per_part(act)

    def need(self):
        if 1 in self.across:
            self.core_copy().wait_recv()

        def act(part):
            for m in self.across:
                if m != 1:
                    self.relay_copy(m, 1 - part).wait_recv()

        self.per_part(act)

    def close(self):
        if 1 in self.across:
            self.core_copy().wait_send()

        def act(part):
            for m in self.across:
                if m != 1:
                    self.chip_copy(m, part).wait_send()
                    self.relay_copy(m, part).wait_send()

        self.per_part(act)


def forward_kernel(
    x_in, cot_in, code_in, g1_in, b1_in, ob_in, g2_in, b2_in, pb_in, qv_in, fcb_in, wq_in, wf_in, wo_in,
    h1_out, h2_out, cot_out, wf_out, wq_out, wo_out, q_ref, k_ref, v_ref, att_ref, lse_ref, code_out,
    middle_out, x_own, small_ref, fcb_out,
    xt_vm, ct_vm, x_vm, cot_vm, vec_in, code_land, vec_land, bias_ref, h1, wq_vm, stage_q, wf_vm, stage_f, own_q, full_out, att_land, h2_own,
    x_sem, code_sem, cot_sem, small_sem, load_sem, h1_send, h1_recv, cd_send, cd_recv, ct_send, ct_recv, h2_send,
    h2_recv, wq_send, wq_recv, wf_send, wf_recv, wo_send, wo_recv, at_send, at_recv, out_sem,
):
    s, r, z = (lax.axis_index(a) for a in ("s", "r", "z"))
    s_size, r_size = lax.axis_size("s"), lax.axis_size("r")
    devices = s_size * r_size
    me = s * r_size + r
    width, rows = x_in.shape
    tokens = rows * devices
    own_cols = q_ref.shape[1]
    own_ff = wf_out.shape[1]
    shard_rows = wq_in.shape[0]

    def shard_at(i, first=0, count=shard_rows):
        return pl.ds(pl.multiple_of(i * shard_rows + first, 16), count)

    x_loads = [
        pltpu.make_async_copy(x_in, xt_vm, load_sem.at[3]),
        pltpu.make_async_copy(cot_in, ct_vm, load_sem.at[4]),
    ]
    for load in x_loads:
        load.start()

    barrier = pltpu.get_barrier_semaphore()
    for offset in range(1, devices):
        pl.semaphore_signal(barrier, inc=1, device_id=plane_device(offset, r_size), device_id_type=MESH_ID)
    pl.semaphore_signal(barrier, inc=1, device_id={"z": z ^ 1}, device_id_type=MESH_ID)

    @pl.when(s != z)
    def _():
        pl.semaphore_signal(barrier, inc=1, device_id={"z": s, "s": z}, device_id_type=MESH_ID)

    at = 0
    for ref in (g1_in, b1_in, ob_in, g2_in, b2_in, pb_in, qv_in, fcb_in):
        vec_in[0:1, at : at + ref.shape[0]] = ref[...].astype(F32).reshape(1, ref.shape[0])
        at += ref.shape[0]
    for load, src, dst in zip(x_loads, (xt_vm, ct_vm), (x_vm, cot_vm)):
        load.wait()
        dst[...] = jnp.transpose(src[...])
    pl.semaphore_wait(barrier, devices + jnp.where(s != z, 1, 0))

    def moved(src, dst, sem):
        far = remote(src, dst, sem.at[0], sem.at[1], z=s, s=z)
        near = pltpu.make_async_copy(src, dst, sem.at[1])

        @pl.when(s != z)
        def _():
            far.start()

        @pl.when(s == z)
        def _():
            near.start()

        def arrived():
            @pl.when(s != z)
            def _():
                far.wait_recv()

            @pl.when(s == z)
            def _():
                near.wait()

        def sent():
            @pl.when(s != z)
            def _():
                far.wait_send()

        return arrived, sent

    x_arrived, x_sent = moved(x_vm, x_own, x_sem)
    code_arrived, code_sent = moved(code_in, code_land.at[0], code_sem)
    loads = [
        pltpu.make_async_copy(wq_in, wq_vm, load_sem.at[0]),
        pltpu.make_async_copy(wf_in, wf_vm, load_sem.at[1]),
        pltpu.make_async_copy(wo_in, full_out.at[shard_at(s)], load_sem.at[2]),
    ]
    for load in loads:
        load.start()
    small_copies = [
        remote(vec_in, vec_land.at[s], small_sem.at[0, m], small_sem.at[1, m], s=s ^ m) for m in range(1, s_size)
    ]
    for copy in small_copies:
        copy.start()
    vec_land[s] = vec_in[...]
    if full_out.shape[0] > width:
        full_out[width:, :] = jnp.zeros((full_out.shape[0] - width, width), BF16)

    loads[0].wait()
    for s2 in range(s_size):
        for r2 in range(r_size):

            @pl.when(r == r2)
            def _(s2=s2, r2=r2):
                device = s2 * r_size + r2
                for part in range(3):
                    lo = device * own_cols
                    n = max(0, min(own_cols, width - lo))
                    if n:
                        stage_q[s2, :, part * own_cols : part * own_cols + n] = wq_vm[
                            :, part * width + lo : part * width + lo + n
                        ]
                    if n < own_cols:
                        stage_q[s2, :, part * own_cols + n : (part + 1) * own_cols] = jnp.zeros(
                            (shard_rows, own_cols - n), BF16
                        )

    push_q = WeightPush(
        lambda i: stage_q.at[i],
        lambda i, first, count: own_q.at[shard_at(i, first, count)],
        shard_rows, wq_send, wq_recv, (1, 2, 3),
    )
    push_q.start()
    own_q[shard_at(s), :] = stage_q[s]

    for copy in small_copies:
        copy.wait_recv()
    per = shard_rows
    small_ref[...] = jnp.zeros_like(small_ref)
    for s2 in range(s_size):
        for i in range(6):
            small_ref[i : i + 1, s2 * per : (s2 + 1) * per] = vec_land[s2, :, i * per : (i + 1) * per]
    for part in range(2):
        q_or_v = jnp.concatenate(
            [vec_land[part * s_size // 2 + i, :, 6 * per : 8 * per] for i in range(s_size // 2)], axis=1
        )
        for device in range(devices):
            n = max(0, min(own_cols, width - device * own_cols))
            if n:
                bias_ref[part, device : device + 1, 0:n] = q_or_v[:, device * own_cols : device * own_cols + n]
            if n < own_cols:
                bias_ref[part, device : device + 1, n:] = jnp.zeros((1, own_cols - n), F32)
    for r2 in range(r_size):

        @pl.when(r == r2)
        def _(r2=r2):
            fcb_out[...] = vec_in[:, 8 * per + r2 * own_ff : 8 * per + (r2 + 1) * own_ff]

    gain_one, bias_one, out_bias, gain_two, bias_two = (small_ref[i : i + 1, :] for i in range(5))
    x_arrived()
    resid = x_own[...].astype(F32)
    normed, _ = norm_parts(resid)
    h1[0:rows, :] = (normed * gain_one + bias_one).astype(BF16)
    half = rows // 2

    def block_of(ref):
        return lambda offset, part: ref.at[pl.ds(offset * rows + part * half, half)]

    gather_one = Gather(block_of(h1), h1_send, h1_recv, r_size)
    gather_one.start(0)
    code_arrived()
    gather_code = Gather(lambda offset, part: code_land.at[offset], cd_send, cd_recv, r_size, parts=1)
    gather_code.start(0)

    loads[1].wait()
    for s2 in range(s_size):
        for r2 in range(r_size):

            @pl.when(r == r2)
            def _(s2=s2, r2=r2):
                lo = (s2 * r_size + r2) * own_ff
                stage_f[s2] = wf_vm[:, lo : lo + own_ff]

    gather_one.start(1)
    gather_code.start(1)
    push_q.relay()
    for level in range(2, len(gather_one.levels[0])):
        gather_one.start(level)
        gather_code.start(level)

    push_o = WeightPush(
        lambda i: full_out.at[shard_at(s)],
        lambda i, first, count: full_out.at[shard_at(i, first, count)],
        shard_rows, wo_send, wo_recv, (1, 2),
    )
    push_f = WeightPush(
        lambda i: stage_f.at[i],
        lambda i, first, count: wf_out.at[shard_at(i, first, count)],
        shard_rows, wf_send, wf_recv, (1, 2, 3),
    )
    own_f = pltpu.make_async_copy(
        stage_f.at[s], wf_out.at[shard_at(s)], load_sem.at[1]
    )
    own_f.start()
    gather_one.need_all()
    cot_arrived, cot_sent = moved(cot_vm, cot_out.at[pl.ds(0, rows)], cot_sem)
    loads[2].wait()
    push_o.start()
    push_f.start()

    push_q.need()
    save_q = pltpu.make_async_copy(own_q, wq_out, out_sem.at[0])
    save_q.start()
    save_h = pltpu.make_async_copy(h1, h1_out, out_sem.at[1])
    save_h.start()
    q_bias = bias_ref[0, pl.ds(me, 1), :]
    v_bias = bias_ref[1, pl.ds(me, 1), :]
    step = min(512, tokens)
    score_scale = jnp.asarray(1.0 / math.sqrt(HEAD_DIM), BF16)

    def project(i, carry):
        at = pl.ds(pl.multiple_of(i * step, step), step)
        packed = jnp.dot(h1[at, :], own_q[...], preferred_element_type=F32)
        q_ref[at, :] = (packed[:, :own_cols] + q_bias).astype(BF16) * score_scale
        k_ref[at, :] = packed[:, own_cols : 2 * own_cols].astype(BF16)
        v_ref[at, :] = (packed[:, 2 * own_cols :] + v_bias).astype(BF16)
        return carry

    lax.fori_loop(0, tokens // step, project, 0)
    gather_code.need_all()
    code_out[...] = code_land[:, 0, :]
    code_row = jnp.concatenate([code_land[i, 0:1, :] for i in range(devices)], axis=1)

    q_rows = min(rows if tokens > 2048 else 256, tokens)

    def attend(i, carry):
        first = pl.multiple_of(i * q_rows, q_rows)
        per = q_rows // rows
        code_col = jnp.concatenate(
            [jnp.transpose(code_land[i * per + j])[:, 0:1] for j in range(per)], axis=0
        )
        out, sums = attention_rows(q_rows, first, q_ref, k_ref, v_ref, code_col, code_row)
        att_ref[pl.ds(first, q_rows), :] = out
        lse_ref[pl.ds(first, q_rows), :] = sums
        return carry

    lax.fori_loop(0, tokens // q_rows, attend, 0)

    at_copies = []
    for offset in range(1, devices):
        at_copies.append(
            remote(
                att_ref.at[pl.ds(offset * rows, rows)],
                att_land.at[me],
                at_send.at[offset],
                at_recv.at[offset],
                **plane_device(offset, r_size),
            )
        )
    for copy in at_copies:
        copy.start()
    att_land[me] = att_ref[0:rows, :]
    cot_arrived()
    gather_cot = Gather(block_of(cot_out), ct_send, ct_recv, r_size)
    gather_cot.start(0)
    push_o.relay()
    push_o.need()
    far = full_out.at[shard_at(s ^ 2)]
    out_core = remote(far, far, wo_send.at[5], wo_recv.at[5], s=s ^ 1)
    out_core.start()
    gather_cot.start(1)
    for copy in at_copies:
        copy.wait_recv()
    out_core.wait_recv()
    middle = resid + out_bias
    for device in range(devices):
        middle = middle + jnp.dot(
            att_land[device],
            full_out[device * own_cols : (device + 1) * own_cols, :],
            preferred_element_type=F32,
        )
    middle_out[...] = middle
    normed, _ = norm_parts(middle)
    h2_own[...] = (normed * gain_two + bias_two).astype(BF16)
    save_h2 = pltpu.make_async_copy(h2_own, h2_out.at[pl.ds(0, rows)], out_sem.at[2])
    save_h2.start()
    gather_two = Gather(
        block_of(h2_out), h2_send, h2_recv, r_size, own=lambda o, part: h2_own.at[pl.ds(part * half, half)]
    )
    gather_two.start(0)
    save_o = pltpu.make_async_copy(
        full_out.at[pl.ds(pl.multiple_of(me * own_cols, own_cols), own_cols)], wo_out, out_sem.at[3]
    )
    save_o.start()
    for level in range(2, len(gather_cot.levels[0])):
        gather_cot.start(level)
    push_f.relay()
    gather_two.start_rest()
    gather_two.close()
    gather_cot.close()
    gather_one.close()
    gather_code.close()
    push_f.need()
    for push in (push_q, push_o, push_f):
        push.close()
    out_core.wait_send()
    for copy in at_copies + small_copies:
        copy.wait_send()
    x_sent()
    code_sent()
    cot_sent()
    own_f.wait()
    for save in (save_q, save_h, save_h2, save_o):
        save.wait()


def forward_part(x, cot, code, small, w_qkv, w_fc, w_out):
    s_size, r_size = lax.axis_size("s"), lax.axis_size("r")
    devices = s_size * r_size
    width, rows = x.shape
    tokens = rows * devices
    shard_rows = w_qkv.shape[0]
    heads = width // HEAD_DIM
    own_heads = -(-heads // devices)
    own_cols = own_heads * HEAD_DIM
    own_ff = w_fc.shape[1] // devices
    anywhere = pl.BlockSpec(memory_space=pl.ANY)
    vmem = pl.BlockSpec(memory_space=pltpu.VMEM)
    shape = jax.ShapeDtypeStruct
    dma = pltpu.SemaphoreType.DMA
    flops = 2 * tokens * width * 3 * own_cols + 4 * own_heads * tokens * tokens * HEAD_DIM
    return pl.pallas_call(
        forward_kernel,
        in_specs=[anywhere] * 3 + [vmem] * 8 + [anywhere] * 3,
        out_specs=[anywhere] * 6 + [vmem] * 10,
        out_shape=[
            shape((tokens, width), BF16),
            shape((tokens, width), BF16),
            shape((tokens, width), BF16),
            shape((width, own_ff), BF16),
            shape((width, 3 * own_cols), BF16),
            shape((own_cols, width), BF16),
            shape((tokens, own_cols), BF16),
            shape((tokens, own_cols), BF16),
            shape((tokens, own_cols), BF16),
            shape((tokens, own_cols), BF16),
            shape((tokens, own_heads), F32),
            shape((devices, rows), jnp.int32),
            shape((rows, width), F32),
            shape((rows, width), BF16),
            shape((8, width), F32),
            shape((1, own_ff), F32),
        ],
        scratch_shapes=[
            pltpu.VMEM((width, rows), BF16),
            pltpu.VMEM((width, rows), BF16),
            pltpu.VMEM((rows, width), BF16),
            pltpu.VMEM((rows, width), BF16),
            pltpu.VMEM((1, sum(a.shape[0] for a in small)), F32),
            pltpu.VMEM((devices, 8, rows), jnp.int32),
            pltpu.VMEM((s_size, 1, sum(a.shape[0] for a in small)), F32),
            pltpu.VMEM((2, devices, own_cols), F32),
            pltpu.VMEM((tokens, width), BF16),
            pltpu.VMEM(w_qkv.shape, BF16),
            pltpu.VMEM((s_size, shard_rows, 3 * own_cols), BF16),
            pltpu.VMEM(w_fc.shape, BF16),
            pltpu.VMEM((s_size, shard_rows, own_ff), BF16),
            pltpu.VMEM((width, 3 * own_cols), BF16),
            pltpu.VMEM((devices * own_cols, width), BF16),
            pltpu.VMEM((devices, rows, own_cols), BF16),
            pltpu.VMEM((rows, width), BF16),
            dma((2,)), dma((2,)), dma((2,)), dma((2, s_size)), dma((5,)),
            dma((2, devices)), dma((2, devices)), dma((1, devices)), dma((1, devices)),
            dma((2, devices)), dma((2, devices)), dma((2, devices)), dma((2, devices)),
            dma((6,)), dma((6,)), dma((6,)), dma((6,)), dma((6,)), dma((6,)),
            dma((devices,)), dma((devices,)), dma((4,)),
        ],
        compiler_params=pltpu.CompilerParams(
            collective_id=0, has_side_effects=True, vmem_limit_bytes=60 << 20
        ),
        cost_estimate=pl.CostEstimate(flops=flops, bytes_accessed=40 << 20, transcendentals=0),
        name="forward_part",
    )(x, cot, code, *small, w_qkv, w_fc, w_out)


class Scatter:
    def __init__(self, leaf, acc, land, load, send_sem, recv_sem, r_size):
        self.leaf, self.acc, self.land, self.load = leaf, acc, land, load
        self.send_sem, self.recv_sem = send_sem, recv_sem
        self.levels = [tree_of(order, r_size) for order in chip_orders(r_size)]

    def copy(self, part, transfer):
        offset, _, axis, bit = transfer
        src = self.acc(offset, part) if self.children(part, offset) else self.leaf(offset, part)
        return remote(
            src,
            self.land(offset, part),
            self.send_sem.at[part, offset],
            self.recv_sem.at[part, offset],
            **partner(axis, bit),
        )

    def children(self, part, offset):
        return [t for level in self.levels[part] for t in level if t[1] == offset]

    def start_leaves(self):
        for level in range(len(self.levels[0]) - 1, -1, -1):
            for i in range(len(self.levels[0][level])):
                for part in range(2):
                    t = self.levels[part][level][i]
                    if not self.children(part, t[0]):
                        self.copy(part, t).start()

    def total(self, part, offset):
        value = self.acc(offset, part)[...].astype(F32)
        for t in self.children(part, offset)[::-1]:
            self.copy(part, t).wait_recv()
            value = value + self.load(t[0], part).astype(F32)
        return value

    def start_inner(self):
        for level in range(len(self.levels[0]) - 1, -1, -1):
            for i in range(len(self.levels[0][level])):
                for part in range(2):
                    t = self.levels[part][level][i]
                    if self.children(part, t[0]):
                        self.acc(t[0], part)[...] = self.total(part, t[0]).astype(BF16)
                        self.copy(part, t).start()

    def finish(self):
        return jnp.concatenate([self.total(part, 0) for part in range(2)], axis=0)

    def close(self):
        for part in range(2):
            for level in self.levels[part]:
                for t in level:
                    self.copy(part, t).wait_send()


class LineSum:
    def __init__(self, jobs, land, rs_send, rs_recv, ag_send, ag_recv, home, start, lag):
        self.jobs, self.land = jobs, land
        self.rs_send, self.rs_recv, self.ag_send, self.ag_recv = rs_send, rs_recv, ag_send, ag_recv
        self.home = home
        self.n = jobs.shape[1]
        self.z = lax.axis_index("z")
        self.last = lax.axis_size("z") - 1
        self.start = start
        self.lag = lag
        self.end = start + self.n + 2 * lag * self.last

    def place(self, d):
        return self.z if d == 0 else self.last - self.z

    def up(self, d, j):
        return remote(
            self.jobs.at[d, j], self.land.at[d, j], self.rs_send.at[d, j], self.rs_recv.at[d, j], z=self.z + 1 - 2 * d
        )

    def down(self, d, j):
        return remote(
            self.land.at[d, j], self.land.at[d, j], self.ag_send.at[d, j], self.ag_recv.at[d, j], z=self.z - 1 + 2 * d
        )

    def add(self, d, j):
        place = self.place(d)

        @pl.when(place > 0)
        def _():
            self.up(d, j).wait_recv()
            total = (self.jobs[d, j].astype(F32) + self.land[d, j].astype(F32)).astype(BF16)

            @pl.when(place < self.last)
            def _():
                self.jobs[d, j] = total

            @pl.when(place == self.last)
            def _():
                self.land[d, j] = total

        @pl.when(place < self.last)
        def _():
            self.up(d, j).start()

        @pl.when(place == self.last)
        def _():
            self.down(d, j).start()
            self.home(d, j)

    def back(self, d, j):
        place = self.place(d)
        self.down(d, j).wait_recv()

        @pl.when(place > 0)
        def _():
            self.down(d, j).start()

        self.home(d, j)

    def tick(self, k):
        for d in range(2):
            j = k - self.start - self.lag * self.place(d)

            @pl.when(jnp.logical_and(j >= 0, j < self.n))
            def _(d=d, j=j):
                self.add(d, j)

        for d in range(2):
            place = self.place(d)
            j = k - self.start - self.lag * (2 * self.last - place)

            @pl.when(jnp.logical_and(place < self.last, jnp.logical_and(j >= 0, j < self.n)))
            def _(d=d, j=j):
                self.back(d, j)

    def close(self):
        def one(j, carry):
            for d in range(2):
                place = self.place(d)

                @pl.when(place < self.last)
                def _(d=d):
                    self.up(d, j).wait_send()

                @pl.when(place > 0)
                def _(d=d):
                    self.down(d, j).wait_send()

            return carry

        lax.fori_loop(0, self.n, one, 0)


class Clock:
    def __init__(self, sums):
        self.sums = sums
        self.now = 0
        self.end = max(one.end for one in sums)

    def ticks(self, first, lo, hi):
        for one in self.sums:
            if one.start < hi and one.end > lo:
                one.tick(first)

    def run(self, count):
        lo, hi = self.now, min(self.now + count, self.end)
        self.now = hi
        if hi - lo == 1:
            self.ticks(lo, lo, hi)
        elif hi > lo:

            def step(k, carry):
                self.ticks(k, lo, hi)
                return carry

            lax.fori_loop(lo, hi, step, 0)

    def loop(self, count, per, body):
        lo, hi = self.now, min(self.now + count * per, self.end)
        self.now = hi

        def step(i, carry):
            body(i)
            for j in range(per):
                self.ticks(lo + i * per + j, lo, lo + count * per)
            return carry

        lax.fori_loop(0, count, step, 0)


def product_rows(lhs, rhs, write):
    for lo in range(0, lhs.shape[1], 256):
        hi = min(lhs.shape[1], lo + 256)
        value = lax.dot_general(
            lhs[:, lo:hi], rhs[...], (((0,), (0,)), ((), ())), preferred_element_type=F32
        )
        write(lo, hi, value)


def into_jobs(jobs):
    n, size = jobs.shape[1:3]

    def write(lo, hi, value):
        value = value.astype(BF16)
        for job in range(lo // size, -(-hi // size)):
            a, b = max(lo, job * size), min(hi, (job + 1) * size)
            jobs[job // n, job % n, a - job * size : b - job * size, :] = value[a - lo : b - lo, :]

    return write


def into_sum(acc):
    def write(lo, hi, value):
        acc[lo:hi, :] += value

    return write


def job_rows(n, most=80):
    for rows in range(most, 15, -16):
        if n % rows == 0:
            return rows
    return n


def norm_backward_rows(grad, normed, inverse, gain):
    scaled = grad * gain
    mean_scaled = jnp.mean(scaled, axis=-1, keepdims=True)
    mean_product = jnp.mean(scaled * normed, axis=-1, keepdims=True)
    grad_in = inverse * (scaled - mean_scaled - normed * mean_product)
    return (
        grad_in,
        jnp.sum(grad * normed, axis=0, keepdims=True),
        jnp.sum(grad, axis=0, keepdims=True),
    )


TICKS = (1, 1, 1, 1, 1, 1, 1, 1, 1, 1, 2, 1)
LAG = 1


def backward_kernel(
    h2, cot_in, wf, wp, h1, wq, wo, q_ref, k_ref, v_ref, att_ref, lse_ref, code_ref, middle_ref, x_ref,
    small_ref, fcb_ref,
    out_home, ig_home, home_proj, home_fc, home_qkv, home_out, small_out, landp, land_far, gb,
    acc, leaf, land_near, tmp, jp, jf, jq, jo, lp, lf, lq, lo_, own_f, own_p, own_q, own_o, cot_v, chunk, chunk2,
    gp_acc, gf_acc, gq_acc, act, gpre, do_ref, gp, dk_acc, dv_acc, go_acc, vec, vec_land, gb_own, out_v, ig_v,
    load_sem, s2_send, s2_recv, sp_send, sp_recv, s1_send, s1_recv, g_send, g_recv, tmp_sem, mv_sem,
    vec_send, vec_recv,
    p_rs, p_rr, p_as, p_ar, f_rs, f_rr, f_as, f_ar, q_rs, q_rr, q_as, q_ar, o_rs, o_rr, o_as, o_ar,
    ph_send, ph_recv, fh_send, fh_recv, qh_send, qh_recv, oh_send, oh_recv,
):
    s, r, z = (lax.axis_index(a) for a in ("s", "r", "z"))
    s_size, r_size, z_size = (lax.axis_size(a) for a in ("s", "r", "z"))
    devices = s_size * r_size
    me = s * r_size + r
    rows, width = x_ref.shape
    tokens = rows * devices
    half = rows // 2
    own_cols = q_ref.shape[1]
    own_ff = wf.shape[1]
    heads = own_cols // HEAD_DIM
    shard_rows = width // s_size
    step = chunk.shape[0]
    contract_last = (((1,), (1,)), ((), ()))
    contract_first = (((0,), (0,)), ((), ()))

    barrier = pltpu.get_barrier_semaphore()
    for offset in range(1, devices):
        pl.semaphore_signal(barrier, inc=1, device_id=plane_device(offset, r_size), device_id_type=MESH_ID)
    for bit in bits_of(z_size):
        pl.semaphore_signal(barrier, inc=1, device_id={"z": z ^ bit}, device_id_type=MESH_ID)
    inner = jnp.logical_and(z > 0, z < z_size - 1)

    @pl.when(s != z)
    def _():
        pl.semaphore_signal(barrier, inc=1, device_id={"z": s, "s": z}, device_id_type=MESH_ID)

    @pl.when(inner)
    def _():
        pl.semaphore_signal(
            barrier, inc=1, device_id={"z": jnp.where(z % 2 == 1, z + 1, z - 1)}, device_id_type=MESH_ID
        )

    loads = [
        pltpu.make_async_copy(src, dst, load_sem.at[i])
        for i, (src, dst) in enumerate(
            (
                (wf, own_f),
                (wp.at[pl.ds(pl.multiple_of(r * own_ff, 8), own_ff)], own_p),
                (wo, own_o),
                (cot_in.at[pl.ds(0, rows)], cot_v),
            )
        )
    ]
    for load in loads:
        load.start()
    early = []
    if tokens == step:
        early = [
            pltpu.make_async_copy(h2, chunk, tmp_sem.at[2]),
            pltpu.make_async_copy(cot_in, chunk2, tmp_sem.at[3]),
        ]
        for load in early:
            load.start()
    if own_q.shape[0] != width:
        own_q = own_f.at[:, : 3 * own_cols]
    load_q = pltpu.make_async_copy(wq, own_q, load_sem.at[4])

    loads[0].wait()
    loads[1].wait()
    chunks = tokens // step
    if chunks > 1:
        gp_acc[...] = jnp.zeros_like(gp_acc)
        gf_acc[...] = jnp.zeros_like(gf_acc)
        gq_acc[...] = jnp.zeros_like(gq_acc)

    def fetch(src, at, dst, i):
        copy = pltpu.make_async_copy(src.at[at], dst, tmp_sem.at[i])
        copy.start()
        return copy

    piece = min(256, step)

    def feed_forward(i, carry):
        at = pl.ds(pl.multiple_of(i * step, step), step)
        first, second = early or (fetch(h2, at, chunk, 2), fetch(cot_in, at, chunk2, 3))
        first.wait()
        second.wait()

        def one(j, inner_carry):
            here = pl.ds(pl.multiple_of(j * piece, piece), piece)
            there = pl.ds(pl.multiple_of(i * step + j * piece, piece), piece)
            pre = jnp.dot(chunk[here, :], own_f[...], preferred_element_type=F32) + fcb_ref[...]
            value, slope = gelu_parts(pre)
            act[there, :] = value.astype(BF16)
            back = lax.dot_general(chunk2[here, :], own_p[...], contract_last, preferred_element_type=F32)
            gpre[there, :] = (back * slope).astype(BF16)
            return inner_carry

        lax.fori_loop(0, step // piece, one, 0)
        product_rows(act.at[at], chunk2, into_jobs(jp) if chunks == 1 else into_sum(gp_acc))
        if chunks > 1:
            product_rows(chunk, gpre.at[at], into_sum(gf_acc))
        return carry

    if chunks == 1:
        feed_forward(0, 0)
    else:
        lax.fori_loop(0, chunks, feed_forward, 0)
        into_jobs(jp)(0, own_ff, gp_acc[...])
        into_jobs(jf)(0, width, gf_acc[...])

    peers = devices - 1 + len(bits_of(z_size))
    pl.semaphore_wait(barrier, peers + jnp.where(s != z, 1, 0) + jnp.where(inner, 1, 0))

    def to_home(src, dst, send, recv, s_to, m):
        far = remote(src, dst, send, recv, s=s_to, r=r ^ m)
        if m:
            far.start()
        else:
            near = pltpu.make_async_copy(src, dst, recv)

            @pl.when(s_to == s)
            def _():
                near.start()

            @pl.when(s_to != s)
            def _():
                far.start()

    def home_of_proj(d, j):
        for m in range(r_size):
            src, dst = lp.at[d, j], home_proj.at[r, d, j]
            if m:
                remote(src, dst, ph_send.at[m], ph_recv.at[r], r=r ^ m).start()
            else:
                pltpu.make_async_copy(src, dst, ph_recv.at[r]).start()

    def home_of_columns(landing, home, send, recv):
        per = landing.shape[1] // (s_size // 2)

        def go(d, j):
            s_to = d * (s_size // 2) + j // per
            for m in range(r_size):
                to_home(landing.at[d, j], home.at[me, j % per], send.at[s_to, m], recv.at[me], s_to, m)

        return go

    def out_targets():
        a = (me * own_cols) // shard_rows
        b = (me * own_cols + own_cols - 1) // shard_rows
        return ((a, a < s_size), (b, jnp.logical_and(b != a, b < s_size)))

    margin = (home_out.shape[0] - shard_rows) // 2

    def out_at(s_to, d, j):
        n_out, size = lo_.shape[1:3]
        first = margin + me * own_cols - s_to * shard_rows + (d * n_out + j) * size
        return pl.ds(pl.multiple_of(first, 16), size)

    def home_of_out(d, j):
        for i, (s_to, valid) in enumerate(out_targets()):

            @pl.when(valid)
            def _(i=i, s_to=s_to):
                for m in range(r_size):
                    to_home(lo_.at[d, j], home_out.at[out_at(s_to, d, j)], oh_send.at[i, m], oh_recv.at[me], s_to, m)

    def line(jobs, landing, sems, home, start):
        return LineSum(jobs, landing, *sems, home, start, LAG)

    sum_proj = line(jp, lp, (p_rs, p_rr, p_as, p_ar), home_of_proj, 0)
    start = sum_proj.n
    sum_fc = line(jf, lf, (f_rs, f_rr, f_as, f_ar), home_of_columns(lf, home_fc, fh_send, fh_recv), start)
    start += sum_fc.n
    sum_out = line(jo, lo_, (o_rs, o_rr, o_as, o_ar), home_of_out, start)
    start += sum_out.n
    sum_qkv = line(jq, lq, (q_rs, q_rr, q_as, q_ar), home_of_columns(lq, home_qkv, qh_send, qh_recv), start)
    clock = Clock([sum_proj, sum_fc, sum_out, sum_qkv])
    clock.run(TICKS[0])

    def slot(offset):
        return (offset // r_size) // 2 * r_size + offset % r_size

    def block(ref):
        return lambda o, part: ref.at[pl.ds(o * rows + part * half, half)]

    def packed_block(ref):
        return lambda o, part: ref.at[pl.ds(slot(o) * rows + part * half, half)]

    def far_load(ref):
        def load(o, part):
            copy = pltpu.make_async_copy(block(ref)(o, part), tmp, tmp_sem.at[0])
            copy.start()
            copy.wait()
            return tmp[...]

        return load

    if land_near.shape[0] == tokens:
        land, load_land = block(land_near), lambda o, part: block(land_near)(o, part)[...]
    else:
        land, load_land = block(land_far), far_load(land_far)
    scatter_two = Scatter(packed_block(leaf), packed_block(acc), land, load_land, s2_send, s2_recv, r_size)
    if chunks == 1:
        land_p, load_p = block(chunk2), lambda o, part: block(chunk2)(o, part)[...]
    else:
        land_p, load_p = block(landp), far_load(landp)
    scatter_proj = Scatter(packed_block(leaf), packed_block(acc), land_p, load_p, sp_send, sp_recv, r_size)
    scatter_one = Scatter(packed_block(leaf), packed_block(acc), land, load_land, s1_send, s1_recv, r_size)
    n = r_size * rows

    def partial_sums(dst, odd, lhs, rhs, contract):
        def one(i, carry):
            dst[pl.ds(pl.multiple_of(i * n, n), n), :] = lax.dot_general(
                lhs[pl.ds(pl.multiple_of((2 * i + odd) * n, n), n), :], rhs[...], contract, preferred_element_type=F32
            ).astype(BF16)
            return carry

        lax.fori_loop(0, s_size // 2, one, 0)

    partial_sums(leaf, 1, gpre, own_f, contract_last)
    scatter_two.start_leaves()
    clock.run(TICKS[1])
    partial_sums(acc, 0, gpre, own_f, contract_last)
    load_q.start()
    if chunks == 1:
        product_rows(chunk, gpre, into_jobs(jf))
    clock.run(TICKS[2])

    scatter_two.start_inner()
    clock.run(TICKS[3])
    vec[...] = jnp.zeros_like(vec)
    gain_one, gain_two, proj_bias = (small_ref[i : i + 1, :] for i in (0, 3, 5))
    for load in loads[2:]:
        load.wait()
    cot = cot_v[...].astype(F32)
    middle = middle_ref[...]
    normed, inverse = norm_parts(middle)
    grad_in, grad_gain, grad_bias = norm_backward_rows(scatter_two.finish(), normed, inverse, gain_two)
    grad_middle = cot + grad_in
    branch = grad_middle.astype(BF16)
    gb_own[...] = branch
    gather = Gather(block(gb), g_send, g_recv, r_size, own=lambda o, part: gb_own.at[pl.ds(part * half, half)])
    gather.start(0)
    save_gb = pltpu.make_async_copy(gb_own, gb.at[pl.ds(0, rows)], tmp_sem.at[1])
    save_gb.start()
    vec[2:3, :] = jnp.sum(branch.astype(F32), axis=0, keepdims=True)
    vec[3:4, :] = grad_gain
    vec[4:5, :] = grad_bias
    vec[5:6, :] = jnp.sum(cot, axis=0, keepdims=True)
    clock.run(TICKS[4])
    gather.start_rest()
    scatter_two.close()
    partial_sums(leaf, 1, act, own_p, (((1,), (0,)), ((), ())))
    scatter_proj.start_leaves()
    clock.run(TICKS[5])
    partial_sums(acc, 0, act, own_p, (((1,), (0,)), ((), ())))
    gather.need_all()
    save_gb.wait()
    scatter_proj.start_inner()
    clock.run(TICKS[6])

    if chunks > 1:
        go_acc[...] = jnp.zeros_like(go_acc)

    def branch_rows(i, carry):
        at = pl.ds(pl.multiple_of(i * step, step), step)
        fetch(gb, at, chunk, 2).wait()
        do_ref[at, :] = lax.dot_general(
            chunk[...], own_o[...], contract_last, preferred_element_type=F32
        ).astype(BF16)
        product_rows(att_ref.at[at], chunk, into_jobs(jo) if chunks == 1 else into_sum(go_acc))
        return carry

    if chunks == 1:
        branch_rows(0, 0)
    else:
        lax.fori_loop(0, chunks, branch_rows, 0)
        into_jobs(jo)(0, own_cols, go_acc[...])
    clock.run(TICKS[7])
    out_v[...] = (middle + (scatter_proj.finish() + proj_bias)).astype(BF16)

    def moved(src, dst, sem):
        far = remote(src, dst, sem.at[0], sem.at[1], z=s, s=z)
        near = pltpu.make_async_copy(src, dst, sem.at[1])

        @pl.when(s != z)
        def _():
            far.start()

        @pl.when(s == z)
        def _():
            near.start()

        def done():
            @pl.when(s != z)
            def _():
                far.wait()

            @pl.when(s == z)
            def _():
                near.wait()

        return done

    out_done = moved(out_v, out_home, mv_sem.at[0])
    if chunks == 1:
        early = [pltpu.make_async_copy(h1, chunk2, tmp_sem.at[3])]
        early[0].start()

    code_row = jnp.concatenate([code_ref[i : i + 1, :] for i in range(devices)], axis=1)
    q_rows = min(rows if tokens > 2048 else 256, tokens)
    dk_acc[...] = jnp.zeros_like(dk_acc)
    dv_acc[...] = jnp.zeros_like(dv_acc)

    def attend(i):
        at = pl.ds(pl.multiple_of(i * q_rows, q_rows), q_rows)
        per = q_rows // rows
        code_q = jnp.concatenate(
            [
                jnp.transpose(jnp.broadcast_to(code_ref[pl.ds(i * per + j, 1), :], (8, rows)))[:, 0:1]
                for j in range(per)
            ],
            axis=0,
        )
        low_q = (code_q // SEG_STEP) * SEG_STEP
        allowed = jnp.logical_and(code_row >= low_q, code_row <= code_q)
        dqs, dks, dvs = [], [], []
        for h in range(heads):
            cols = slice(h * HEAD_DIM, (h + 1) * HEAD_DIM)
            q, do, k = q_ref[at, cols], do_ref[at, cols], k_ref[:, cols]
            scores = lax.dot_general(q, k, contract_last, preferred_element_type=F32)
            scores = jnp.where(allowed, scores, NEGATIVE)
            probs = jnp.exp(scores - lse_ref[at, h : h + 1])
            dp = lax.dot_general(do, v_ref[:, cols], contract_last, preferred_element_type=F32)
            delta = jnp.sum(probs * dp, axis=-1, keepdims=True)
            ds = (probs * (dp - delta)).astype(BF16)
            dqs.append(jnp.dot(ds, k, preferred_element_type=F32))
            dks.append(lax.dot_general(ds, q, contract_first, preferred_element_type=F32))
            dvs.append(lax.dot_general(probs.astype(BF16), do, contract_first, preferred_element_type=F32))
        gp[at, 0:own_cols] = (jnp.concatenate(dqs, axis=1) * (1.0 / math.sqrt(HEAD_DIM))).astype(BF16)
        dk_acc[...] += jnp.concatenate(dks, axis=1)
        dv_acc[...] += jnp.concatenate(dvs, axis=1)

    if chunks == 1:
        clock.loop(tokens // q_rows, TICKS[8], attend)
    else:

        def attend_step(i, carry):
            attend(i)
            return carry

        lax.fori_loop(0, tokens // q_rows, attend_step, 0)
    gp[:, own_cols : 2 * own_cols] = dk_acc[...].astype(BF16)
    gp[:, 2 * own_cols :] = dv_acc[...].astype(BF16)

    scatter_proj.close()
    load_q.wait()
    partial_sums(leaf, 1, gp, own_q, contract_last)
    scatter_one.start_leaves()
    clock.run(TICKS[9])
    partial_sums(acc, 0, gp, own_q, contract_last)

    def hidden_rows(i, carry):
        at = pl.ds(pl.multiple_of(i * step, step), step)
        (early[0] if early else fetch(h1, at, chunk2, 3)).wait()
        product_rows(chunk2, gp.at[at], into_jobs(jq) if chunks == 1 else into_sum(gq_acc))
        return carry

    if chunks == 1:
        hidden_rows(0, 0)
    else:
        lax.fori_loop(0, chunks, hidden_rows, 0)
        into_jobs(jq)(0, width, gq_acc[...])
    scatter_one.start_inner()
    clock.run(TICKS[10])

    resid = x_ref[...].astype(F32)
    normed, inverse = norm_parts(resid)
    grad_in, grad_gain, grad_bias = norm_backward_rows(scatter_one.finish(), normed, inverse, gain_one)
    ig_v[...] = (grad_middle + grad_in).astype(BF16)
    ig_done = moved(ig_v, ig_home, mv_sem.at[1])
    vec[0:1, :] = grad_gain
    vec[1:2, :] = grad_bias
    ff_lanes = -(-own_ff // 128) * 128
    q_lanes = -(-own_cols // 128) * 128
    vec[7:8, 0:own_ff] = jnp.sum(gpre[...].astype(F32), axis=0, keepdims=True)
    vec[7:8, ff_lanes : ff_lanes + own_cols] = jnp.sum(gp[:, :own_cols].astype(F32), axis=0, keepdims=True)
    vec[7:8, ff_lanes + q_lanes : ff_lanes + q_lanes + own_cols] = jnp.sum(
        gp[:, 2 * own_cols :].astype(F32), axis=0, keepdims=True
    )
    vec[pl.ds(8 + me, 1), :] = vec[7:8, :]

    hops = [("s", 1), ("s", 2)] + [("r", bit) for bit in bits_of(r_size)] + [("z", bit) for bit in bits_of(z_size)]
    for i, (axis, bit) in enumerate(hops):
        copy = remote(vec, vec_land.at[i], vec_send.at[i], vec_recv.at[i], **partner(axis, bit))
        copy.start()
        clock.run(TICKS[11])
        copy.wait()
        vec[...] = vec[...] + vec_land[i]
    small_out[...] = vec[...]
    clock.run(clock.end)

    scatter_one.close()
    gather.close()
    out_done()
    ig_done()
    for total in (sum_proj, sum_fc, sum_qkv, sum_out):
        total.close()
    for i in range(r_size):
        pltpu.make_async_copy(home_proj.at[i], home_proj.at[i], ph_recv.at[i]).wait()
    for m in range(1, r_size):
        pltpu.make_async_copy(home_proj.at[0], home_proj.at[0], ph_send.at[m]).wait()
    for home, send, recv in ((home_fc, fh_send, fh_recv), (home_qkv, qh_send, qh_recv)):
        for i in range(devices):
            pltpu.make_async_copy(home.at[i], home.at[i], recv.at[i]).wait()
        for s_to in range(s_size):
            for m in range(r_size):
                sent = pltpu.make_async_copy(home.at[0], home.at[0], send.at[s_to, m])
                if m:
                    sent.wait()
                else:

                    @pl.when(s != s_to)
                    def _(sent=sent):
                        sent.wait()

    out_block = home_out.at[pl.ds(0, own_cols)]
    for i in range(devices):
        a, b = (i * own_cols) // shard_rows, (i * own_cols + own_cols - 1) // shard_rows

        @pl.when(jnp.logical_or(s == a, s == b))
        def _(i=i):
            pltpu.make_async_copy(out_block, out_block, oh_recv.at[i]).wait()

    for i, (s_to, valid) in enumerate(out_targets()):
        for m in range(r_size):
            far = valid if m else jnp.logical_and(valid, s_to != s)

            @pl.when(far)
            def _(i=i, m=m):
                pltpu.make_async_copy(out_block, out_block, oh_send.at[i, m]).wait()


def backward_part(h2, cot, wf, wp, h1, wq, wo, q, k, v, att, lse, code, middle, x_own, small, fcb):
    s_size, r_size, z_size = (lax.axis_size(a) for a in ("s", "r", "z"))
    devices = s_size * r_size
    rows, width = x_own.shape
    tokens = rows * devices
    own_cols = q.shape[1]
    heads = own_cols // HEAD_DIM
    own_ff = wf.shape[1]
    shard_rows = width // s_size
    p_rows = job_rows(own_ff // 2)
    p_n = own_ff // 2 // p_rows
    c_rows = job_rows(shard_rows)
    c_per = shard_rows // c_rows
    c_n = c_per * s_size // 2
    o_rows = job_rows(own_cols // 2)
    o_n = own_cols // 2 // o_rows
    hops = 2 + len(bits_of(r_size)) + len(bits_of(z_size))
    vec_rows = 8 + devices
    small_plane = tokens <= 1024
    step = tokens if small_plane else 256
    anywhere = pl.BlockSpec(memory_space=pl.ANY)
    vmem = pl.BlockSpec(memory_space=pltpu.VMEM)
    shape = jax.ShapeDtypeStruct
    dma = pltpu.SemaphoreType.DMA
    tree = [dma((2, devices))] * 2
    jobs = [(2, p_n, p_rows, width), (2, c_n, c_rows, own_ff), (2, c_n, c_rows, 3 * own_cols), (2, o_n, o_rows, width)]
    line = [dma(j[:2]) for j in jobs for _ in range(4)]

    def sums(*dims):
        return pltpu.VMEM((8, 128) if small_plane else dims, F32)

    return pl.pallas_call(
        backward_kernel,
        in_specs=[anywhere] * 7 + [vmem] * 10,
        out_specs=[anywhere] * 6 + [vmem] + [anywhere] * 3,
        out_shape=[
            shape((rows, width), BF16),
            shape((rows, width), BF16),
            shape((r_size,) + jobs[0], BF16),
            shape((devices, c_per, c_rows, own_ff), BF16),
            shape((devices, c_per, c_rows, 3 * own_cols), BF16),
            shape((2 * (-(-own_cols // c_rows)) * c_rows + shard_rows, width), BF16),
            shape((vec_rows, width), F32),
            shape((tokens, width), BF16),
            shape((tokens, width), BF16),
            shape((tokens, width), BF16),
        ],
        scratch_shapes=[
            pltpu.VMEM((tokens // 2, width), BF16),
            pltpu.VMEM((tokens // 2, width), BF16),
            pltpu.VMEM((tokens if small_plane else 16, width), BF16),
            pltpu.VMEM((rows // 2, width), BF16),
        ]
        + [pltpu.VMEM(j, BF16) for j in jobs]
        + [pltpu.VMEM(j, BF16) for j in jobs]
        + [
            pltpu.VMEM((width, own_ff), BF16),
            pltpu.VMEM((own_ff, width), BF16),
            pltpu.VMEM((16, 128) if small_plane else (width, 3 * own_cols), BF16),
            pltpu.VMEM((own_cols, width), BF16),
            pltpu.VMEM((rows, width), BF16),
            pltpu.VMEM((step, width), BF16),
            pltpu.VMEM((step, width), BF16),
            sums(own_ff, width),
            sums(width, own_ff),
            sums(width, 3 * own_cols),
            pltpu.VMEM((tokens, own_ff), BF16),
            pltpu.VMEM((tokens, own_ff), BF16),
            pltpu.VMEM((tokens, own_cols), BF16),
            pltpu.VMEM((tokens, 3 * own_cols), BF16),
            pltpu.VMEM((tokens, own_cols), F32),
            pltpu.VMEM((tokens, own_cols), F32),
            sums(own_cols, width),
            pltpu.VMEM((vec_rows, width), F32),
            pltpu.VMEM((hops, vec_rows, width), F32),
            pltpu.VMEM((rows, width), BF16),
            pltpu.VMEM((rows, width), BF16),
            pltpu.VMEM((rows, width), BF16),
            dma((5,)),
        ]
        + tree * 4
        + [dma((4,)), dma((2, 2)), dma((hops,)), dma((hops,))]
        + line
        + [
            dma((r_size,)), dma((r_size,)),
            dma((s_size, r_size)), dma((devices,)),
            dma((s_size, r_size)), dma((devices,)),
            dma((2, r_size)), dma((devices,)),
        ],
        compiler_params=pltpu.CompilerParams(
            collective_id=1, has_side_effects=True, vmem_limit_bytes=62 << 20
        ),
        cost_estimate=pl.CostEstimate(
            flops=10 * heads * tokens * tokens * HEAD_DIM + 12 * tokens * width * own_ff,
            bytes_accessed=40 << 20,
            transcendentals=0,
        ),
        name="backward_part",
    )(h2, cot, wf, wp, h1, wq, wo, q, k, v, att, lse, code, middle, x_own, small, fcb)


def results_kernel(
    out_in, ig_in, proj_in, fc_in, qkv_in, wo_in, sums,
    out, ig, g1, b1, qkv, qv, wo, ob, g2, b2, fc, fcb, proj, pb,
):
    devices = fc_in.shape[0]
    own_ff, own_cols = fc_in.shape[3], qkv_in.shape[3] // 3
    width = wo.shape[1]
    proj[...] = proj_in[...].astype(F32)
    wo[...] = wo_in[...].astype(F32)
    fc[...] = jnp.concatenate([fc_in[device, 0] for device in range(devices)], axis=1).astype(F32)
    parts = []
    for part in range(3):
        for device in range(devices):
            n = max(0, min(own_cols, width - device * own_cols))
            if n:
                parts.append(qkv_in[device, 0, :, part * own_cols : part * own_cols + n])
    qkv[...] = jnp.concatenate(parts, axis=1).astype(F32)

    @pl.when(pl.program_id(0) == 0)
    def _():
        out[...] = jnp.transpose(out_in[...])
        ig[...] = jnp.transpose(ig_in[...].astype(F32))
        s = lax.axis_index("s")
        s_size = lax.axis_size("s")
        ff_lanes = -(-own_ff // 128) * 128
        q_lanes = -(-own_cols // 128) * 128
        by_device = devices // s_size

        def heads_of(first):
            return jnp.concatenate(
                [sums[8 + d : 9 + d, first : first + own_cols] for d in range(devices)], axis=1
            )[:, :width]

        qv_all = jnp.concatenate([heads_of(ff_lanes), heads_of(ff_lanes + q_lanes)], axis=1)
        for s2 in range(s_size):

            @pl.when(s == s2)
            def _(s2=s2):
                n = width // s_size
                for i, ref in enumerate((g1, b1, ob, g2, b2, pb)):
                    ref[...] = sums[i, s2 * n : (s2 + 1) * n]
                qv[...] = qv_all[0, 2 * s2 * n : 2 * (s2 + 1) * n]
                fcb[...] = jnp.concatenate(
                    [sums[8 + d : 9 + d, 0:own_ff] for d in range(s2 * by_device, (s2 + 1) * by_device)], axis=1
                )[0]


def results(out_home, ig_home, home_proj, home_fc, home_qkv, home_out, sums):
    devices, c_per, c_rows, own_ff = home_fc.shape
    rows, width = out_home.shape
    shard_rows = c_per * c_rows
    own_cols = home_qkv.shape[3] // 3
    proj = home_proj.reshape(-1, width)
    ff = devices * own_ff
    steps = c_per
    proj_rows = proj.shape[0] // steps
    first = (home_out.shape[0] - shard_rows) // 2 // c_rows
    whole = lambda *dims: pl.BlockSpec(dims, lambda i: (0,) * len(dims))
    by_rows = lambda n, columns: pl.BlockSpec((n, columns), lambda i: (i, 0))
    by_device = lambda columns: pl.BlockSpec((devices, 1, c_rows, columns), lambda i: (0, i, 0, 0))
    shape = lambda *dims: jax.ShapeDtypeStruct(dims, F32)
    vector = whole(shard_rows)
    return pl.pallas_call(
        results_kernel,
        grid=(steps,),
        in_specs=[
            whole(rows, width),
            whole(rows, width),
            by_rows(proj_rows, width),
            by_device(own_ff),
            by_device(3 * own_cols),
            pl.BlockSpec((c_rows, width), lambda i: (first + i, 0)),
            whole(*sums.shape),
        ],
        out_specs=[
            whole(width, rows),
            whole(width, rows),
            vector,
            vector,
            by_rows(c_rows, 3 * width),
            whole(2 * shard_rows),
            by_rows(c_rows, width),
            vector,
            vector,
            vector,
            by_rows(c_rows, ff),
            whole(proj.shape[0]),
            by_rows(proj_rows, width),
            vector,
        ],
        out_shape=[
            jax.ShapeDtypeStruct((width, rows), BF16),
            shape(width, rows),
            shape(shard_rows),
            shape(shard_rows),
            shape(shard_rows, 3 * width),
            shape(2 * shard_rows),
            shape(shard_rows, width),
            shape(shard_rows),
            shape(shard_rows),
            shape(shard_rows),
            shape(shard_rows, ff),
            shape(proj.shape[0]),
            shape(*proj.shape),
            shape(shard_rows),
        ],
        compiler_params=pltpu.CompilerParams(vmem_limit_bytes=61 << 20),
        name="results",
    )(out_home, ig_home, proj, home_fc, home_qkv, home_out, sums)


def local(
    inputs,
    positions,
    segments,
    cotangent,
    ln1_gain,
    ln1_bias,
    w_qkv,
    qv_bias,
    w_out,
    out_bias,
    ln2_gain,
    ln2_bias,
    w_fc,
    fc_bias,
    w_proj,
    proj_bias,
):
    rows = inputs.shape[0]
    code = jnp.broadcast_to(segments * SEG_STEP + positions // BLOCK, (8, rows))
    vectors = (ln1_gain, ln1_bias, out_bias, ln2_gain, ln2_bias, proj_bias, qv_bias, fc_bias)

    (
        hidden_one, hidden_two, cot, own_fc, own_qkv, own_out, queries, keys, values, attended, lse, code_all,
        middle, x_own, small, own_fcb,
    ) = forward_part(inputs.T, cotangent.T, code, vectors, w_qkv, w_fc, w_out)
    found = backward_part(
        hidden_two, cot, own_fc, w_proj, hidden_one, own_qkv, own_out, queries, keys, values, attended, lse, code_all,
        middle, x_own, small, own_fcb,
    )
    out, input_grad, *grads = results(*found[:7])
    return (out.T, input_grad.T, *grads)


def solution(mesh):
    ctx, shard = mesh.devices.shape
    fine = Mesh(mesh.devices.reshape(shard, ctx // shard, shard), ("z", "r", "s"))
    tokens = ("s", "z", "r")
    arg_specs = (
        P(tokens, None),
        P(tokens),
        P(tokens),
        P(tokens, None),
        P("s"),
        P("s"),
        P("s", None),
        P("s"),
        P("s", None),
        P("s"),
        P("s"),
        P("s"),
        P("s", None),
        P("s"),
        P("s", None),
        P("s"),
    )
    out_specs = (P(tokens, None), P(tokens, None)) + arg_specs[4:]
    return jax.shard_map(local, mesh=fine, in_specs=arg_specs, out_specs=out_specs, check_vma=False)
```

```python
import math

import jax
import jax.numpy as jnp
from jax import lax
from jax.experimental import pallas as pl
from jax.experimental.pallas import tpu as pltpu
from jax.sharding import Mesh, PartitionSpec as P

HEAD_DIM = 64
BLOCK = 256
EPSILON = 1e-05
NEGATIVE = -1e30
SEG_STEP = 65536
BF16 = jnp.bfloat16
F32 = jnp.float32


def bits_of(size):
    return [1 << i for i in range(size.bit_length() - 1)]


def norm_parts(values):
    centre = jnp.mean(values, axis=-1, keepdims=True)
    centred = values - centre
    spread = jnp.mean(centred * centred, axis=-1, keepdims=True)
    inverse = lax.rsqrt(spread + EPSILON)
    return centred * inverse, inverse


def gelu_parts(u):
    c = math.sqrt(2.0 / math.pi)
    squared = u * u
    t = jnp.tanh(c * (u + 0.044715 * (u * squared)))
    half = 0.5 * (1.0 + t)
    slope = half + 0.5 * u * (1.0 - t * t) * (c * (1.0 + 3.0 * 0.044715 * squared))
    return u * half, slope


def dot(a, b, contract=((1,), (0,))):
    return lax.dot_general(a, b, (contract, ((), ())), preferred_element_type=F32)


ACROSS_TOKENS = ((0,), (0,))
ON_LAST = ((1,), (1,))


MESH_ID = pl.DeviceIdType.MESH


def remote(src, dst, send_sem, recv_sem, **device):
    return pltpu.make_async_remote_copy(
        src_ref=src,
        dst_ref=dst,
        send_sem=send_sem,
        recv_sem=recv_sem,
        device_id=device,
        device_id_type=MESH_ID,
    )


def partner(axis, bit):
    return {axis: lax.axis_index(axis) ^ bit}


def plane_device(offset, r_size):
    found = {}
    if offset // r_size:
        found["s"] = lax.axis_index("s") ^ (offset // r_size)
    if offset % r_size:
        found["r"] = lax.axis_index("r") ^ (offset % r_size)
    return found


def tree_of(order, r_size):
    levels = []
    known = [(0, 0)]
    for axis, bit in order:
        step = bit * r_size if axis == "s" else bit
        known = known + [(o ^ step, depth + 1) for o, depth in known]
    found = {}
    for o, depth in known:
        if o == 0:
            continue
        for axis, bit in order[::-1]:
            step = bit * r_size if axis == "s" else bit
            if o & step:
                found.setdefault(depth, []).append((o, o ^ step, axis, bit))
                break
    for depth in sorted(found):
        levels.append(found[depth])
    return levels


def chip_orders(r_size):
    chips = [("s", 2)] + [("r", bit) for bit in bits_of(r_size)]
    return [chips + [("s", 1)], chips[::-1] + [("s", 1)]]


class Gather:
    def __init__(self, block, send_sem, recv_sem, r_size, parts=2, own=None):
        self.block = block
        self.own = own or block
        self.send_sem = send_sem
        self.recv_sem = recv_sem
        self.levels = [tree_of(order, r_size) for order in chip_orders(r_size)[:parts]]
        self.parts = parts
        self.arrived = set()

    def copy(self, part, transfer):
        offset, source, axis, bit = transfer
        src = self.own(0, part) if source == 0 else self.block(source, part)
        return remote(
            src,
            self.block(offset, part),
            self.send_sem.at[part, offset],
            self.recv_sem.at[part, offset],
            **partner(axis, bit),
        )

    def transfers(self):
        for level in range(len(self.levels[0])):
            for i in range(len(self.levels[0][level])):
                for part in range(self.parts):
                    yield level, part, self.levels[part][level][i]

    def find(self, part, offset):
        for _, p, t in self.transfers():
            if p == part and t[0] == offset:
                return t

    def need(self, part, offset):
        if offset and (part, offset) not in self.arrived:
            self.arrived.add((part, offset))
            self.copy(part, self.find(part, offset)).wait_recv()

    def start(self, level):
        for lv, part, t in self.transfers():
            if lv == level:
                self.need(part, t[1])
                self.copy(part, t).start()

    def start_rest(self):
        for level in range(1, len(self.levels[0])):
            self.start(level)

    def need_all(self):
        for _, part, t in self.transfers():
            self.need(part, t[0])

    def close(self):
        self.need_all()
        for _, part, t in self.transfers():
            self.copy(part, t).wait_send()


def attention_rows(rows, first, q_ref, k_ref, v_ref, code_q, code_k):
    heads = q_ref.shape[1] // HEAD_DIM
    low_q = (code_q // SEG_STEP) * SEG_STEP
    allowed = jnp.logical_and(code_k >= low_q, code_k <= code_q)
    outs = []
    sums = []
    for h in range(heads):
        cols = slice(h * HEAD_DIM, (h + 1) * HEAD_DIM)
        scores = lax.dot_general(
            q_ref[pl.ds(first, rows), cols],
            k_ref[:, cols],
            (((1,), (1,)), ((), ())),
            preferred_element_type=F32,
        )
        scores = jnp.where(allowed, scores, NEGATIVE)
        top = jnp.max(scores, axis=-1, keepdims=True)
        unnorm = jnp.exp(scores - top)
        total = jnp.sum(unnorm, axis=-1, keepdims=True)
        mixed = jnp.dot(unnorm.astype(BF16), v_ref[:, cols], preferred_element_type=F32)
        outs.append((mixed / total).astype(BF16))
        sums.append(top + jnp.log(total))
    return jnp.concatenate(outs, axis=1), jnp.concatenate(sums, axis=1)


def split_rows(n):
    first = -(-n // 32) * 16
    return ((0, first), (first, n - first))


class WeightPush:
    def __init__(self, source, dest, rows, send_sem, recv_sem, across):
        self.source, self.dest, self.rows = source, dest, rows
        self.send_sem, self.recv_sem = send_sem, recv_sem
        self.across = across

    def core_copy(self):
        s = lax.axis_index("s")
        return remote(
            self.source(s ^ 1),
            self.dest(s, 0, self.rows),
            self.send_sem.at[0],
            self.recv_sem.at[0],
            s=s ^ 1,
        )

    def chip_copy(self, m, part, landed=None):
        s = lax.axis_index("s")
        first, count = split_rows(self.rows)[part]
        return remote(
            self.source(s ^ m).at[pl.ds(first, count)],
            self.dest(s, first, count),
            self.send_sem.at[m],
            self.recv_sem.at[m],
            s=s ^ m,
        )

    def relay_copy(self, m, part):
        s = lax.axis_index("s")
        first, count = split_rows(self.rows)[part]
        ref = self.dest(s ^ m, first, count)
        return remote(
            ref, ref, self.send_sem.at[2 + m], self.recv_sem.at[2 + m], z=lax.axis_index("z") ^ 1
        )

    def per_part(self, act):
        odd = lax.axis_index("z") % 2
        for part in range(2):

            @pl.when(odd == part)
            def _(part=part):
                act(part)

    def start(self):
        if 1 in self.across:
            self.core_copy().start()

        def act(part):
            for m in self.across:
                if m != 1:
                    self.chip_copy(m, part).start()

        self.per_part(act)

    def relay(self):
        def act(part):
            for m in self.across:
                if m != 1:
                    self.chip_copy(m, part).wait_recv()
                    self.relay_copy(m, part).start()

        self.per_part(act)

    def need(self):
        if 1 in self.across:
            self.core_copy().wait_recv()

        def act(part):
            for m in self.across:
                if m != 1:
                    self.relay_copy(m, 1 - part).wait_recv()

        self.per_part(act)

    def close(self):
        if 1 in self.across:
            self.core_copy().wait_send()

        def act(part):
            for m in self.across:
                if m != 1:
                    self.chip_copy(m, part).wait_send()
                    self.relay_copy(m, part).wait_send()

        self.per_part(act)


def forward_kernel(
    x_in, cot_in, code_in, g1_in, b1_in, ob_in, g2_in, b2_in, pb_in, qv_in, fcb_in, wq_in, wf_in, wo_in,
    h1_out, h2_out, cot_out, wf_out, wq_out, wo_out, q_ref, k_ref, v_ref, att_ref, lse_ref, code_out,
    middle_out, x_own, small_ref, fcb_out,
    xt_vm, ct_vm, x_vm, cot_vm, vec_in, code_land, vec_land, bias_ref, h1, wq_vm, stage_q, wf_vm, stage_f, own_q, full_out, att_land, h2_own,
    x_sem, code_sem, cot_sem, small_sem, load_sem, h1_send, h1_recv, cd_send, cd_recv, ct_send, ct_recv, h2_send,
    h2_recv, wq_send, wq_recv, wf_send, wf_recv, wo_send, wo_recv, at_send, at_recv, out_sem,
):
    s, r, z = (lax.axis_index(a) for a in ("s", "r", "z"))
    s_size, r_size = lax.axis_size("s"), lax.axis_size("r")
    devices = s_size * r_size
    me = s * r_size + r
    width, rows = x_in.shape
    tokens = rows * devices
    own_cols = q_ref.shape[1]
    own_ff = wf_out.shape[1]
    shard_rows = wq_in.shape[0]

    def shard_at(i, first=0, count=shard_rows):
        return pl.ds(pl.multiple_of(i * shard_rows + first, 16), count)

    x_loads = [
        pltpu.make_async_copy(x_in, xt_vm, load_sem.at[3]),
        pltpu.make_async_copy(cot_in, ct_vm, load_sem.at[4]),
    ]
    for load in x_loads:
        load.start()

    barrier = pltpu.get_barrier_semaphore()
    for offset in range(1, devices):
        pl.semaphore_signal(barrier, inc=1, device_id=plane_device(offset, r_size), device_id_type=MESH_ID)
    pl.semaphore_signal(barrier, inc=1, device_id={"z": z ^ 1}, device_id_type=MESH_ID)

    @pl.when(s != z)
    def _():
        pl.semaphore_signal(barrier, inc=1, device_id={"z": s, "s": z}, device_id_type=MESH_ID)

    at = 0
    for ref in (g1_in, b1_in, ob_in, g2_in, b2_in, pb_in, qv_in, fcb_in):
        vec_in[0:1, at : at + ref.shape[0]] = ref[...].astype(F32).reshape(1, ref.shape[0])
        at += ref.shape[0]
    for load, src, dst in zip(x_loads, (xt_vm, ct_vm), (x_vm, cot_vm)):
        load.wait()
        dst[...] = jnp.transpose(src[...])
    pl.semaphore_wait(barrier, devices + jnp.where(s != z, 1, 0))

    def moved(src, dst, sem):
        far = remote(src, dst, sem.at[0], sem.at[1], z=s, s=z)
        near = pltpu.make_async_copy(src, dst, sem.at[1])

        @pl.when(s != z)
        def _():
            far.start()

        @pl.when(s == z)
        def _():
            near.start()

        def arrived():
            @pl.when(s != z)
            def _():
                far.wait_recv()

            @pl.when(s == z)
            def _():
                near.wait()

        def sent():
            @pl.when(s != z)
            def _():
                far.wait_send()

        return arrived, sent

    x_arrived, x_sent = moved(x_vm, x_own, x_sem)
    code_arrived, code_sent = moved(code_in, code_land.at[0], code_sem)
    loads = [
        pltpu.make_async_copy(wq_in, wq_vm, load_sem.at[0]),
        pltpu.make_async_copy(wf_in, wf_vm, load_sem.at[1]),
        pltpu.make_async_copy(wo_in, full_out.at[shard_at(s)], load_sem.at[2]),
    ]
    for load in loads:
        load.start()
    small_copies = [
        remote(vec_in, vec_land.at[s], small_sem.at[0, m], small_sem.at[1, m], s=s ^ m) for m in range(1, s_size)
    ]
    for copy in small_copies:
        copy.start()
    vec_land[s] = vec_in[...]
    if full_out.shape[0] > width:
        full_out[width:, :] = jnp.zeros((full_out.shape[0] - width, width), BF16)

    loads[0].wait()
    for s2 in range(s_size):
        for r2 in range(r_size):

            @pl.when(r == r2)
            def _(s2=s2, r2=r2):
                device = s2 * r_size + r2
                for part in range(3):
                    lo = device * own_cols
                    n = max(0, min(own_cols, width - lo))
                    if n:
                        stage_q[s2, :, part * own_cols : part * own_cols + n] = wq_vm[
                            :, part * width + lo : part * width + lo + n
                        ]
                    if n < own_cols:
                        stage_q[s2, :, part * own_cols + n : (part + 1) * own_cols] = jnp.zeros(
                            (shard_rows, own_cols - n), BF16
                        )

    push_q = WeightPush(
        lambda i: stage_q.at[i],
        lambda i, first, count: own_q.at[shard_at(i, first, count)],
        shard_rows, wq_send, wq_recv, (1, 2, 3),
    )
    push_q.start()
    own_q[shard_at(s), :] = stage_q[s]

    for copy in small_copies:
        copy.wait_recv()
    per = shard_rows
    small_ref[...] = jnp.zeros_like(small_ref)
    for s2 in range(s_size):
        for i in range(6):
            small_ref[i : i + 1, s2 * per : (s2 + 1) * per] = vec_land[s2, :, i * per : (i + 1) * per]
    for part in range(2):
        q_or_v = jnp.concatenate(
            [vec_land[part * s_size // 2 + i, :, 6 * per : 8 * per] for i in range(s_size // 2)], axis=1
        )
        for device in range(devices):
            n = max(0, min(own_cols, width - device * own_cols))
            if n:
                bias_ref[part, device : device + 1, 0:n] = q_or_v[:, device * own_cols : device * own_cols + n]
            if n < own_cols:
                bias_ref[part, device : device + 1, n:] = jnp.zeros((1, own_cols - n), F32)
    for r2 in range(r_size):

        @pl.when(r == r2)
        def _(r2=r2):
            fcb_out[...] = vec_in[:, 8 * per + r2 * own_ff : 8 * per + (r2 + 1) * own_ff]

    gain_one, bias_one, out_bias, gain_two, bias_two = (small_ref[i : i + 1, :] for i in range(5))
    x_arrived()
    resid = x_own[...].astype(F32)
    normed, _ = norm_parts(resid)
    h1[0:rows, :] = (normed * gain_one + bias_one).astype(BF16)
    half = rows // 2

    def block_of(ref):
        return lambda offset, part: ref.at[pl.ds(offset * rows + part * half, half)]

    gather_one = Gather(block_of(h1), h1_send, h1_recv, r_size)
    gather_one.start(0)
    code_arrived()
    gather_code = Gather(lambda offset, part: code_land.at[offset], cd_send, cd_recv, r_size, parts=1)
    gather_code.start(0)

    loads[1].wait()
    for s2 in range(s_size):
        for r2 in range(r_size):

            @pl.when(r == r2)
            def _(s2=s2, r2=r2):
                lo = (s2 * r_size + r2) * own_ff
                stage_f[s2] = wf_vm[:, lo : lo + own_ff]

    gather_one.start(1)
    gather_code.start(1)
    push_q.relay()
    for level in range(2, len(gather_one.levels[0])):
        gather_one.start(level)
        gather_code.start(level)

    push_o = WeightPush(
        lambda i: full_out.at[shard_at(s)],
        lambda i, first, count: full_out.at[shard_at(i, first, count)],
        shard_rows, wo_send, wo_recv, (1, 2),
    )
    push_f = WeightPush(
        lambda i: stage_f.at[i],
        lambda i, first, count: wf_out.at[shard_at(i, first, count)],
        shard_rows, wf_send, wf_recv, (1, 2, 3),
    )
    own_f = pltpu.make_async_copy(
        stage_f.at[s], wf_out.at[shard_at(s)], load_sem.at[1]
    )
    own_f.start()
    gather_one.need_all()
    cot_arrived, cot_sent = moved(cot_vm, cot_out.at[pl.ds(0, rows)], cot_sem)
    loads[2].wait()
    push_o.start()
    push_f.start()

    push_q.need()
    save_q = pltpu.make_async_copy(own_q, wq_out, out_sem.at[0])
    save_q.start()
    save_h = pltpu.make_async_copy(h1, h1_out, out_sem.at[1])
    save_h.start()
    q_bias = bias_ref[0, pl.ds(me, 1), :]
    v_bias = bias_ref[1, pl.ds(me, 1), :]
    step = min(512, tokens)
    score_scale = jnp.asarray(1.0 / math.sqrt(HEAD_DIM), BF16)

    def project(i, carry):
        at = pl.ds(pl.multiple_of(i * step, step), step)
        packed = jnp.dot(h1[at, :], own_q[...], preferred_element_type=F32)
        q_ref[at, :] = (packed[:, :own_cols] + q_bias).astype(BF16) * score_scale
        k_ref[at, :] = packed[:, own_cols : 2 * own_cols].astype(BF16)
        v_ref[at, :] = (packed[:, 2 * own_cols :] + v_bias).astype(BF16)
        return carry

    lax.fori_loop(0, tokens // step, project, 0)
    gather_code.need_all()
    code_out[...] = code_land[:, 0, :]
    code_row = jnp.concatenate([code_land[i, 0:1, :] for i in range(devices)], axis=1)

    q_rows = min(rows if tokens > 2048 else 256, tokens)

    def attend(i, carry):
        first = pl.multiple_of(i * q_rows, q_rows)
        per = q_rows // rows
        code_col = jnp.concatenate(
            [jnp.transpose(code_land[i * per + j])[:, 0:1] for j in range(per)], axis=0
        )
        out, sums = attention_rows(q_rows, first, q_ref, k_ref, v_ref, code_col, code_row)
        att_ref[pl.ds(first, q_rows), :] = out
        lse_ref[pl.ds(first, q_rows), :] = sums
        return carry

    lax.fori_loop(0, tokens // q_rows, attend, 0)

    at_copies = []
    for offset in range(1, devices):
        at_copies.append(
            remote(
                att_ref.at[pl.ds(offset * rows, rows)],
                att_land.at[me],
                at_send.at[offset],
                at_recv.at[offset],
                **plane_device(offset, r_size),
            )
        )
    for copy in at_copies:
        copy.start()
    att_land[me] = att_ref[0:rows, :]
    cot_arrived()
    gather_cot = Gather(block_of(cot_out), ct_send, ct_recv, r_size)
    gather_cot.start(0)
    push_o.relay()
    push_o.need()
    far = full_out.at[shard_at(s ^ 2)]
    out_core = remote(far, far, wo_send.at[5], wo_recv.at[5], s=s ^ 1)
    out_core.start()
    gather_cot.start(1)
    for copy in at_copies:
        copy.wait_recv()
    out_core.wait_recv()
    middle = resid + out_bias
    for device in range(devices):
        middle = middle + jnp.dot(
            att_land[device],
            full_out[device * own_cols : (device + 1) * own_cols, :],
            preferred_element_type=F32,
        )
    middle_out[...] = middle
    normed, _ = norm_parts(middle)
    h2_own[...] = (normed * gain_two + bias_two).astype(BF16)
    save_h2 = pltpu.make_async_copy(h2_own, h2_out.at[pl.ds(0, rows)], out_sem.at[2])
    save_h2.start()
    gather_two = Gather(
        block_of(h2_out), h2_send, h2_recv, r_size, own=lambda o, part: h2_own.at[pl.ds(part * half, half)]
    )
    gather_two.start(0)
    save_o = pltpu.make_async_copy(
        full_out.at[pl.ds(pl.multiple_of(me * own_cols, own_cols), own_cols)], wo_out, out_sem.at[3]
    )
    save_o.start()
    for level in range(2, len(gather_cot.levels[0])):
        gather_cot.start(level)
    push_f.relay()
    gather_two.start_rest()
    gather_two.close()
    gather_cot.close()
    gather_one.close()
    gather_code.close()
    push_f.need()
    for push in (push_q, push_o, push_f):
        push.close()
    out_core.wait_send()
    for copy in at_copies + small_copies:
        copy.wait_send()
    x_sent()
    code_sent()
    cot_sent()
    own_f.wait()
    for save in (save_q, save_h, save_h2, save_o):
        save.wait()


def forward_part(x, cot, code, small, w_qkv, w_fc, w_out):
    s_size, r_size = lax.axis_size("s"), lax.axis_size("r")
    devices = s_size * r_size
    width, rows = x.shape
    tokens = rows * devices
    shard_rows = w_qkv.shape[0]
    heads = width // HEAD_DIM
    own_heads = -(-heads // devices)
    own_cols = own_heads * HEAD_DIM
    own_ff = w_fc.shape[1] // devices
    anywhere = pl.BlockSpec(memory_space=pl.ANY)
    vmem = pl.BlockSpec(memory_space=pltpu.VMEM)
    shape = jax.ShapeDtypeStruct
    dma = pltpu.SemaphoreType.DMA
    flops = 2 * tokens * width * 3 * own_cols + 4 * own_heads * tokens * tokens * HEAD_DIM
    return pl.pallas_call(
        forward_kernel,
        in_specs=[anywhere] * 3 + [vmem] * 8 + [anywhere] * 3,
        out_specs=[anywhere] * 6 + [vmem] * 10,
        out_shape=[
            shape((tokens, width), BF16),
            shape((tokens, width), BF16),
            shape((tokens, width), BF16),
            shape((width, own_ff), BF16),
            shape((width, 3 * own_cols), BF16),
            shape((own_cols, width), BF16),
            shape((tokens, own_cols), BF16),
            shape((tokens, own_cols), BF16),
            shape((tokens, own_cols), BF16),
            shape((tokens, own_cols), BF16),
            shape((tokens, own_heads), F32),
            shape((devices, rows), jnp.int32),
            shape((rows, width), F32),
            shape((rows, width), BF16),
            shape((8, width), F32),
            shape((1, own_ff), F32),
        ],
        scratch_shapes=[
            pltpu.VMEM((width, rows), BF16),
            pltpu.VMEM((width, rows), BF16),
            pltpu.VMEM((rows, width), BF16),
            pltpu.VMEM((rows, width), BF16),
            pltpu.VMEM((1, sum(a.shape[0] for a in small)), F32),
            pltpu.VMEM((devices, 8, rows), jnp.int32),
            pltpu.VMEM((s_size, 1, sum(a.shape[0] for a in small)), F32),
            pltpu.VMEM((2, devices, own_cols), F32),
            pltpu.VMEM((tokens, width), BF16),
            pltpu.VMEM(w_qkv.shape, BF16),
            pltpu.VMEM((s_size, shard_rows, 3 * own_cols), BF16),
            pltpu.VMEM(w_fc.shape, BF16),
            pltpu.VMEM((s_size, shard_rows, own_ff), BF16),
            pltpu.VMEM((width, 3 * own_cols), BF16),
            pltpu.VMEM((devices * own_cols, width), BF16),
            pltpu.VMEM((devices, rows, own_cols), BF16),
            pltpu.VMEM((rows, width), BF16),
            dma((2,)), dma((2,)), dma((2,)), dma((2, s_size)), dma((5,)),
            dma((2, devices)), dma((2, devices)), dma((1, devices)), dma((1, devices)),
            dma((2, devices)), dma((2, devices)), dma((2, devices)), dma((2, devices)),
            dma((6,)), dma((6,)), dma((6,)), dma((6,)), dma((6,)), dma((6,)),
            dma((devices,)), dma((devices,)), dma((4,)),
        ],
        compiler_params=pltpu.CompilerParams(
            collective_id=0, has_side_effects=True, vmem_limit_bytes=60 << 20
        ),
        cost_estimate=pl.CostEstimate(flops=flops, bytes_accessed=40 << 20, transcendentals=0),
        name="forward_part",
    )(x, cot, code, *small, w_qkv, w_fc, w_out)


class Scatter:
    def __init__(self, leaf, acc, land, load, send_sem, recv_sem, r_size):
        self.leaf, self.acc, self.land, self.load = leaf, acc, land, load
        self.send_sem, self.recv_sem = send_sem, recv_sem
        self.levels = [tree_of(order, r_size) for order in chip_orders(r_size)]

    def copy(self, part, transfer):
        offset, _, axis, bit = transfer
        src = self.acc(offset, part) if self.children(part, offset) else self.leaf(offset, part)
        return remote(
            src,
            self.land(offset, part),
            self.send_sem.at[part, offset],
            self.recv_sem.at[part, offset],
            **partner(axis, bit),
        )

    def children(self, part, offset):
        return [t for level in self.levels[part] for t in level if t[1] == offset]

    def start_leaves(self):
        for level in range(len(self.levels[0]) - 1, -1, -1):
            for i in range(len(self.levels[0][level])):
                for part in range(2):
                    t = self.levels[part][level][i]
                    if not self.children(part, t[0]):
                        self.copy(part, t).start()

    def total(self, part, offset):
        value = self.acc(offset, part)[...].astype(F32)
        for t in self.children(part, offset)[::-1]:
            self.copy(part, t).wait_recv()
            value = value + self.load(t[0], part).astype(F32)
        return value

    def start_inner(self):
        for level in range(len(self.levels[0]) - 1, -1, -1):
            for i in range(len(self.levels[0][level])):
                for part in range(2):
                    t = self.levels[part][level][i]
                    if self.children(part, t[0]):
                        self.acc(t[0], part)[...] = self.total(part, t[0]).astype(BF16)
                        self.copy(part, t).start()

    def finish(self):
        return jnp.concatenate([self.total(part, 0) for part in range(2)], axis=0)

    def close(self):
        for part in range(2):
            for level in self.levels[part]:
                for t in level:
                    self.copy(part, t).wait_send()


class LineSum:
    def __init__(self, jobs, land, rs_send, rs_recv, ag_send, ag_recv, home, start, lag):
        self.jobs, self.land = jobs, land
        self.rs_send, self.rs_recv, self.ag_send, self.ag_recv = rs_send, rs_recv, ag_send, ag_recv
        self.home = home
        self.n = jobs.shape[1]
        self.z = lax.axis_index("z")
        self.last = lax.axis_size("z") - 1
        self.start = start
        self.lag = lag
        self.end = start + self.n + 2 * lag * self.last

    def place(self, d):
        return self.z if d == 0 else self.last - self.z

    def up(self, d, j):
        return remote(
            self.jobs.at[d, j], self.land.at[d, j], self.rs_send.at[d, j], self.rs_recv.at[d, j], z=self.z + 1 - 2 * d
        )

    def down(self, d, j):
        return remote(
            self.land.at[d, j], self.land.at[d, j], self.ag_send.at[d, j], self.ag_recv.at[d, j], z=self.z - 1 + 2 * d
        )

    def add(self, d, j):
        place = self.place(d)

        @pl.when(place > 0)
        def _():
            self.up(d, j).wait_recv()
            total = (self.jobs[d, j].astype(F32) + self.land[d, j].astype(F32)).astype(BF16)

            @pl.when(place < self.last)
            def _():
                self.jobs[d, j] = total

            @pl.when(place == self.last)
            def _():
                self.land[d, j] = total

        @pl.when(place < self.last)
        def _():
            self.up(d, j).start()

        @pl.when(place == self.last)
        def _():
            self.down(d, j).start()
            self.home(d, j)

    def back(self, d, j):
        place = self.place(d)
        self.down(d, j).wait_recv()

        @pl.when(place > 0)
        def _():
            self.down(d, j).start()

        self.home(d, j)

    def tick(self, k):
        for d in range(2):
            place = self.place(d)
            j = k - self.start - self.lag * (2 * self.last - place)

            @pl.when(jnp.logical_and(place < self.last, jnp.logical_and(j >= 0, j < self.n)))
            def _(d=d, j=j):
                self.back(d, j)

        for d in range(2):
            j = k - self.start - self.lag * self.place(d)

            @pl.when(jnp.logical_and(j >= 0, j < self.n))
            def _(d=d, j=j):
                self.add(d, j)

    def close(self):
        def one(j, carry):
            for d in range(2):
                place = self.place(d)

                @pl.when(place < self.last)
                def _(d=d):
                    self.up(d, j).wait_send()

                @pl.when(place > 0)
                def _(d=d):
                    self.down(d, j).wait_send()

            return carry

        lax.fori_loop(0, self.n, one, 0)


class Clock:
    def __init__(self, sums):
        self.sums = sums
        self.now = 0
        self.end = max(one.end for one in sums)

    def ticks(self, first, lo, hi):
        for one in self.sums:
            if one.start < hi and one.end > lo:
                one.tick(first)

    def run(self, count):
        lo, hi = self.now, min(self.now + count, self.end)
        self.now = hi
        if hi - lo == 1:
            self.ticks(lo, lo, hi)
        elif hi > lo:

            def step(k, carry):
                self.ticks(k, lo, hi)
                return carry

            lax.fori_loop(lo, hi, step, 0)

    def loop(self, count, per, body):
        lo, hi = self.now, min(self.now + count * per, self.end)
        self.now = hi

        def step(i, carry):
            body(i)
            for j in range(per):
                self.ticks(lo + i * per + j, lo, lo + count * per)
            return carry

        lax.fori_loop(0, count, step, 0)


def product_rows(lhs, rhs, write):
    for lo in range(0, lhs.shape[1], 256):
        hi = min(lhs.shape[1], lo + 256)
        value = lax.dot_general(
            lhs[:, lo:hi], rhs[...], (((0,), (0,)), ((), ())), preferred_element_type=F32
        )
        write(lo, hi, value)


def into_jobs(jobs):
    n, size = jobs.shape[1:3]

    def write(lo, hi, value):
        value = value.astype(BF16)
        for job in range(lo // size, -(-hi // size)):
            a, b = max(lo, job * size), min(hi, (job + 1) * size)
            jobs[job // n, job % n, a - job * size : b - job * size, :] = value[a - lo : b - lo, :]

    return write


def into_sum(acc):
    def write(lo, hi, value):
        acc[lo:hi, :] += value

    return write


def job_rows(n, most=80):
    for rows in range(most, 15, -16):
        if n % rows == 0:
            return rows
    return n


def norm_backward_rows(grad, normed, inverse, gain):
    scaled = grad * gain
    mean_scaled = jnp.mean(scaled, axis=-1, keepdims=True)
    mean_product = jnp.mean(scaled * normed, axis=-1, keepdims=True)
    grad_in = inverse * (scaled - mean_scaled - normed * mean_product)
    return (
        grad_in,
        jnp.sum(grad * normed, axis=0, keepdims=True),
        jnp.sum(grad, axis=0, keepdims=True),
    )


TICKS = (1, 1, 1, 1, 1, 1, 1, 1, 1, 1, 2, 1)
LAG = 1


def backward_kernel(
    h2, cot_in, wf, wp, h1, wq, wo, q_ref, k_ref, v_ref, att_ref, lse_ref, code_ref, middle_ref, x_ref,
    small_ref, fcb_ref,
    out_home, ig_home, home_proj, home_fc, home_qkv, home_out, small_out, landp, land_far, gb,
    acc, leaf, land_near, tmp, jp, jf, jq, jo, lp, lf, lq, lo_, own_f, own_p, own_q, own_o, cot_v, chunk, chunk2,
    gp_acc, gf_acc, gq_acc, act, gpre, do_ref, gp, dk_acc, dv_acc, go_acc, vec, vec_land, gb_own, out_v, ig_v,
    load_sem, s2_send, s2_recv, sp_send, sp_recv, s1_send, s1_recv, g_send, g_recv, tmp_sem, mv_sem,
    vec_send, vec_recv,
    p_rs, p_rr, p_as, p_ar, f_rs, f_rr, f_as, f_ar, q_rs, q_rr, q_as, q_ar, o_rs, o_rr, o_as, o_ar,
    ph_send, ph_recv, fh_send, fh_recv, qh_send, qh_recv, oh_send, oh_recv,
):
    s, r, z = (lax.axis_index(a) for a in ("s", "r", "z"))
    s_size, r_size, z_size = (lax.axis_size(a) for a in ("s", "r", "z"))
    devices = s_size * r_size
    me = s * r_size + r
    rows, width = x_ref.shape
    tokens = rows * devices
    half = rows // 2
    own_cols = q_ref.shape[1]
    own_ff = wf.shape[1]
    heads = own_cols // HEAD_DIM
    shard_rows = width // s_size
    step = chunk.shape[0]
    contract_last = (((1,), (1,)), ((), ()))
    contract_first = (((0,), (0,)), ((), ()))

    barrier = pltpu.get_barrier_semaphore()
    for offset in range(1, devices):
        pl.semaphore_signal(barrier, inc=1, device_id=plane_device(offset, r_size), device_id_type=MESH_ID)
    for bit in bits_of(z_size):
        pl.semaphore_signal(barrier, inc=1, device_id={"z": z ^ bit}, device_id_type=MESH_ID)
    inner = jnp.logical_and(z > 0, z < z_size - 1)

    @pl.when(s != z)
    def _():
        pl.semaphore_signal(barrier, inc=1, device_id={"z": s, "s": z}, device_id_type=MESH_ID)

    @pl.when(inner)
    def _():
        pl.semaphore_signal(
            barrier, inc=1, device_id={"z": jnp.where(z % 2 == 1, z + 1, z - 1)}, device_id_type=MESH_ID
        )

    loads = [
        pltpu.make_async_copy(src, dst, load_sem.at[i])
        for i, (src, dst) in enumerate(
            (
                (wf, own_f),
                (wp.at[pl.ds(pl.multiple_of(r * own_ff, 8), own_ff)], own_p),
                (wo, own_o),
                (cot_in.at[pl.ds(0, rows)], cot_v),
            )
        )
    ]
    for load in loads:
        load.start()
    early = []
    if tokens == step:
        early = [
            pltpu.make_async_copy(h2, chunk, tmp_sem.at[2]),
            pltpu.make_async_copy(cot_in, chunk2, tmp_sem.at[3]),
        ]
        for load in early:
            load.start()
    if own_q.shape[0] != width:
        own_q = own_f.at[:, : 3 * own_cols]
    load_q = pltpu.make_async_copy(wq, own_q, load_sem.at[4])

    loads[0].wait()
    loads[1].wait()
    chunks = tokens // step
    if chunks > 1:
        gp_acc[...] = jnp.zeros_like(gp_acc)
        gf_acc[...] = jnp.zeros_like(gf_acc)
        gq_acc[...] = jnp.zeros_like(gq_acc)

    def fetch(src, at, dst, i):
        copy = pltpu.make_async_copy(src.at[at], dst, tmp_sem.at[i])
        copy.start()
        return copy

    piece = min(256, step)

    def feed_forward(i, carry):
        at = pl.ds(pl.multiple_of(i * step, step), step)
        first, second = early or (fetch(h2, at, chunk, 2), fetch(cot_in, at, chunk2, 3))
        first.wait()
        second.wait()

        def one(j, inner_carry):
            here = pl.ds(pl.multiple_of(j * piece, piece), piece)
            there = pl.ds(pl.multiple_of(i * step + j * piece, piece), piece)
            pre = jnp.dot(chunk[here, :], own_f[...], preferred_element_type=F32) + fcb_ref[...]
            value, slope = gelu_parts(pre)
            act[there, :] = value.astype(BF16)
            back = lax.dot_general(chunk2[here, :], own_p[...], contract_last, preferred_element_type=F32)
            gpre[there, :] = (back * slope).astype(BF16)
            return inner_carry

        lax.fori_loop(0, step // piece, one, 0)
        product_rows(act.at[at], chunk2, into_jobs(jp) if chunks == 1 else into_sum(gp_acc))
        if chunks > 1:
            product_rows(chunk, gpre.at[at], into_sum(gf_acc))
        return carry

    if chunks == 1:
        feed_forward(0, 0)
    else:
        lax.fori_loop(0, chunks, feed_forward, 0)
        into_jobs(jp)(0, own_ff, gp_acc[...])
        into_jobs(jf)(0, width, gf_acc[...])

    peers = devices - 1 + len(bits_of(z_size))
    pl.semaphore_wait(barrier, peers + jnp.where(s != z, 1, 0) + jnp.where(inner, 1, 0))

    def to_home(src, dst, send, recv, s_to, m):
        far = remote(src, dst, send, recv, s=s_to, r=r ^ m)
        if m:
            far.start()
        else:
            near = pltpu.make_async_copy(src, dst, recv)

            @pl.when(s_to == s)
            def _():
                near.start()

            @pl.when(s_to != s)
            def _():
                far.start()

    def home_of_proj(d, j):
        for m in range(r_size):
            src, dst = lp.at[d, j], home_proj.at[r, d, j]
            if m:
                remote(src, dst, ph_send.at[m], ph_recv.at[r], r=r ^ m).start()
            else:
                pltpu.make_async_copy(src, dst, ph_recv.at[r]).start()

    def home_of_columns(landing, home, send, recv):
        per = landing.shape[1] // (s_size // 2)

        def go(d, j):
            s_to = d * (s_size // 2) + j // per
            for m in range(r_size):
                to_home(landing.at[d, j], home.at[me, j % per], send.at[s_to, m], recv.at[me], s_to, m)

        return go

    def out_targets():
        a = (me * own_cols) // shard_rows
        b = (me * own_cols + own_cols - 1) // shard_rows
        return ((a, a < s_size), (b, jnp.logical_and(b != a, b < s_size)))

    margin = (home_out.shape[0] - shard_rows) // 2

    def out_at(s_to, d, j):
        n_out, size = lo_.shape[1:3]
        first = margin + me * own_cols - s_to * shard_rows + (d * n_out + j) * size
        return pl.ds(pl.multiple_of(first, 16), size)

    def home_of_out(d, j):
        for i, (s_to, valid) in enumerate(out_targets()):

            @pl.when(valid)
            def _(i=i, s_to=s_to):
                for m in range(r_size):
                    to_home(lo_.at[d, j], home_out.at[out_at(s_to, d, j)], oh_send.at[i, m], oh_recv.at[me], s_to, m)

    def line(jobs, landing, sems, home, start):
        return LineSum(jobs, landing, *sems, home, start, LAG)

    sum_proj = line(jp, lp, (p_rs, p_rr, p_as, p_ar), home_of_proj, 0)
    start = sum_proj.n
    sum_fc = line(jf, lf, (f_rs, f_rr, f_as, f_ar), home_of_columns(lf, home_fc, fh_send, fh_recv), start)
    start += sum_fc.n
    sum_out = line(jo, lo_, (o_rs, o_rr, o_as, o_ar), home_of_out, start)
    start += sum_out.n
    sum_qkv = line(jq, lq, (q_rs, q_rr, q_as, q_ar), home_of_columns(lq, home_qkv, qh_send, qh_recv), start)
    clock = Clock([sum_proj, sum_fc, sum_out, sum_qkv])
    clock.run(TICKS[0])

    def slot(offset):
        return (offset // r_size) // 2 * r_size + offset % r_size

    def block(ref):
        return lambda o, part: ref.at[pl.ds(o * rows + part * half, half)]

    def packed_block(ref):
        return lambda o, part: ref.at[pl.ds(slot(o) * rows + part * half, half)]

    def far_load(ref):
        def load(o, part):
            copy = pltpu.make_async_copy(block(ref)(o, part), tmp, tmp_sem.at[0])
            copy.start()
            copy.wait()
            return tmp[...]

        return load

    if land_near.shape[0] == tokens:
        land, load_land = block(land_near), lambda o, part: block(land_near)(o, part)[...]
    else:
        land, load_land = block(land_far), far_load(land_far)
    scatter_two = Scatter(packed_block(leaf), packed_block(acc), land, load_land, s2_send, s2_recv, r_size)
    if chunks == 1:
        land_p, load_p = block(chunk2), lambda o, part: block(chunk2)(o, part)[...]
    else:
        land_p, load_p = block(landp), far_load(landp)
    scatter_proj = Scatter(packed_block(leaf), packed_block(acc), land_p, load_p, sp_send, sp_recv, r_size)
    scatter_one = Scatter(packed_block(leaf), packed_block(acc), land, load_land, s1_send, s1_recv, r_size)
    n = r_size * rows

    def partial_sums(dst, odd, lhs, rhs, contract):
        def one(i, carry):
            dst[pl.ds(pl.multiple_of(i * n, n), n), :] = lax.dot_general(
                lhs[pl.ds(pl.multiple_of((2 * i + odd) * n, n), n), :], rhs[...], contract, preferred_element_type=F32
            ).astype(BF16)
            return carry

        lax.fori_loop(0, s_size // 2, one, 0)

    partial_sums(leaf, 1, gpre, own_f, contract_last)
    scatter_two.start_leaves()
    clock.run(TICKS[1])
    partial_sums(acc, 0, gpre, own_f, contract_last)
    load_q.start()
    if chunks == 1:
        product_rows(chunk, gpre, into_jobs(jf))
    clock.run(TICKS[2])

    scatter_two.start_inner()
    clock.run(TICKS[3])
    vec[...] = jnp.zeros_like(vec)
    gain_one, gain_two, proj_bias = (small_ref[i : i + 1, :] for i in (0, 3, 5))
    for load in loads[2:]:
        load.wait()
    cot = cot_v[...].astype(F32)
    middle = middle_ref[...]
    normed, inverse = norm_parts(middle)
    grad_in, grad_gain, grad_bias = norm_backward_rows(scatter_two.finish(), normed, inverse, gain_two)
    grad_middle = cot + grad_in
    branch = grad_middle.astype(BF16)
    gb_own[...] = branch
    gather = Gather(block(gb), g_send, g_recv, r_size, own=lambda o, part: gb_own.at[pl.ds(part * half, half)])
    gather.start(0)
    save_gb = pltpu.make_async_copy(gb_own, gb.at[pl.ds(0, rows)], tmp_sem.at[1])
    save_gb.start()
    vec[2:3, :] = jnp.sum(branch.astype(F32), axis=0, keepdims=True)
    vec[3:4, :] = grad_gain
    vec[4:5, :] = grad_bias
    vec[5:6, :] = jnp.sum(cot, axis=0, keepdims=True)
    clock.run(TICKS[4])
    gather.start_rest()
    scatter_two.close()
    partial_sums(leaf, 1, act, own_p, (((1,), (0,)), ((), ())))
    scatter_proj.start_leaves()
    clock.run(TICKS[5])
    partial_sums(acc, 0, act, own_p, (((1,), (0,)), ((), ())))
    gather.need_all()
    save_gb.wait()
    scatter_proj.start_inner()
    clock.run(TICKS[6])

    if chunks > 1:
        go_acc[...] = jnp.zeros_like(go_acc)

    def branch_rows(i, carry):
        at = pl.ds(pl.multiple_of(i * step, step), step)
        fetch(gb, at, chunk, 2).wait()
        do_ref[at, :] = lax.dot_general(
            chunk[...], own_o[...], contract_last, preferred_element_type=F32
        ).astype(BF16)
        product_rows(att_ref.at[at], chunk, into_jobs(jo) if chunks == 1 else into_sum(go_acc))
        return carry

    if chunks == 1:
        branch_rows(0, 0)
    else:
        lax.fori_loop(0, chunks, branch_rows, 0)
        into_jobs(jo)(0, own_cols, go_acc[...])
    clock.run(TICKS[7])
    out_v[...] = (middle + (scatter_proj.finish() + proj_bias)).astype(BF16)

    def moved(src, dst, sem):
        far = remote(src, dst, sem.at[0], sem.at[1], z=s, s=z)
        near = pltpu.make_async_copy(src, dst, sem.at[1])

        @pl.when(s != z)
        def _():
            far.start()

        @pl.when(s == z)
        def _():
            near.start()

        def done():
            @pl.when(s != z)
            def _():
                far.wait()

            @pl.when(s == z)
            def _():
                near.wait()

        return done

    out_done = moved(out_v, out_home, mv_sem.at[0])
    if chunks == 1:
        early = [pltpu.make_async_copy(h1, chunk2, tmp_sem.at[3])]
        early[0].start()

    code_row = jnp.concatenate([code_ref[i : i + 1, :] for i in range(devices)], axis=1)
    q_rows = min(rows if tokens > 2048 else 256, tokens)
    dk_acc[...] = jnp.zeros_like(dk_acc)
    dv_acc[...] = jnp.zeros_like(dv_acc)

    def attend(i):
        at = pl.ds(pl.multiple_of(i * q_rows, q_rows), q_rows)
        per = q_rows // rows
        code_q = jnp.concatenate(
            [
                jnp.transpose(jnp.broadcast_to(code_ref[pl.ds(i * per + j, 1), :], (8, rows)))[:, 0:1]
                for j in range(per)
            ],
            axis=0,
        )
        low_q = (code_q // SEG_STEP) * SEG_STEP
        allowed = jnp.logical_and(code_row >= low_q, code_row <= code_q)
        dqs, dks, dvs = [], [], []
        for h in range(heads):
            cols = slice(h * HEAD_DIM, (h + 1) * HEAD_DIM)
            q, do, k = q_ref[at, cols], do_ref[at, cols], k_ref[:, cols]
            scores = lax.dot_general(q, k, contract_last, preferred_element_type=F32)
            scores = jnp.where(allowed, scores, NEGATIVE)
            probs = jnp.exp(scores - lse_ref[at, h : h + 1])
            dp = lax.dot_general(do, v_ref[:, cols], contract_last, preferred_element_type=F32)
            delta = jnp.sum(probs * dp, axis=-1, keepdims=True)
            ds = (probs * (dp - delta)).astype(BF16)
            dqs.append(jnp.dot(ds, k, preferred_element_type=F32))
            dks.append(lax.dot_general(ds, q, contract_first, preferred_element_type=F32))
            dvs.append(lax.dot_general(probs.astype(BF16), do, contract_first, preferred_element_type=F32))
        gp[at, 0:own_cols] = (jnp.concatenate(dqs, axis=1) * (1.0 / math.sqrt(HEAD_DIM))).astype(BF16)
        dk_acc[...] += jnp.concatenate(dks, axis=1)
        dv_acc[...] += jnp.concatenate(dvs, axis=1)

    if chunks == 1:
        clock.loop(tokens // q_rows, TICKS[8], attend)
    else:

        def attend_step(i, carry):
            attend(i)
            return carry

        lax.fori_loop(0, tokens // q_rows, attend_step, 0)
    gp[:, own_cols : 2 * own_cols] = dk_acc[...].astype(BF16)
    gp[:, 2 * own_cols :] = dv_acc[...].astype(BF16)

    scatter_proj.close()
    load_q.wait()
    partial_sums(leaf, 1, gp, own_q, contract_last)
    scatter_one.start_leaves()
    clock.run(TICKS[9])
    partial_sums(acc, 0, gp, own_q, contract_last)

    def hidden_rows(i, carry):
        at = pl.ds(pl.multiple_of(i * step, step), step)
        (early[0] if early else fetch(h1, at, chunk2, 3)).wait()
        product_rows(chunk2, gp.at[at], into_jobs(jq) if chunks == 1 else into_sum(gq_acc))
        return carry

    if chunks == 1:
        hidden_rows(0, 0)
    else:
        lax.fori_loop(0, chunks, hidden_rows, 0)
        into_jobs(jq)(0, width, gq_acc[...])
    scatter_one.start_inner()
    clock.run(TICKS[10])

    resid = x_ref[...].astype(F32)
    normed, inverse = norm_parts(resid)
    grad_in, grad_gain, grad_bias = norm_backward_rows(scatter_one.finish(), normed, inverse, gain_one)
    ig_v[...] = (grad_middle + grad_in).astype(BF16)
    ig_done = moved(ig_v, ig_home, mv_sem.at[1])
    vec[0:1, :] = grad_gain
    vec[1:2, :] = grad_bias
    ff_lanes = -(-own_ff // 128) * 128
    q_lanes = -(-own_cols // 128) * 128
    vec[7:8, 0:own_ff] = jnp.sum(gpre[...].astype(F32), axis=0, keepdims=True)
    vec[7:8, ff_lanes : ff_lanes + own_cols] = jnp.sum(gp[:, :own_cols].astype(F32), axis=0, keepdims=True)
    vec[7:8, ff_lanes + q_lanes : ff_lanes + q_lanes + own_cols] = jnp.sum(
        gp[:, 2 * own_cols :].astype(F32), axis=0, keepdims=True
    )
    vec[pl.ds(8 + me, 1), :] = vec[7:8, :]

    hops = [("s", 1), ("s", 2)] + [("r", bit) for bit in bits_of(r_size)] + [("z", bit) for bit in bits_of(z_size)]
    for i, (axis, bit) in enumerate(hops):
        copy = remote(vec, vec_land.at[i], vec_send.at[i], vec_recv.at[i], **partner(axis, bit))
        copy.start()
        clock.run(TICKS[11])
        copy.wait()
        vec[...] = vec[...] + vec_land[i]
    small_out[...] = vec[...]
    clock.run(clock.end)

    scatter_one.close()
    gather.close()
    out_done()
    ig_done()
    for total in (sum_proj, sum_fc, sum_qkv, sum_out):
        total.close()
    for i in range(r_size):
        pltpu.make_async_copy(home_proj.at[i], home_proj.at[i], ph_recv.at[i]).wait()
    for m in range(1, r_size):
        pltpu.make_async_copy(home_proj.at[0], home_proj.at[0], ph_send.at[m]).wait()
    for home, send, recv in ((home_fc, fh_send, fh_recv), (home_qkv, qh_send, qh_recv)):
        for i in range(devices):
            pltpu.make_async_copy(home.at[i], home.at[i], recv.at[i]).wait()
        for s_to in range(s_size):
            for m in range(r_size):
                sent = pltpu.make_async_copy(home.at[0], home.at[0], send.at[s_to, m])
                if m:
                    sent.wait()
                else:

                    @pl.when(s != s_to)
                    def _(sent=sent):
                        sent.wait()

    out_block = home_out.at[pl.ds(0, own_cols)]
    for i in range(devices):
        a, b = (i * own_cols) // shard_rows, (i * own_cols + own_cols - 1) // shard_rows

        @pl.when(jnp.logical_or(s == a, s == b))
        def _(i=i):
            pltpu.make_async_copy(out_block, out_block, oh_recv.at[i]).wait()

    for i, (s_to, valid) in enumerate(out_targets()):
        for m in range(r_size):
            far = valid if m else jnp.logical_and(valid, s_to != s)

            @pl.when(far)
            def _(i=i, m=m):
                pltpu.make_async_copy(out_block, out_block, oh_send.at[i, m]).wait()


def backward_part(h2, cot, wf, wp, h1, wq, wo, q, k, v, att, lse, code, middle, x_own, small, fcb):
    s_size, r_size, z_size = (lax.axis_size(a) for a in ("s", "r", "z"))
    devices = s_size * r_size
    rows, width = x_own.shape
    tokens = rows * devices
    own_cols = q.shape[1]
    heads = own_cols // HEAD_DIM
    own_ff = wf.shape[1]
    shard_rows = width // s_size
    p_rows = job_rows(own_ff // 2)
    p_n = own_ff // 2 // p_rows
    c_rows = job_rows(shard_rows)
    c_per = shard_rows // c_rows
    c_n = c_per * s_size // 2
    o_rows = job_rows(own_cols // 2)
    o_n = own_cols // 2 // o_rows
    hops = 2 + len(bits_of(r_size)) + len(bits_of(z_size))
    vec_rows = 8 + devices
    small_plane = tokens <= 1024
    step = tokens if small_plane else 256
    anywhere = pl.BlockSpec(memory_space=pl.ANY)
    vmem = pl.BlockSpec(memory_space=pltpu.VMEM)
    shape = jax.ShapeDtypeStruct
    dma = pltpu.SemaphoreType.DMA
    tree = [dma((2, devices))] * 2
    jobs = [(2, p_n, p_rows, width), (2, c_n, c_rows, own_ff), (2, c_n, c_rows, 3 * own_cols), (2, o_n, o_rows, width)]
    line = [dma(j[:2]) for j in jobs for _ in range(4)]

    def sums(*dims):
        return pltpu.VMEM((8, 128) if small_plane else dims, F32)

    return pl.pallas_call(
        backward_kernel,
        in_specs=[anywhere] * 7 + [vmem] * 10,
        out_specs=[anywhere] * 6 + [vmem] + [anywhere] * 3,
        out_shape=[
            shape((rows, width), BF16),
            shape((rows, width), BF16),
            shape((r_size,) + jobs[0], BF16),
            shape((devices, c_per, c_rows, own_ff), BF16),
            shape((devices, c_per, c_rows, 3 * own_cols), BF16),
            shape((2 * (-(-own_cols // c_rows)) * c_rows + shard_rows, width), BF16),
            shape((vec_rows, width), F32),
            shape((tokens, width), BF16),
            shape((tokens, width), BF16),
            shape((tokens, width), BF16),
        ],
        scratch_shapes=[
            pltpu.VMEM((tokens // 2, width), BF16),
            pltpu.VMEM((tokens // 2, width), BF16),
            pltpu.VMEM((tokens if small_plane else 16, width), BF16),
            pltpu.VMEM((rows // 2, width), BF16),
        ]
        + [pltpu.VMEM(j, BF16) for j in jobs]
        + [pltpu.VMEM(j, BF16) for j in jobs]
        + [
            pltpu.VMEM((width, own_ff), BF16),
            pltpu.VMEM((own_ff, width), BF16),
            pltpu.VMEM((16, 128) if small_plane else (width, 3 * own_cols), BF16),
            pltpu.VMEM((own_cols, width), BF16),
            pltpu.VMEM((rows, width), BF16),
            pltpu.VMEM((step, width), BF16),
            pltpu.VMEM((step, width), BF16),
            sums(own_ff, width),
            sums(width, own_ff),
            sums(width, 3 * own_cols),
            pltpu.VMEM((tokens, own_ff), BF16),
            pltpu.VMEM((tokens, own_ff), BF16),
            pltpu.VMEM((tokens, own_cols), BF16),
            pltpu.VMEM((tokens, 3 * own_cols), BF16),
            pltpu.VMEM((tokens, own_cols), F32),
            pltpu.VMEM((tokens, own_cols), F32),
            sums(own_cols, width),
            pltpu.VMEM((vec_rows, width), F32),
            pltpu.VMEM((hops, vec_rows, width), F32),
            pltpu.VMEM((rows, width), BF16),
            pltpu.VMEM((rows, width), BF16),
            pltpu.VMEM((rows, width), BF16),
            dma((5,)),
        ]
        + tree * 4
        + [dma((4,)), dma((2, 2)), dma((hops,)), dma((hops,))]
        + line
        + [
            dma((r_size,)), dma((r_size,)),
            dma((s_size, r_size)), dma((devices,)),
            dma((s_size, r_size)), dma((devices,)),
            dma((2, r_size)), dma((devices,)),
        ],
        compiler_params=pltpu.CompilerParams(
            collective_id=1, has_side_effects=True, vmem_limit_bytes=62 << 20
        ),
        cost_estimate=pl.CostEstimate(
            flops=10 * heads * tokens * tokens * HEAD_DIM + 12 * tokens * width * own_ff,
            bytes_accessed=40 << 20,
            transcendentals=0,
        ),
        name="backward_part",
    )(h2, cot, wf, wp, h1, wq, wo, q, k, v, att, lse, code, middle, x_own, small, fcb)


def results_kernel(
    out_in, ig_in, proj_in, fc_in, qkv_in, wo_in, sums,
    out, ig, g1, b1, qkv, qv, wo, ob, g2, b2, fc, fcb, proj, pb,
):
    devices = fc_in.shape[0]
    own_ff, own_cols = fc_in.shape[3], qkv_in.shape[3] // 3
    width = wo.shape[1]
    proj[...] = proj_in[...].astype(F32)
    wo[...] = wo_in[...].astype(F32)
    fc[...] = jnp.concatenate([fc_in[device, 0] for device in range(devices)], axis=1).astype(F32)
    parts = []
    for part in range(3):
        for device in range(devices):
            n = max(0, min(own_cols, width - device * own_cols))
            if n:
                parts.append(qkv_in[device, 0, :, part * own_cols : part * own_cols + n])
    qkv[...] = jnp.concatenate(parts, axis=1).astype(F32)

    @pl.when(pl.program_id(0) == 0)
    def _():
        out[...] = jnp.transpose(out_in[...])
        ig[...] = jnp.transpose(ig_in[...].astype(F32))
        s = lax.axis_index("s")
        s_size = lax.axis_size("s")
        ff_lanes = -(-own_ff // 128) * 128
        q_lanes = -(-own_cols // 128) * 128
        by_device = devices // s_size

        def heads_of(first):
            return jnp.concatenate(
                [sums[8 + d : 9 + d, first : first + own_cols] for d in range(devices)], axis=1
            )[:, :width]

        qv_all = jnp.concatenate([heads_of(ff_lanes), heads_of(ff_lanes + q_lanes)], axis=1)
        for s2 in range(s_size):

            @pl.when(s == s2)
            def _(s2=s2):
                n = width // s_size
                for i, ref in enumerate((g1, b1, ob, g2, b2, pb)):
                    ref[...] = sums[i, s2 * n : (s2 + 1) * n]
                qv[...] = qv_all[0, 2 * s2 * n : 2 * (s2 + 1) * n]
                fcb[...] = jnp.concatenate(
                    [sums[8 + d : 9 + d, 0:own_ff] for d in range(s2 * by_device, (s2 + 1) * by_device)], axis=1
                )[0]


def results(out_home, ig_home, home_proj, home_fc, home_qkv, home_out, sums):
    devices, c_per, c_rows, own_ff = home_fc.shape
    rows, width = out_home.shape
    shard_rows = c_per * c_rows
    own_cols = home_qkv.shape[3] // 3
    proj = home_proj.reshape(-1, width)
    ff = devices * own_ff
    steps = c_per
    proj_rows = proj.shape[0] // steps
    first = (home_out.shape[0] - shard_rows) // 2 // c_rows
    whole = lambda *dims: pl.BlockSpec(dims, lambda i: (0,) * len(dims))
    by_rows = lambda n, columns: pl.BlockSpec((n, columns), lambda i: (i, 0))
    by_device = lambda columns: pl.BlockSpec((devices, 1, c_rows, columns), lambda i: (0, i, 0, 0))
    shape = lambda *dims: jax.ShapeDtypeStruct(dims, F32)
    vector = whole(shard_rows)
    return pl.pallas_call(
        results_kernel,
        grid=(steps,),
        in_specs=[
            whole(rows, width),
            whole(rows, width),
            by_rows(proj_rows, width),
            by_device(own_ff),
            by_device(3 * own_cols),
            pl.BlockSpec((c_rows, width), lambda i: (first + i, 0)),
            whole(*sums.shape),
        ],
        out_specs=[
            whole(width, rows),
            whole(width, rows),
            vector,
            vector,
            by_rows(c_rows, 3 * width),
            whole(2 * shard_rows),
            by_rows(c_rows, width),
            vector,
            vector,
            vector,
            by_rows(c_rows, ff),
            whole(proj.shape[0]),
            by_rows(proj_rows, width),
            vector,
        ],
        out_shape=[
            jax.ShapeDtypeStruct((width, rows), BF16),
            shape(width, rows),
            shape(shard_rows),
            shape(shard_rows),
            shape(shard_rows, 3 * width),
            shape(2 * shard_rows),
            shape(shard_rows, width),
            shape(shard_rows),
            shape(shard_rows),
            shape(shard_rows),
            shape(shard_rows, ff),
            shape(proj.shape[0]),
            shape(*proj.shape),
            shape(shard_rows),
        ],
        compiler_params=pltpu.CompilerParams(vmem_limit_bytes=61 << 20),
        name="results",
    )(out_home, ig_home, proj, home_fc, home_qkv, home_out, sums)


def local(
    inputs,
    positions,
    segments,
    cotangent,
    ln1_gain,
    ln1_bias,
    w_qkv,
    qv_bias,
    w_out,
    out_bias,
    ln2_gain,
    ln2_bias,
    w_fc,
    fc_bias,
    w_proj,
    proj_bias,
):
    rows = inputs.shape[0]
    code = jnp.broadcast_to(segments * SEG_STEP + positions // BLOCK, (8, rows))
    vectors = (ln1_gain, ln1_bias, out_bias, ln2_gain, ln2_bias, proj_bias, qv_bias, fc_bias)

    (
        hidden_one, hidden_two, cot, own_fc, own_qkv, own_out, queries, keys, values, attended, lse, code_all,
        middle, x_own, small, own_fcb,
    ) = forward_part(inputs.T, cotangent.T, code, vectors, w_qkv, w_fc, w_out)
    found = backward_part(
        hidden_two, cot, own_fc, w_proj, hidden_one, own_qkv, own_out, queries, keys, values, attended, lse, code_all,
        middle, x_own, small, own_fcb,
    )
    out, input_grad, *grads = results(*found[:7])
    return (out.T, input_grad.T, *grads)


def solution(mesh):
    ctx, shard = mesh.devices.shape
    fine = Mesh(mesh.devices.reshape(shard, ctx // shard, shard), ("z", "r", "s"))
    tokens = ("s", "z", "r")
    arg_specs = (
        P(tokens, None),
        P(tokens),
        P(tokens),
        P(tokens, None),
        P("s"),
        P("s"),
        P("s", None),
        P("s"),
        P("s", None),
        P("s"),
        P("s"),
        P("s"),
        P("s", None),
        P("s"),
        P("s", None),
        P("s"),
    )
    out_specs = (P(tokens, None), P(tokens, None)) + arg_specs[4:]
    return jax.shard_map(local, mesh=fine, in_specs=arg_specs, out_specs=out_specs, check_vma=False)
```
